32 devices in a mesh: groups: 2 (over x), fsdp: 16 (over z, y, core).
Axes of the slice: x: 2, y: 2, z: 4, core: 2. Of those that a mesh axis runs over, the one named last changes fastest.
Arguments:
- obs_feat: bfloat16 [12288, 2048], P(('groups', 'fsdp')), parts along dimension 0, may hold values from -6 to 6
- reward: float32 [512, 24], P(('groups', 'fsdp')), parts along dimension 0, may hold values from -22 to 22
- value_old: float32 [512, 25], P(('groups', 'fsdp')), parts along dimension 0, may hold values from -6 to 6
- done: int32 [512, 24], P(('groups', 'fsdp')), parts along dimension 0, may hold values 0 or 1
- minibatch_perm: int32 [12288], P(('groups', 'fsdp')), parts along dimension 0, may hold values from 0 to 6143, as said below
- old_mean: bfloat16 [12288, 12], P(('groups', 'fsdp')), parts along dimension 0, may hold values from -6 to 6
- noise: bfloat16 [12288, 12], P(('groups', 'fsdp')), parts along dimension 0, may hold values from -6 to 6
- gain_in: float32 [2048], replicated, may hold values from 0.5 to 1.5
- out_weight: bfloat16 [2048, 2048], P('fsdp'), may hold values from -0.125 to 0.125
- head_weight: bfloat16 [2048, 13], replicated, may hold values from -0.125 to 0.125
- log_std: float32 [12], replicated, may hold values from 0.7 to 1.3
Outputs:
- hidden_out: bfloat16 [12288, 2048], P(('groups', 'fsdp')), parts along dimension 0
- grad_weight: float32 [4096, 2048], P(('groups', 'fsdp')), parts along dimension 0
- grad_head: float32 [4096, 13], P('groups'), parts along dimension 0
- grad_std: float32 [24], P('groups'), parts along dimension 0
The draws below stay inside these ranges and needn't reach their ends.
There are 2 independent parts, one for each index of `groups`. The reference program is written for one: setup_inputs(seed, part) draws one part's arguments, and reference() takes and returns one part's arrays. A program takes and returns all parts, laid end to end along the dimension named above; an argument that names none is the same for every part. Nothing has to cross between parts.
Inputs may be any that keep to these rules, and one draw needn't show every extreme that they name: `minibatch_perm`: rows of one index of fsdp go 24 to each index of fsdp; the block of 384 minibatch positions of index j holds at positions j * 384 + s * 24 + c the rows from index s; a permutation of all rows.
All inputs are finite; a program needn't handle non-finite values. No bound on the sum of `done` on one device may be relied on, other than what follows from the above.
Results may differ from the reference program's by a relative error of at most 0.0095.
Values may be sent and summed in bfloat16 or wider, within the bound.
No kernel may reach another device: no remote copies, remote signals or barrier semaphores. Data moves between devices by JAX's collectives and lax.ppermute only.
A program may use at most 128 MiB of HBM per device.

```python
import jax
import jax.numpy as jnp
from jax import lax

D = 2048
ACT = 12
STEPS = 24
ENVS = 256
ROWS_DEV = 384
ROWS = 6144
PEER = 24
N_FSDP = 16


def draw_reward(key, part):
    first = jax.random.fold_in(jax.random.fold_in(key, 11), 0)
    env_pos = jnp.arange(ENVS, dtype=jnp.float32) / ENVS
    rising = jnp.exp(jnp.log(3.0) * env_pos)[:, None]
    values = jnp.clip(jax.random.normal(first, (ENVS, STEPS), jnp.float32), -5.0, 5.0) * rising
    return jnp.clip(values, -22.0, 22.0).astype(jnp.float32)


def draw_minibatch_perm(key, part):
    keys = jax.random.split(jax.random.fold_in(key, 23), N_FSDP)
    shuffled = jax.vmap(lambda single: jax.random.permutation(single, ROWS_DEV))(keys).astype(jnp.int32)
    source = jnp.arange(N_FSDP, dtype=jnp.int32)[:, None]
    target = shuffled // PEER
    within = shuffled % PEER
    return (target * ROWS_DEV + source * PEER + within).reshape(-1).astype(jnp.int32)


def place_ends(result, own_key, low, high):
    spot = [jax.random.randint(jax.random.fold_in(own_key, axis), (), 0, length) for axis, length in enumerate(result.shape)]
    longest = result.shape.index(max(result.shape))
    neighbour = spot[:longest] + [(spot[longest] + 1) % result.shape[longest]] + spot[longest + 1:]
    return result.at[tuple(spot)].set(low).at[tuple(neighbour)].set(high)


def level_of(key, shape, cuts, low, top_value):
    def one(dim, parts):
        steps = jax.random.uniform(jax.random.fold_in(jax.random.fold_in(key, 6), dim), (parts,), jnp.float32, low / len(cuts), top_value / len(cuts))
        return jnp.repeat(jnp.exp(steps), shape[dim] // parts).reshape((-1,) + (1,) * (len(shape) - dim - 1))

    loudness = one(*cuts[0])
    for cut in cuts[1:]:
        loudness = loudness * one(*cut)
    return loudness


def gaussian(stream_key, dims, deviation, limit, shards=(), kind=jnp.bfloat16):
    array = jax.random.normal(stream_key, dims, jnp.float32) * deviation
    if len(shards) > 0:
        array = level_of(stream_key, dims, shards, -0.22, 0.18) * array
    return jnp.clip(array, min=-limit, max=limit).astype(kind)


def setup_inputs(seed: int = 0, part: int = 0) -> dict:
    seeds = jax.random.split(jax.random.key(seed), 12)
    own_keys = jax.random.split(jax.random.fold_in(seeds[11], part), 12)
    return {
        "obs_feat": gaussian(own_keys[0], (ROWS, D), 1.0, 6.0, ((0, 16),)),
        "reward": draw_reward(jax.random.fold_in(jax.random.fold_in(seeds[11], part), 71), part),
        "value_old": gaussian(own_keys[2], (ENVS, STEPS + 1), 1.0, 6.0, ((0, 16),), jnp.float32),
        "done": place_ends((jax.random.randint(own_keys[3], (ENVS, STEPS), 0, 32) < 1).astype(jnp.int32), jax.random.fold_in(own_keys[3], 1), 0, 1),
        "minibatch_perm": draw_minibatch_perm(jax.random.fold_in(jax.random.fold_in(seeds[11], part), 71), part),
        "old_mean": gaussian(own_keys[5], (ROWS, ACT), 1.0, 6.0, ((0, 16),)),
        "noise": gaussian(own_keys[6], (ROWS, ACT), 1.0, 6.0, ((0, 16),)),
        "gain_in": jnp.clip(1.0 + 0.1 * jax.random.normal(seeds[7], (D,), jnp.float32), 0.5, 1.5),
        "out_weight": gaussian(seeds[8], (D, D), D ** -0.5, 0.125, ((0, 16),)),
        "head_weight": gaussian(seeds[9], (D, ACT + 1), D ** -0.5, 0.125),
        "log_std": jnp.clip(jax.random.uniform(seeds[10], (ACT,), jnp.float32, 0.7, 1.3), 0.7, 1.3),
    }


GAMMA = 0.99
LAMBDA_GAE = 0.95
CLIP_EPS = 0.2
NORM_EPS = 1e-05

def advantages(reward, value_old, done):
    keep = 1.0 - done.astype(jnp.float32)
    deltas = reward + GAMMA * value_old[:, 1:] * keep - value_old[:, :-1]

    def walk(carry, inputs):
        dstep, kstep = inputs
        carry = dstep + GAMMA * LAMBDA_GAE * kstep * carry
        return (carry, carry)
    start = jnp.zeros((reward.shape[0],), jnp.float32)
    _, stacked = lax.scan(walk, start, (deltas.T, keep.T), reverse=True)
    gae = stacked.T
    return (gae.reshape(-1), (gae + value_old[:, :-1]).reshape(-1))

def row_block(rows_x, old_mean, noise, adv_b, ret_b, gain_in, out_weight, head_weight, log_std, scale):
    xf = rows_x.astype(jnp.float32)
    normed = (xf * lax.rsqrt(lax.optimization_barrier(jnp.mean(xf * xf, -1, keepdims=True)) + NORM_EPS) * gain_in).astype(jnp.bfloat16)
    hidden = xf + jnp.dot(normed, out_weight, preferred_element_type=jnp.float32)
    rinv = lax.rsqrt(lax.optimization_barrier(jnp.mean(hidden * hidden, -1, keepdims=True)) + NORM_EPS)
    hnorm = hidden * rinv
    hnorm_b = hnorm.astype(jnp.bfloat16)
    heads = jnp.dot(hnorm_b, head_weight, preferred_element_type=jnp.float32)
    nact = log_std.shape[0]
    mean_act = heads[:, :nact]
    value = heads[:, nact]
    std_dev = jnp.exp(log_std)
    offset = old_mean.astype(jnp.float32) - mean_act
    sample = noise.astype(jnp.float32)
    logr = lax.optimization_barrier(jnp.sum(-sample * offset / std_dev - offset * offset / (2.0 * std_dev * std_dev), -1))
    ratio = jnp.exp(logr)
    advant = adv_b.astype(jnp.float32)
    clipped = jnp.clip(ratio, 1.0 - CLIP_EPS, 1.0 + CLIP_EPS)
    active = ratio * advant <= clipped * advant
    gratio = jnp.where(active, -scale * advant, 0.0)
    glogr = gratio * ratio
    gmean = glogr[:, None] * (sample / std_dev + offset / (std_dev * std_dev))
    gvalue = scale * (value - ret_b.astype(jnp.float32))
    std_part = lax.optimization_barrier(jnp.sum(glogr[:, None] * (sample * offset / std_dev + offset * offset / (std_dev * std_dev)), 0))
    ghead = jnp.concatenate([gmean, gvalue[:, None]], 1)
    head_part = jnp.dot(hnorm_b.astype(jnp.float32).T, ghead, precision=lax.Precision.HIGHEST)
    ghn = jnp.dot(ghead, head_weight.astype(jnp.float32).T, precision=lax.Precision.HIGHEST)
    ghid = rinv * (ghn - hnorm * lax.optimization_barrier(jnp.mean(ghn * hnorm, -1, keepdims=True)))
    ghid_b = ghid.astype(jnp.bfloat16)
    return (hidden.astype(jnp.bfloat16), normed, ghid_b, head_part, std_part)

def reference(obs_feat, reward, value_old, done, minibatch_perm, old_mean, noise, gain_in, out_weight, head_weight, log_std):
    gae, returns = advantages(reward, value_old, done)
    mean_adv = jnp.sum(gae) / ROWS
    var_adv = jnp.sum(gae * gae) / ROWS - mean_adv * mean_adv
    adv_b = ((gae - mean_adv) * lax.rsqrt(var_adv + NORM_EPS)).astype(jnp.bfloat16)
    ret_b = returns.astype(jnp.bfloat16)
    scale = 1.0 / jnp.sqrt(jnp.float32(ROWS))
    nblock = ROWS // ROWS_DEV

    def one_block(carry, inputs):
        wsum, hsum, ssum = carry
        bx, bm, bn, ba, br = inputs
        hid_b, normed, ghid_b, head_part, std_part = row_block(bx, bm, bn, ba, br, gain_in, out_weight, head_weight, log_std, scale)
        wpart = lax.dot_general(normed, ghid_b, (((0,), (0,)), ((), ())), preferred_element_type=jnp.float32)
        return ((wsum + wpart, hsum + head_part, ssum + std_part), hid_b)
    init = (jnp.zeros((D, D), jnp.float32), jnp.zeros((D, ACT + 1), jnp.float32), jnp.zeros((ACT,), jnp.float32))
    inputs = (obs_feat.reshape(nblock, ROWS_DEV, D), old_mean.reshape(nblock, ROWS_DEV, ACT), noise.reshape(nblock, ROWS_DEV, ACT), adv_b.reshape(nblock, ROWS_DEV), ret_b.reshape(nblock, ROWS_DEV))
    (grad_weight, grad_head, grad_std), hid_all = lax.scan(one_block, init, inputs)
    hidden_out = jnp.zeros((ROWS, D), jnp.bfloat16).at[minibatch_perm].set(hid_all.reshape(ROWS, D))
    return (hidden_out, grad_weight, grad_head, grad_std)
```

```python
import functools

import jax
import jax.numpy as jnp
from jax import lax
from jax.experimental import pallas as pl
from jax.experimental.pallas import tpu as pltpu
from jax.sharding import PartitionSpec as P

GAMMA = 0.99
LAMBDA_GAE = 0.95
CLIP_EPS = 0.2
NORM_EPS = 1e-05
F32 = jnp.float32
BF16 = jnp.bfloat16
LANES = 128
HALF = 16
VMEM_BYTES = 56 * 1024 * 1024
CHEAP = pl.CostEstimate(flops=1, bytes_accessed=1, transcendentals=0)


def params():
    return pltpu.CompilerParams(
        vmem_limit_bytes=VMEM_BYTES, dimension_semantics=("arbitrary",)
    )


def split(x):
    high = x.astype(BF16)
    return high, (x - high.astype(F32)).astype(BF16)


def dot(a, b):
    return jnp.dot(a, b, preferred_element_type=F32)


def dot_t(a, b):
    return lax.dot_general(a, b, (((1,), (1,)), ((), ())), preferred_element_type=F32)


def shifted(x, by):
    return pltpu.roll(x, LANES - by, 1)


def small_kernel(
    nact, per_peer, reward_ref, value_ref, done_ref, old_ref, noise_ref, perm_ref, small_ref, pair_ref, pad_ref, tall_ref
):
    envs, steps = reward_ref.shape
    rows = perm_ref.shape[1]

    def wide(x):
        pad_ref[...] = jnp.zeros_like(pad_ref)
        pad_ref[:, : x.shape[1]] = x
        return pad_ref[...]

    inside = lax.broadcasted_iota(jnp.int32, (envs, LANES), 1) < steps
    value = wide(value_ref[...])
    keep = 1.0 - wide(done_ref[...].astype(F32))
    delta = wide(reward_ref[...]) + GAMMA * shifted(value, 1) * keep - value
    gae = jnp.where(inside, delta, 0.0)
    factor = jnp.where(inside, GAMMA * LAMBDA_GAE * keep, 0.0)
    reach = 1
    while reach < steps:
        gae = gae + factor * shifted(gae, reach)
        factor = factor * shifted(factor, reach)
        reach *= 2
    ret = gae + value
    high, low = split(gae)
    mid, low = split(gae - high.astype(F32))
    lane = lax.broadcasted_iota(jnp.int32, (LANES, rows), 1)
    pick = jnp.where(
        lax.rem(lane, steps) == lax.broadcasted_iota(jnp.int32, (LANES, rows), 0), 1.0, 0.0
    ).astype(BF16)
    lane = lax.broadcasted_iota(jnp.int32, (envs, rows), 1)
    mine = lane // steps == lax.broadcasted_iota(jnp.int32, (envs, rows), 0)

    def flat(x):
        return jnp.sum(jnp.where(mine, dot(x, pick), 0.0), 0, keepdims=True)

    perm = perm_ref[...]
    slot = perm // rows * per_peer + lax.rem(perm, per_peer)
    row = lax.broadcasted_iota(jnp.int32, (HALF, rows), 0)

    def put(block, index, values):
        return jnp.where(row == index, values, block)

    def tall(x):
        tall_ref[...] = jnp.zeros_like(tall_ref)
        tall_ref[:nact, :] = x.astype(F32)
        return tall_ref[...]

    top = tall(old_ref[...])
    for index, values in enumerate((high, mid, low, ret.astype(BF16))):
        top = put(top, nact + index, flat(values))
    bottom = tall(noise_ref[...])
    bottom = put(bottom, nact, (slot // 256).astype(F32))
    bottom = put(bottom, nact + 1, lax.rem(slot, 256).astype(F32))
    small = jnp.concatenate([top, bottom], 0).astype(BF16)
    small_ref[...] = small
    gae = gae_of(small[:HALF], nact)
    lane = lax.broadcasted_iota(jnp.int32, pair_ref.shape, 1)
    pair = jnp.zeros(pair_ref.shape, F32)
    for first, value in ((0, gae), (3, gae * gae)):
        value = jnp.sum(value, 1, keepdims=True)
        for i in range(3):
            rounded = value.astype(BF16).astype(F32)
            pair = jnp.where(lane == first + i, rounded, pair)
            value = value - rounded
    pair_ref[...] = pair.astype(BF16)


def gae_of(small, nact):
    block = small.astype(F32)
    return block[nact : nact + 1] + block[nact + 1 : nact + 2] + block[nact + 2 : nact + 3]


def join_kernel(where_ref, *refs):
    pieces, pair_ref, block_ref = refs[:-2], refs[-2], refs[-1]
    kr = pieces[0].shape[0]
    for r, piece in enumerate(pieces):
        here = pl.ds(pl.multiple_of((where_ref[0] ^ r) * kr, kr), kr)
        block_ref[here, :] = piece[...]
    block_ref[kr * len(pieces) :, :] = pair_ref[...]


def norm_kernel(count, where_ref, *refs):
    x_refs, xq_refs, gain_ref = refs[:count], refs[count : 2 * count], refs[2 * count]
    normed_ref, turned_ref, xq_ref = refs[-3:]
    if count == 1:
        x, xq = x_refs[0][...], xq_refs[0][...]
    else:
        first = pl.program_id(0) == 0
        x = jnp.where(first, x_refs[0][...], x_refs[1][...])
        xq = jnp.where(first, xq_refs[0][...], xq_refs[1][...])
    xf = x.astype(F32)
    rms = lax.rsqrt(jnp.mean(xf * xf, -1, keepdims=True) + NORM_EPS)
    normed = xf * rms * gain_ref[...]
    normed_ref[...] = normed.astype(BF16)
    turned_ref[...] = normed.T.astype(BF16)
    xq_ref[...] = xq


def norm_piece(where, xs, gain, start, apart, total, part, buffers):
    rows, width = xs[0].shape
    step = LANES
    base = start // step
    far = apart // step
    if len(xs) == 1:
        grid, source, target = rows // step, (lambda i: i), (lambda i: base + i)
    else:
        grid, source, target = len(xs), (lambda i: 0), (lambda i: base + i * far)
    shapes = (
        jax.ShapeDtypeStruct((total, width), BF16),
        jax.ShapeDtypeStruct((width, total), BF16),
        jax.ShapeDtypeStruct((total, part), BF16),
    )
    buffers = () if buffers is None else buffers
    return pl.pallas_call(
        functools.partial(norm_kernel, len(xs)),
        out_shape=shapes,
        grid_spec=pltpu.PrefetchScalarGridSpec(
            num_scalar_prefetch=1,
            grid=(grid,),
            in_specs=[pl.BlockSpec((step, width), lambda i, w: (source(i), 0))] * len(xs)
            + [pl.BlockSpec((step, part), lambda i, w: (source(i), w[0]))] * len(xs)
            + [pl.BlockSpec((1, width), lambda i, w: (0, 0))]
            + [pl.BlockSpec(memory_space=pl.ANY)] * len(buffers),
            out_specs=[
                pl.BlockSpec((step, width), lambda i, w: (target(i), 0)),
                pl.BlockSpec((width, step), lambda i, w: (0, target(i))),
                pl.BlockSpec((step, part), lambda i, w: (target(i), 0)),
            ],
        ),
        input_output_aliases={2 * len(xs) + 2 + i: i for i in range(len(buffers))},
        compiler_params=params(),
        cost_estimate=CHEAP,
        name="norm",
    )(where, *xs, *xs, gain, *buffers)


def hidden_kernel(line, nact, packed, given, where_ref, *refs):
    count = 1 if given else 2 * line - 2
    weights, refs = refs[:count], refs[count:]
    normed_ref, xq_ref, row_ref, hw_ref, high_ref, sums_ref, send_ref = refs[:7]
    w_ref = weights[0] if given else refs[7]
    step = pl.program_id(0)
    z = where_ref[1]
    rows = normed_ref.shape[0]
    slab = w_ref.shape[0] // line

    def pick():
        own, direct = weights[0], weights[-1]
        fwd, bwd = weights[1 : line - 1] + (direct,), weights[line - 1 : -1] + (direct,)
        w_ref[pl.ds(pl.multiple_of(z * slab, slab), slab), :] = own[:slab, :]
        for j in range(1, line):
            place = pl.multiple_of(lax.rem(z - j + line, line) * slab, slab)
            w_ref[pl.ds(place, slab), :] = jnp.where(
                z >= j, fwd[j - 1][:slab, :], bwd[line - j - 1][:slab, :]
            )

    if not given:
        pl.when(step == 0)(pick)

    hidden = xq_ref[...].astype(F32) + dot(normed_ref[...], w_ref[...])
    high, low = split(hidden)
    high_ref[...] = high
    heads = dot(high, hw_ref[...]) + dot(low, hw_ref[...])
    lane = lax.broadcasted_iota(jnp.int32, heads.shape, 1)
    square = jnp.sum(hidden * hidden, 1, keepdims=True)
    sums = jnp.where(lane == nact + 1, square, heads).T[:HALF]
    if not given:
        pair = jnp.zeros((HALF, LANES), F32)
        for ref in weights:
            pair = pair + ref[slab:, :LANES].astype(F32)
        pair = jnp.concatenate([pair[:1], jnp.zeros((1, rows - LANES), F32)], 1)
        row = lax.broadcasted_iota(jnp.int32, sums.shape, 0)
        sums = jnp.where(row == nact + 2, pair, sums)
    sums_ref[...] = sums
    slot = row_ref[HALF + nact : HALF + nact + 1, :].astype(F32) * 256.0
    slot = (slot + row_ref[HALF + nact + 1 : HALF + nact + 2, :].astype(F32)).astype(jnp.int32)
    order = jnp.where(lax.broadcasted_iota(jnp.int32, (rows, rows), 0) == slot, 1.0, 0.0).astype(BF16)
    ranked = dot(order, high)
    if not packed:
        send_ref[...] = ranked.astype(BF16)
        return
    sorted_ref = refs[-1]
    sorted_ref[pl.ds(pl.multiple_of(step * rows, rows), rows), :] = ranked

    @pl.when(step == sorted_ref.shape[0] // rows - 1)
    def _():
        n, size, _ = send_ref.shape
        members = sorted_ref.shape[0] // rows
        peer = size // members
        for j in range(n):
            send_ref[j] = jnp.concatenate(
                [sorted_ref[r * rows + j * peer : r * rows + (j + 1) * peer, :] for r in range(members)],
                0,
            ).astype(BF16)


def rest_kernel(line, team, nact, width, total_rows, where_ref, *refs):
    sums, refs = refs[:team], refs[team:]
    row_ref, isd_ref, *high_refs = refs[:4]
    hw_ref, turned_ref = refs[4:6]
    grads = refs[6 : 6 + line]
    firsts, (direct_ref, head_ref, ghid_ref) = refs[6 + line : -3], refs[-3:]
    z = where_ref[1]
    step = pl.program_id(0)
    scale = total_rows**-0.5
    slab, part = grads[0].shape

    @pl.when(step == 0)
    def _():
        half = team // 2
        rows = high_refs[0].shape[0] // half
        row = lax.broadcasted_iota(jnp.int32, (HALF, rows), 0)
        isd = isd_ref[:, :1]
        pair = sums[0][nact + 2 : nact + 3, :LANES]
        for other in sums[1:]:
            pair = pair + other[nact + 2 : nact + 3, :LANES]
        lane = lax.broadcasted_iota(jnp.int32, (1, LANES), 1)
        mean = jnp.sum(jnp.where(lane < 3, pair, 0.0), 1, keepdims=True) / total_rows
        square = jnp.sum(jnp.where((lane >= 3) & (lane < 6), pair, 0.0), 1, keepdims=True) / total_rows
        spread = lax.rsqrt(square - mean * mean + NORM_EPS)
        std = jnp.zeros((HALF, rows), F32)
        head = jnp.zeros((HALF, part), F32)
        for r in range(team):
            here = slice(r * rows, (r + 1) * rows)
            total = sums[0][:, here]
            for s in range(1, team):
                total = total + sums[s][:, (r ^ s) * rows : ((r ^ s) + 1) * rows]
            rinv = lax.rsqrt(total[nact + 1 : nact + 2] / width + NORM_EPS)
            heads = total * rinv
            top = row_ref[:HALF, here].astype(F32)
            offset = jnp.where(row < nact, top - heads, 0.0)
            sample = row_ref[HALF:, here].astype(F32)
            advant = ((gae_of(row_ref[:HALF, here], nact) - mean) * spread).astype(BF16).astype(F32)
            ret = top[nact + 3 : nact + 4]
            logr = jnp.sum(
                -sample * offset * isd - 0.5 * offset * offset * isd * isd, 0, keepdims=True
            )
            ratio = jnp.exp(logr)
            clipped = jnp.clip(ratio, 1.0 - CLIP_EPS, 1.0 + CLIP_EPS)
            active = ratio * advant <= clipped * advant
            glogr = jnp.where(active, -scale * advant, 0.0) * ratio
            slope = sample * isd + offset * isd * isd
            ghead = jnp.where(
                row < nact, glogr * slope, jnp.where(row == nact, scale * (heads - ret), 0.0)
            )
            std = std + jnp.where(row < nact, glogr * slope * offset, 0.0)
            mean_gh = jnp.sum(ghead * heads, 0, keepdims=True) / width
            scaled = ghead * rinv
            high = high_refs[r // half][(r % half) * rows : (r % half + 1) * rows, :]
            both = dot(jnp.concatenate(split(scaled), 0), high)
            head = head + both[:HALF] + both[HALF:]
            turned = jnp.concatenate(
                [
                    scaled,
                    jnp.broadcast_to(rinv * rinv * mean_gh, (HALF, rows)),
                    jnp.zeros((LANES - 2 * HALF, rows), F32),
                ],
                0,
            ).T
            ghn = dot(jnp.concatenate(split(turned), 1), hw_ref[...])
            ghid_ref[here, :] = (
                ghn - high.astype(F32) * turned[:, HALF : HALF + 1]
            ).astype(BF16)
        row = lax.broadcasted_iota(jnp.int32, (HALF, part), 0)
        lane = lax.broadcasted_iota(jnp.int32, (HALF, part), 1)
        std = jnp.where(row == lane, jnp.sum(std, 1, keepdims=True), 0.0)
        std = jnp.sum(std, 0, keepdims=True)
        head = jnp.where(row == nact + 1, std, head)
        head_ref[...] = head
        for ref in (*firsts, direct_ref):
            ref[slab:, :] = jnp.concatenate(split(head), 0)

    grad = dot(turned_ref[...], ghid_ref[...])
    for k in range(line):

        @pl.when(step == k)
        def _(k=k):
            grads[k][...] = grad
            for ref, index in zip(firsts, first_blocks(line)):
                if k == index:
                    ref[:slab, :] = grad.astype(BF16)

    @pl.when(step == jnp.where(z == 0, line - 1, 1))
    def _():
        direct_ref[:slab, :] = grad.astype(BF16)


def first_blocks(line):
    return sorted({line - 2, 2})


def hop_kernel(head_ref, *refs):
    head = head_ref[...]
    for mine, got, send in zip(refs[:2], refs[2:4], refs[4:]):
        slab = mine.shape[0]
        send[:slab, :] = (mine[...] + got[:slab, :].astype(F32)).astype(BF16)
        send[slab:, :] = jnp.concatenate(split(head + joined(got, slab)), 0)


def joined(ref, slab):
    return ref[slab : slab + HALF, :].astype(F32) + ref[slab + HALF :, :].astype(F32)


def final_kernel(where_ref, mine_ref, head_ref, *refs):
    got, pieces = refs[:3], refs[3:]
    q = where_ref[0]
    slab = mine_ref.shape[0]
    kr = slab // len(pieces)
    head = head_ref[...]
    for ref in got:
        head = head + joined(ref, slab)
    for r, piece in enumerate(pieces):
        here = pl.ds(pl.multiple_of((q ^ r) * kr, kr), kr)
        total = mine_ref[here, :]
        for ref in got:
            total = total + ref[here, :].astype(F32)
        if r == 0:
            piece[:kr, :] = total
            piece[kr:, :] = head
        else:
            piece[:kr, :] = total.astype(BF16)
            piece[kr:, :] = jnp.concatenate(split(head), 0)


def assemble_kernel(where_ref, *refs):
    pieces, (grad_ref, head_ref, std_ref) = refs[:-3], refs[-3:]
    heads_n = head_ref.shape[0]
    q = where_ref[0]
    kr, part = grad_ref.shape[0], pieces[0].shape[1]
    for r, piece in enumerate(pieces):
        here = pl.ds(pl.multiple_of((q ^ r) * part, part), part)
        grad_ref[:, here] = piece[:kr, :].astype(F32)
        head = piece[kr:, :] if r == 0 else joined(piece, kr)
        head_ref[:, here] = head[:heads_n]
        if r == 0:
            std_ref[...] = head[heads_n : heads_n + 1, :LANES]


def plain(shape):
    return pl.BlockSpec(shape, lambda i: (0,) * len(shape))


def whole(shape):
    return pl.BlockSpec(shape, lambda i, w: (0,) * len(shape))


def local(
    obs_feat,
    reward,
    value_old,
    done,
    minibatch_perm,
    old_mean,
    noise,
    gain_in,
    out_weight,
    head_weight,
    log_std,
):
    n = lax.axis_size("fsdp")
    me = lax.axis_index("fsdp")
    team = 4
    line = n // team
    q = me % team
    z = me // team
    rows, width = obs_feat.shape
    part = width // team
    kr = out_weight.shape[0]
    slab = kr * team
    nact = log_std.shape[0]
    heads_n = nact + 1
    per_peer = rows // n
    total_rows = rows * n
    team_rows = team * rows
    where = jnp.stack([q, z]).astype(jnp.int32)

    def mate(x, r):
        return lax.ppermute(x, "fsdp", [(i, i ^ r) for i in range(n)]) if r else x

    def up(x, low, high):
        return lax.ppermute(
            x, "fsdp", [(a * team + b, (a + 1) * team + b) for a in range(low, high) for b in range(team)]
        )

    def down(x, low, high):
        return lax.ppermute(
            x, "fsdp", [(a * team + b, (a - 1) * team + b) for a in range(low, high) for b in range(team)]
        )

    def ends(x):
        far = n - team
        pairs = [(b, far + b) for b in range(team)] + [(far + b, b) for b in range(team)]
        return lax.ppermute(x, "fsdp", pairs)

    pieces = [
        mate(lax.dynamic_slice(out_weight, (0, (q ^ r) * part), (kr, part)), r) for r in range(team)
    ]
    x_core = mate(obs_feat, 1)
    small, pair = pl.pallas_call(
        functools.partial(small_kernel, nact, per_peer),
        out_shape=(
            jax.ShapeDtypeStruct((2 * HALF, rows), BF16),
            jax.ShapeDtypeStruct((HALF, part), BF16),
        ),
        grid=(1,),
        in_specs=[
            plain(reward.shape),
            plain(value_old.shape),
            plain(done.shape),
            plain((nact, rows)),
            plain((nact, rows)),
            plain((1, rows)),
        ],
        out_specs=[plain((2 * HALF, rows)), plain((HALF, part))],
        scratch_shapes=[pltpu.VMEM((reward.shape[0], LANES), F32), pltpu.VMEM((HALF, rows), F32)],
        compiler_params=params(),
        cost_estimate=CHEAP,
        name="small",
    )(reward, value_old, done, old_mean.T, noise.T, minibatch_perm[None, :])
    obs_late, x_core, small, pair, pieces = lax.optimization_barrier(
        (obs_feat, x_core, small, pair, pieces)
    )

    gain = gain_in[None, :]
    cut = rows // 3 * 2 if rows % 3 == 0 and rows // 3 % LANES == 0 else rows
    block = pl.pallas_call(
        join_kernel,
        out_shape=jax.ShapeDtypeStruct((slab + HALF, part), BF16),
        grid_spec=pltpu.PrefetchScalarGridSpec(
            num_scalar_prefetch=1,
            grid=(1,),
            in_specs=[whole((kr, part))] * team + [whole((HALF, part))],
            out_specs=whole((slab + HALF, part)),
        ),
        compiler_params=params(),
        cost_estimate=CHEAP,
        name="join",
    )(where, *pieces, pair)

    def norm(xs, start, apart=0):
        return norm_piece(where, xs, gain, start, apart, team_rows, part, buffers)

    direct = ends(block)
    fs, bs = [up(block, 0, line - 1)], [down(block, 1, line)]
    far = mate(obs_late[:cut], 2)
    small_core = mate(small, 1)
    buffers = None
    buffers = norm([obs_late], 0)
    buffers = norm([x_core], rows)
    direct, fs, bs, far, small, small_core, buffers, obs_late = lax.optimization_barrier(
        (direct, fs, bs, far, small, small_core, buffers, obs_late)
    )
    small = jnp.concatenate([small, small_core], 1)
    small_far = mate(small, 2)
    for j in range(2, line - 1):
        fs.append(up(fs[-1], j - 1, line - 1))
        bs.append(down(bs[-1], 1, line - j + 1))
    diag = mate(far, 1)
    late = mate(obs_late[cut:], 2) if cut < rows else far
    buffers = norm([far], 2 * rows)
    buffers = norm([diag], 3 * rows)
    fs, bs, late, small, small_far, buffers = lax.optimization_barrier(
        (fs, bs, late, small, small_far, buffers)
    )
    weights = [block] + fs + bs + [direct]

    hw = lax.dynamic_slice(head_weight, (q * part, 0), (part, heads_n)).T
    hw_twice = jnp.pad(hw, ((0, LANES - heads_n), (0, 0)))
    hw_wide = hw_twice.T
    hw_twice = jnp.concatenate([hw_twice, hw_twice], 0)
    isd = jnp.pad(jnp.exp(-log_std), (0, HALF - nact))
    isd = jnp.broadcast_to(isd[:, None], (HALF, LANES))

    packed = per_peer % 8 == 0 and team // 2 * per_peer % 16 == 0
    some = team // 2
    some_rows = some * rows

    def hidden(weights, first, rowdata):
        given = len(weights) == 1
        send_shape = (n, some * per_peer, part) if packed else (some_rows, part)
        out = pl.pallas_call(
            functools.partial(hidden_kernel, line, nact, packed, given),
            out_shape=[
                jax.ShapeDtypeStruct((some_rows, part), BF16),
                jax.ShapeDtypeStruct((HALF, some_rows), F32),
                jax.ShapeDtypeStruct(send_shape, BF16),
            ]
            + ([] if given else [jax.ShapeDtypeStruct((width, part), BF16)]),
            grid_spec=pltpu.PrefetchScalarGridSpec(
                num_scalar_prefetch=1,
                grid=(some,),
                in_specs=[whole(weight.shape) for weight in weights]
                + [
                    pl.BlockSpec((rows, width), lambda i, w: (first + i, 0)),
                    pl.BlockSpec((rows, part), lambda i, w: (first + i, 0)),
                    pl.BlockSpec((2 * HALF, rows), lambda i, w: (0, i)),
                    whole((part, LANES)),
                ],
                out_specs=[
                    pl.BlockSpec((rows, part), lambda i, w: (i, 0)),
                    pl.BlockSpec((HALF, rows), lambda i, w: (0, i)),
                    whole(send_shape) if packed else pl.BlockSpec((rows, part), lambda i, w: (i, 0)),
                ]
                + ([] if given else [whole((width, part))]),
                scratch_shapes=[pltpu.VMEM((some_rows, part), F32)] if packed else [],
            ),
            compiler_params=params(),
            cost_estimate=CHEAP,
            name="hidden",
        )(where, *weights, normed, xq, rowdata, hw_wide)
        if not packed:
            high, sums, send, *weight = out
            send = send.reshape(some, n, per_peer, part).transpose(1, 0, 2, 3)
            return high, sums, send.reshape(n, some * per_peer, part), *weight
        return out

    def scatter(send):
        return lax.all_to_all(send, "fsdp", split_axis=0, concat_axis=0, tiled=True)

    normed, turned, xq = buffers
    high_near, sums_near, send, weight = hidden(weights, 0, small)
    recv_near = scatter(send)
    if cut < rows:
        last = mate(late, 1)
        late, last, sums_near, buffers = lax.optimization_barrier((late, last, sums_near, buffers))
        buffers = norm([late, last], 2 * rows + cut, rows)
        normed, turned, xq = buffers
    high_far, sums_far, send, *_ = hidden([weight], some, small_far)
    sums = jnp.concatenate([sums_near, sums_far], 1)
    sums = [mate(sums, r) for r in range(team)]
    send, recv_near, *sums = lax.optimization_barrier((send, recv_near, *sums))
    recv_far = scatter(send)
    small = jnp.concatenate([small, small_far], 1)

    nfirst = len(first_blocks(line))
    outs = pl.pallas_call(
        functools.partial(rest_kernel, line, team, nact, width, total_rows),
        out_shape=[jax.ShapeDtypeStruct((slab, part), F32)] * line
        + [jax.ShapeDtypeStruct((slab + 2 * HALF, part), BF16)] * (nfirst + 1)
        + [jax.ShapeDtypeStruct((HALF, part), F32)],
        grid_spec=pltpu.PrefetchScalarGridSpec(
            num_scalar_prefetch=1,
            grid=(line,),
            in_specs=[whole((HALF, team_rows))] * team
            + [
                whole((2 * HALF, team_rows)),
                whole((HALF, LANES)),
                whole((some_rows, part)),
                whole((some_rows, part)),
                whole((2 * LANES, part)),
                pl.BlockSpec((slab, team_rows), lambda i, w: (lax.rem(w[1] + i, line), 0)),
            ],
            out_specs=[whole((slab, part))] * line
            + [whole((slab + 2 * HALF, part))] * (nfirst + 1)
            + [whole((HALF, part))],
            scratch_shapes=[pltpu.VMEM((team_rows, part), BF16)],
        ),
        compiler_params=params(),
        cost_estimate=CHEAP,
        name="rest",
    )(where, *sums, small, isd, high_near, high_far, hw_twice, turned)
    grads, firsts, direct, head = outs[:line], outs[line:-2], outs[-2], outs[-1]

    def hop(*operands):
        return pl.pallas_call(
            hop_kernel,
            out_shape=[jax.ShapeDtypeStruct((slab + 2 * HALF, part), BF16)] * 2,
            grid=(1,),
            in_specs=[plain((HALF, part))] + [plain((slab, part))] * 2 + [plain((slab + 2 * HALF, part))] * 2,
            out_specs=[plain((slab + 2 * HALF, part))] * 2,
            compiler_params=params(),
            cost_estimate=CHEAP,
            name="hop",
        )(head, *operands)

    direct = ends(direct)
    send_f, send_b = firsts[-1], firsts[0]
    for k in range(line - 2, 0, -1):
        got_f = up(send_f, 0, line - k)
        got_b = down(send_b, k, line)
        if k == 2:
            got_f, got_b, recv_far = lax.optimization_barrier((got_f, got_b, recv_far))
        if k > 1:
            send_f, send_b = hop(grads[k - 1], grads[line - k + 1], got_f, got_b)
    pieces = pl.pallas_call(
        final_kernel,
        out_shape=[jax.ShapeDtypeStruct((kr + HALF, part), F32)]
        + [jax.ShapeDtypeStruct((kr + 2 * HALF, part), BF16)] * (team - 1),
        grid_spec=pltpu.PrefetchScalarGridSpec(
            num_scalar_prefetch=1,
            grid=(1,),
            in_specs=[whole((slab, part)), whole((HALF, part))]
            + [whole((slab + 2 * HALF, part))] * 3,
            out_specs=[whole((kr + HALF, part))] + [whole((kr + 2 * HALF, part))] * (team - 1),
        ),
        compiler_params=params(),
        cost_estimate=CHEAP,
        name="final",
    )(where, grads[0], head, got_f, got_b, direct)
    pieces = [mate(piece, r) for r, piece in enumerate(pieces)]
    grad_weight, heads, std = pl.pallas_call(
        assemble_kernel,
        out_shape=(
            jax.ShapeDtypeStruct((kr, width), F32),
            jax.ShapeDtypeStruct((heads_n, width), F32),
            jax.ShapeDtypeStruct((1, LANES), F32),
        ),
        grid_spec=pltpu.PrefetchScalarGridSpec(
            num_scalar_prefetch=1,
            grid=(1,),
            in_specs=[whole(piece.shape) for piece in pieces],
            out_specs=[whole((kr, width)), whole((heads_n, width)), whole((1, LANES))],
        ),
        compiler_params=params(),
        cost_estimate=CHEAP,
        name="assemble",
    )(where, *pieces)
    grad_head = heads.T
    grad_std = std[0, :nact]

    recv_near = recv_near.reshape(line, team, some, per_peer, part)
    recv_far = recv_far.reshape(line, team, some, per_peer, part)

    def from_member(c, m):
        r = c ^ m
        return recv_near[:, c, r] if r < some else recv_far[:, c, r - some]

    hidden_out = jnp.concatenate(
        [jnp.stack([from_member(c, m) for m in range(team)], 1) for c in range(team)], -1
    ).reshape(rows, width)
    return (hidden_out, grad_weight, grad_head, grad_std)


def solution(mesh):
    return jax.shard_map(
        local,
        mesh=mesh,
        in_specs=(
            P(("groups", "fsdp"), None),
            P(("groups", "fsdp"), None),
            P(("groups", "fsdp"), None),
            P(("groups", "fsdp"), None),
            P(("groups", "fsdp")),
            P(("groups", "fsdp"), None),
            P(("groups", "fsdp"), None),
            P(),
            P("fsdp", None),
            P(),
            P(),
        ),
        out_specs=(
            P(("groups", "fsdp"), None),
            P(("groups", "fsdp"), None),
            P("groups", None),
            P("groups"),
        ),
        check_vma=False,
    )
```

```python
import functools

import jax
import jax.numpy as jnp
from jax import lax
from jax.experimental import pallas as pl
from jax.experimental.pallas import tpu as pltpu
from jax.sharding import PartitionSpec as P

GAMMA = 0.99
LAMBDA_GAE = 0.95
CLIP_EPS = 0.2
NORM_EPS = 1e-05
F32 = jnp.float32
BF16 = jnp.bfloat16
LANES = 128
HALF = 16
MIB = 1024 * 1024
CHEAP = pl.CostEstimate(flops=1, bytes_accessed=1, transcendentals=0)


def params(mib=50):
    return pltpu.CompilerParams(vmem_limit_bytes=mib * MIB, dimension_semantics=("arbitrary",))


def split(x):
    high = x.astype(BF16)
    return high, (x - high.astype(F32)).astype(BF16)


def dot(a, b):
    return jnp.dot(a, b, preferred_element_type=F32)


def dot_t(a, b):
    return lax.dot_general(a, b, (((1,), (1,)), ((), ())), preferred_element_type=F32)


def shifted(x, by):
    return pltpu.roll(x, LANES - by, 1)


def small_kernel(
    nact, per_peer, reward_ref, value_ref, done_ref, old_ref, noise_ref, perm_ref, small_ref, pair_ref, pad_ref, tall_ref
):
    envs, steps = reward_ref.shape
    rows = perm_ref.shape[1]

    def wide(x):
        pad_ref[...] = jnp.zeros_like(pad_ref)
        pad_ref[:, : x.shape[1]] = x
        return pad_ref[...]

    inside = lax.broadcasted_iota(jnp.int32, (envs, LANES), 1) < steps
    value = wide(value_ref[...])
    keep = 1.0 - wide(done_ref[...].astype(F32))
    delta = wide(reward_ref[...]) + GAMMA * shifted(value, 1) * keep - value
    gae = jnp.where(inside, delta, 0.0)
    factor = jnp.where(inside, GAMMA * LAMBDA_GAE * keep, 0.0)
    reach = 1
    while reach < steps:
        gae = gae + factor * shifted(gae, reach)
        factor = factor * shifted(factor, reach)
        reach *= 2
    ret = gae + value
    high, low = split(gae)
    mid, low = split(gae - high.astype(F32))
    lane = lax.broadcasted_iota(jnp.int32, (LANES, rows), 1)
    pick = jnp.where(
        lax.rem(lane, steps) == lax.broadcasted_iota(jnp.int32, (LANES, rows), 0), 1.0, 0.0
    ).astype(BF16)
    lane = lax.broadcasted_iota(jnp.int32, (envs, rows), 1)
    mine = lane // steps == lax.broadcasted_iota(jnp.int32, (envs, rows), 0)

    def flat(x):
        return jnp.sum(jnp.where(mine, dot(x, pick), 0.0), 0, keepdims=True)

    perm = perm_ref[...]
    slot = perm // rows * per_peer + lax.rem(perm, per_peer)
    row = lax.broadcasted_iota(jnp.int32, (HALF, rows), 0)

    def put(block, index, values):
        return jnp.where(row == index, values, block)

    def tall(x):
        tall_ref[...] = jnp.zeros_like(tall_ref)
        tall_ref[:nact, :] = x.astype(F32)
        return tall_ref[...]

    top = tall(old_ref[...])
    for index, values in enumerate((high, mid, low, ret.astype(BF16))):
        top = put(top, nact + index, flat(values))
    bottom = tall(noise_ref[...])
    bottom = put(bottom, nact, (slot // 256).astype(F32))
    bottom = put(bottom, nact + 1, lax.rem(slot, 256).astype(F32))
    small = jnp.concatenate([top, bottom], 0).astype(BF16)
    small_ref[...] = small
    gae = gae_of(small[:HALF], nact)
    lane = lax.broadcasted_iota(jnp.int32, pair_ref.shape, 1)
    pair = jnp.zeros(pair_ref.shape, F32)
    for first, value in ((0, gae), (3, gae * gae)):
        value = jnp.sum(value, 1, keepdims=True)
        for i in range(3):
            rounded = value.astype(BF16).astype(F32)
            pair = jnp.where(lane == first + i, rounded, pair)
            value = value - rounded
    pair_ref[...] = pair.astype(BF16)


def gae_of(small, nact):
    block = small.astype(F32)
    return block[nact : nact + 1] + block[nact + 1 : nact + 2] + block[nact + 2 : nact + 3]


def join_kernel(where_ref, *refs):
    pieces, pair_ref, block_ref = refs[:-2], refs[-2], refs[-1]
    kr = pieces[0].shape[0]
    for r, piece in enumerate(pieces):
        here = pl.ds(pl.multiple_of((where_ref[0] ^ r) * kr, kr), kr)
        block_ref[here, :] = piece[...]
    block_ref[kr * len(pieces) :, :] = pair_ref[...]


def norm_kernel(*refs):
    x_refs, gain_ref, normed_ref, turned_ref = refs[:-3], refs[-3], refs[-2], refs[-1]

    def one(x):
        xf = x.astype(F32)
        rms = lax.rsqrt(jnp.mean(xf * xf, -1, keepdims=True) + NORM_EPS)
        normed = xf * rms * gain_ref[...]
        normed_ref[...] = normed.astype(BF16)
        turned_ref[...] = normed.T.astype(BF16)

    if len(x_refs) == 1:
        one(x_refs[0][...])
    else:
        for i, ref in enumerate(x_refs):
            pl.when(pl.program_id(0) == i)(functools.partial(lambda ref: one(ref[...]), ref))


def norm(xs, gain):
    rows, width = xs[0].shape
    grid = rows // LANES if len(xs) == 1 else len(xs)
    source = (lambda i: (i, 0)) if len(xs) == 1 else (lambda i: (0, 0))
    return pl.pallas_call(
        norm_kernel,
        out_shape=(
            jax.ShapeDtypeStruct((rows * len(xs), width), BF16),
            jax.ShapeDtypeStruct((width, rows * len(xs)), BF16),
        ),
        grid=(grid,),
        in_specs=[pl.BlockSpec((LANES, width), source)] * len(xs)
        + [pl.BlockSpec((1, width), lambda i: (0, 0))],
        out_specs=[
            pl.BlockSpec((LANES, width), lambda i: (i, 0)),
            pl.BlockSpec((width, LANES), lambda i: (0, i)),
        ],
        compiler_params=params(58),
        cost_estimate=CHEAP,
        name="norm",
    )(*xs, gain)


def hidden_kernel(line, nact, packed, given, layout, where_ref, *refs):
    count = 1 if given else 2 * line - 3
    weights, refs = refs[:count], refs[count:]
    n_x = 1 + max(p[0] for pieces in layout for p in pieces)
    n_normed = 1 + max(p[1] for pieces in layout for p in pieces)
    xq_refs, refs = refs[:n_x], refs[n_x:]
    normed_refs, refs = refs[:n_normed], refs[n_normed:]
    row_ref, hw_ref, high_ref, sums_ref, send_ref = refs[:5]
    w_ref = weights[0] if given else refs[5]
    sorted_ref = refs[-1]
    z = where_ref[1]
    members = len(layout)
    rows = high_ref.shape[0] // members
    slab = w_ref.shape[0] // line

    if not given:
        own, fwd, bwd = weights[0], weights[1 : line - 1], weights[line - 1 :]
        w_ref[pl.ds(pl.multiple_of(z * slab, slab), slab), :] = own[:slab, :]
        for j in range(1, line):
            place = pl.multiple_of(lax.rem(z - j + line, line) * slab, slab)
            if j == 1:
                block = fwd[0][:slab, :]
            elif j == line - 1:
                block = bwd[0][:slab, :]
            else:
                block = jnp.where(z >= j, fwd[j - 1][:slab, :], bwd[line - j - 1][:slab, :])
            w_ref[pl.ds(place, slab), :] = block

    for m, pieces in enumerate(layout):
        at = m * rows
        for x, normed, first, size in pieces:
            piece = dot(normed_refs[normed][first : first + size, :], w_ref[...])
            sorted_ref[at : at + size, :] = piece + xq_refs[x][...].astype(F32)
            at += size
        here = slice(m * rows, (m + 1) * rows)
        hidden = sorted_ref[here, :]
        high, low = split(hidden)
        high_ref[here, :] = high
        heads = dot(high, hw_ref[...]) + dot(low, hw_ref[...])
        lane = lax.broadcasted_iota(jnp.int32, heads.shape, 1)
        square = jnp.sum(hidden * hidden, 1, keepdims=True)
        sums = jnp.where(lane == nact + 1, square, heads).T[:HALF]
        if not given:
            pair = jnp.zeros((HALF, LANES), F32)
            for ref in weights:
                pair = pair + ref[slab:, :LANES].astype(F32)
            pair = jnp.concatenate([pair[:1], jnp.zeros((1, rows - LANES), F32)], 1)
            row = lax.broadcasted_iota(jnp.int32, sums.shape, 0)
            sums = jnp.where(row == nact + 2, pair, sums)
        sums_ref[:, here] = sums
        slot = row_ref[HALF + nact : HALF + nact + 1, here].astype(F32) * 256.0
        slot = slot + row_ref[HALF + nact + 1 : HALF + nact + 2, here].astype(F32)
        slot = slot.astype(jnp.int32)
        order = lax.broadcasted_iota(jnp.int32, (rows, rows), 0) == slot
        ranked = dot(jnp.where(order, 1.0, 0.0).astype(BF16), high)
        if packed:
            sorted_ref[here, :] = ranked
        else:
            send_ref[here, :] = ranked.astype(BF16)
    if packed:
        n, size, _ = send_ref.shape
        peer = size // members
        for j in range(n):
            send_ref[j] = jnp.concatenate(
                [sorted_ref[r * rows + j * peer : r * rows + (j + 1) * peer, :] for r in range(members)],
                0,
            ).astype(BF16)


def rest_kernel(line, team, nact, width, total_rows, places, where_ref, *refs):
    sums, refs = refs[:team], refs[team:]
    row_ref, isd_ref, *high_refs = refs[:4]
    hw_ref, *turned_refs = refs[4:10]
    grad_ref = refs[10]
    firsts, (head_ref, ghid_ref) = refs[11:-2], refs[-2:]
    step = pl.program_id(0)
    scale = total_rows**-0.5
    slab, part = grad_ref.shape

    @pl.when(step == 0)
    def _():
        half = team // 2
        rows = high_refs[0].shape[0] // half
        row = lax.broadcasted_iota(jnp.int32, (HALF, rows), 0)
        isd = isd_ref[:, :1]
        pair = sums[0][nact + 2 : nact + 3, :LANES]
        for other in sums[1:]:
            pair = pair + other[nact + 2 : nact + 3, :LANES]
        lane = lax.broadcasted_iota(jnp.int32, (1, LANES), 1)
        mean = jnp.sum(jnp.where(lane < 3, pair, 0.0), 1, keepdims=True) / total_rows
        square = jnp.sum(jnp.where((lane >= 3) & (lane < 6), pair, 0.0), 1, keepdims=True) / total_rows
        spread = lax.rsqrt(square - mean * mean + NORM_EPS)
        std = jnp.zeros((HALF, rows), F32)
        head = jnp.zeros((HALF, part), F32)
        for r in range(team):
            here = slice(r * rows, (r + 1) * rows)
            total = sums[0][:, here]
            for s in range(1, team):
                total = total + sums[s][:, (r ^ s) * rows : ((r ^ s) + 1) * rows]
            rinv = lax.rsqrt(total[nact + 1 : nact + 2] / width + NORM_EPS)
            heads = total * rinv
            top = row_ref[:HALF, here].astype(F32)
            offset = jnp.where(row < nact, top - heads, 0.0)
            sample = row_ref[HALF:, here].astype(F32)
            advant = ((gae_of(row_ref[:HALF, here], nact) - mean) * spread).astype(BF16).astype(F32)
            ret = top[nact + 3 : nact + 4]
            logr = jnp.sum(
                -sample * offset * isd - 0.5 * offset * offset * isd * isd, 0, keepdims=True
            )
            ratio = jnp.exp(logr)
            clipped = jnp.clip(ratio, 1.0 - CLIP_EPS, 1.0 + CLIP_EPS)
            active = ratio * advant <= clipped * advant
            glogr = jnp.where(active, -scale * advant, 0.0) * ratio
            slope = sample * isd + offset * isd * isd
            ghead = jnp.where(
                row < nact, glogr * slope, jnp.where(row == nact, scale * (heads - ret), 0.0)
            )
            std = std + jnp.where(row < nact, glogr * slope * offset, 0.0)
            mean_gh = jnp.sum(ghead * heads, 0, keepdims=True) / width
            scaled = ghead * rinv
            high = high_refs[r // half][(r % half) * rows : (r % half + 1) * rows, :]
            both = dot(jnp.concatenate(split(scaled), 0), high)
            head = head + both[:HALF] + both[HALF:]
            turned = jnp.concatenate(
                [
                    scaled,
                    jnp.broadcast_to(rinv * rinv * mean_gh, (HALF, rows)),
                    jnp.zeros((LANES - 2 * HALF, rows), F32),
                ],
                0,
            ).T
            ghn = dot(jnp.concatenate(split(turned), 1), hw_ref[...])
            ghid = (ghn - high.astype(F32) * turned[:, HALF : HALF + 1]).astype(BF16)
            for first, size, place in places[r]:
                ghid_ref[place : place + size, :] = ghid[first : first + size]
        row = lax.broadcasted_iota(jnp.int32, (HALF, part), 0)
        lane = lax.broadcasted_iota(jnp.int32, (HALF, part), 1)
        std = jnp.where(row == lane, jnp.sum(std, 1, keepdims=True), 0.0)
        std = jnp.sum(std, 0, keepdims=True)
        head = jnp.where(row == nact + 1, std, head)
        head_ref[...] = head
        for ref in firsts:
            ref[slab:, :] = jnp.concatenate(split(head), 0)

    grad = dot(jnp.concatenate([ref[...] for ref in turned_refs], 1), ghid_ref[...])
    grad_ref[...] = grad
    for ref, index in zip(firsts, first_blocks(line)):

        @pl.when(step == index)
        def _(ref=ref):
            ref[:slab, :] = grad.astype(BF16)


def first_blocks(line):
    return sorted({line - 2, 2})


def hop_kernel(head_ref, *refs):
    head = head_ref[...]
    for mine, got, send in zip(refs[:2], refs[2:4], refs[4:]):
        slab = mine.shape[0]
        send[:slab, :] = (mine[...] + got[:slab, :].astype(F32)).astype(BF16)
        send[slab:, :] = jnp.concatenate(split(head + joined(got, slab)), 0)


def joined(ref, slab):
    return ref[slab : slab + HALF, :].astype(F32) + ref[slab + HALF :, :].astype(F32)


def final_kernel(where_ref, mine_ref, head_ref, *refs):
    got, pieces = refs[:2], refs[2:]
    q = where_ref[0]
    slab = mine_ref.shape[0]
    kr = slab // len(pieces)
    head = head_ref[...]
    for ref in got:
        head = head + joined(ref, slab)
    for r, piece in enumerate(pieces):
        here = pl.ds(pl.multiple_of((q ^ r) * kr, kr), kr)
        total = mine_ref[here, :]
        for ref in got:
            total = total + ref[here, :].astype(F32)
        if r == 0:
            piece[:kr, :] = total
            piece[kr:, :] = head
        else:
            piece[:kr, :] = total.astype(BF16)
            piece[kr:, :] = jnp.concatenate(split(head), 0)


def assemble_kernel(where_ref, *refs):
    pieces, (grad_ref, head_ref, std_ref) = refs[:-3], refs[-3:]
    heads_n = head_ref.shape[0]
    q = where_ref[0]
    kr, part = grad_ref.shape[0], pieces[0].shape[1]
    for r, piece in enumerate(pieces):
        here = pl.ds(pl.multiple_of((q ^ r) * part, part), part)
        grad_ref[:, here] = piece[:kr, :].astype(F32)
        head = piece[kr:, :] if r == 0 else joined(piece, kr)
        head_ref[:, here] = head[:heads_n]
        if r == 0:
            std_ref[...] = head[heads_n : heads_n + 1, :LANES]


def plain(shape):
    return pl.BlockSpec(shape, lambda i: (0,) * len(shape))


def whole(shape):
    return pl.BlockSpec(shape, lambda i, w: (0,) * len(shape))


def local(
    obs_feat,
    reward,
    value_old,
    done,
    minibatch_perm,
    old_mean,
    noise,
    gain_in,
    out_weight,
    head_weight,
    log_std,
):
    n = lax.axis_size("fsdp")
    me = lax.axis_index("fsdp")
    team = 4
    line = n // team
    q = me % team
    z = me // team
    rows, width = obs_feat.shape
    part = width // team
    kr = out_weight.shape[0]
    slab = kr * team
    nact = log_std.shape[0]
    heads_n = nact + 1
    per_peer = rows // n
    total_rows = rows * n
    team_rows = team * rows
    where = jnp.stack([q, z]).astype(jnp.int32)

    def mate(x, r):
        return lax.ppermute(x, "fsdp", [(i, i ^ r) for i in range(n)]) if r else x

    def up(x, low, high, wrap=False):
        steps = [(a, a + 1) for a in range(low, high)] + ([(line - 1, 0)] if wrap else [])
        return lax.ppermute(x, "fsdp", [(a * team + i, b * team + i) for a, b in steps for i in range(team)])

    def down(x, low, high, wrap=False):
        steps = [(a, a - 1) for a in range(low, high)] + ([(0, line - 1)] if wrap else [])
        return lax.ppermute(x, "fsdp", [(a * team + i, b * team + i) for a, b in steps for i in range(team)])

    pieces = [
        mate(lax.dynamic_slice(out_weight, (0, (q ^ r) * part), (kr, part)), r) for r in range(team)
    ]
    x_core = mate(obs_feat, 1)
    small, pair = pl.pallas_call(
        functools.partial(small_kernel, nact, per_peer),
        out_shape=(
            jax.ShapeDtypeStruct((2 * HALF, rows), BF16),
            jax.ShapeDtypeStruct((HALF, part), BF16),
        ),
        grid=(1,),
        in_specs=[
            plain(reward.shape),
            plain(value_old.shape),
            plain(done.shape),
            plain((nact, rows)),
            plain((nact, rows)),
            plain((1, rows)),
        ],
        out_specs=[plain((2 * HALF, rows)), plain((HALF, part))],
        scratch_shapes=[pltpu.VMEM((reward.shape[0], LANES), F32), pltpu.VMEM((HALF, rows), F32)],
        compiler_params=params(60),
        cost_estimate=CHEAP,
        name="small",
    )(reward, value_old, done, old_mean.T, noise.T, minibatch_perm[None, :])
    cut = rows - LANES
    obs_first = obs_feat[:cut]
    x_core, small, pair, pieces, where, obs_first, obs_late, head_weight, log_std = (
        lax.optimization_barrier(
            (x_core, small, pair, pieces, where, obs_first, obs_feat, head_weight, log_std)
        )
    )
    obs_last = obs_late[cut:]

    hw = lax.dynamic_slice(head_weight, (q * part, 0), (part, heads_n)).T
    hw_twice = jnp.pad(hw, ((0, LANES - heads_n), (0, 0)))
    hw_wide = hw_twice.T
    hw_twice = jnp.concatenate([hw_twice, hw_twice], 0)
    isd = jnp.pad(jnp.exp(-log_std), (0, HALF - nact))
    isd = jnp.broadcast_to(isd[:, None], (HALF, LANES))

    gain = gain_in[None, :]
    block = pl.pallas_call(
        join_kernel,
        out_shape=jax.ShapeDtypeStruct((slab + HALF, part), BF16),
        grid_spec=pltpu.PrefetchScalarGridSpec(
            num_scalar_prefetch=1,
            grid=(1,),
            in_specs=[whole((kr, part))] * team + [whole((HALF, part))],
            out_specs=whole((slab + HALF, part)),
        ),
        compiler_params=params(),
        cost_estimate=CHEAP,
        name="join",
    )(where, *pieces, pair)

    fs, bs = [up(block, 0, line - 1, True)], [down(block, 1, line, True)]
    far = mate(obs_first, 2)
    small_core = mate(small, 1)
    obs_late, small_core = lax.optimization_barrier((obs_late, small_core))
    normed_own, normed_core = norm([obs_late], gain), norm([x_core], gain)
    (fs, bs, far, small, small_core, normed_own, normed_core, obs_last, hw_wide, hw_twice, isd) = (
        lax.optimization_barrier(
            (fs, bs, far, small, small_core, normed_own, normed_core, obs_last, hw_wide, hw_twice, isd)
        )
    )
    small = jnp.concatenate([small, small_core], 1)
    small_far = mate(small, 2)
    for j in range(2, line - 1):
        fs.append(up(fs[-1], j - 1, line - 1))
        bs.append(down(bs[-1], 1, line - j + 1))
    diag = mate(far, 1)
    late = mate(obs_last, 2)
    normed_far, normed_diag = norm([far], gain), norm([diag], gain)
    fs, bs, late, small, small_far, normed_far, normed_diag = lax.optimization_barrier(
        (fs, bs, late, small, small_far, normed_far, normed_diag)
    )
    weights = [block] + fs + bs

    packed = per_peer % 8 == 0 and team // 2 * per_peer % 16 == 0
    some = team // 2
    some_rows = some * rows

    def hidden(weights, xs, normed, layout, rowdata):
        given = len(weights) == 1
        send_shape = (n, some * per_peer, part) if packed else (some_rows, part)
        out = pl.pallas_call(
            functools.partial(hidden_kernel, line, nact, packed, given, layout),
            out_shape=[
                jax.ShapeDtypeStruct((some_rows, part), BF16),
                jax.ShapeDtypeStruct((HALF, some_rows), F32),
                jax.ShapeDtypeStruct(send_shape, BF16),
            ]
            + ([] if given else [jax.ShapeDtypeStruct((width, part), BF16)]),
            grid_spec=pltpu.PrefetchScalarGridSpec(
                num_scalar_prefetch=1,
                grid=(1,),
                in_specs=[whole(weight.shape) for weight in weights]
                + [pl.BlockSpec((x.shape[0], part), lambda i, w: (0, w[0])) for x in xs]
                + [whole(x.shape) for x in normed]
                + [whole((2 * HALF, some_rows)), whole((part, LANES))],
                out_specs=[whole((some_rows, part)), whole((HALF, some_rows)), whole(send_shape)]
                + ([] if given else [whole((width, part))]),
                scratch_shapes=[pltpu.VMEM((some_rows, part), F32)],
            ),
            compiler_params=params(58),
            cost_estimate=CHEAP,
            name="hidden",
        )(where, *weights, *xs, *normed, rowdata, hw_wide)
        if not packed:
            high, sums, send, *weight = out
            send = send.reshape(some, n, per_peer, part).transpose(1, 0, 2, 3)
            return high, sums, send.reshape(n, some * per_peer, part), *weight
        return out

    def scatter(send):
        return lax.all_to_all(send, "fsdp", split_axis=0, concat_axis=0, tiled=True)

    small_all = jnp.concatenate([small, small_far], 1)
    layout = [[(0, 0, 0, rows)], [(1, 1, 0, rows)]]
    high_near, sums_near, send, weight = hidden(
        weights, [obs_feat, x_core], [normed_own[0], normed_core[0]], layout, small
    )
    recv_near = scatter(send)
    last = mate(late, 1)
    late, last, sums_near, small_all = lax.optimization_barrier((late, last, sums_near, small_all))
    normed_last = norm([late, last], gain)
    layout = [[(0, 0, 0, cut), (2, 2, 0, LANES)], [(1, 1, 0, cut), (3, 2, LANES, LANES)]]
    high_far, sums_far, send, *_ = hidden(
        [weight],
        [far, diag, late, last],
        [normed_far[0], normed_diag[0], normed_last[0]],
        layout,
        small_far,
    )
    sums = jnp.concatenate([sums_near, sums_far], 1)
    sums = [mate(sums, r) for r in range(team)]
    send, recv_near, *sums = lax.optimization_barrier((send, recv_near, *sums))
    recv_far = scatter(send)
    nfirst = len(first_blocks(line))
    turned = [pair[1] for pair in (normed_own, normed_core, normed_far, normed_diag, normed_last)]
    places = [[(0, rows, 0)], [(0, rows, rows)]] + [
        [(0, cut, 2 * rows + i * cut), (cut, LANES, 2 * rows + 2 * cut + i * LANES)] for i in range(2)
    ]
    outs = pl.pallas_call(
        functools.partial(rest_kernel, line, team, nact, width, total_rows, places),
        out_shape=[jax.ShapeDtypeStruct((width, part), F32)]
        + [jax.ShapeDtypeStruct((slab + 2 * HALF, part), BF16)] * nfirst
        + [jax.ShapeDtypeStruct((HALF, part), F32)],
        grid_spec=pltpu.PrefetchScalarGridSpec(
            num_scalar_prefetch=1,
            grid=(line,),
            in_specs=[whole((HALF, team_rows))] * team
            + [
                whole((2 * HALF, team_rows)),
                whole((HALF, LANES)),
                whole((some_rows, part)),
                whole((some_rows, part)),
                whole((2 * LANES, part)),
            ]
            + [
                pl.BlockSpec((slab, piece.shape[1]), lambda i, w: (lax.rem(w[1] + i, line), 0))
                for piece in turned
            ],
            out_specs=[pl.BlockSpec((slab, part), lambda i, w: (i, 0))]
            + [whole((slab + 2 * HALF, part))] * nfirst
            + [whole((HALF, part))],
            scratch_shapes=[pltpu.VMEM((team_rows, part), BF16)],
        ),
        compiler_params=params(58),
        cost_estimate=CHEAP,
        name="rest",
    )(where, *sums, small_all, isd, high_near, high_far, hw_twice, *turned)
    grads, firsts, head = outs[0], outs[1:-1], outs[-1]

    def hop(up_block, down_block, *got):
        return pl.pallas_call(
            hop_kernel,
            out_shape=[jax.ShapeDtypeStruct((slab + 2 * HALF, part), BF16)] * 2,
            grid=(1,),
            in_specs=[
                plain((HALF, part)),
                pl.BlockSpec((slab, part), lambda i: (up_block, 0)),
                pl.BlockSpec((slab, part), lambda i: (down_block, 0)),
            ]
            + [plain((slab + 2 * HALF, part))] * 2,
            out_specs=[plain((slab + 2 * HALF, part))] * 2,
            compiler_params=params(),
            cost_estimate=CHEAP,
            name="hop",
        )(head, grads, grads, *got)

    send_f, send_b = firsts[-1], firsts[0]
    for k in range(line - 2, 0, -1):
        got_f = up(send_f, 0, line - k, k == 1)
        got_b = down(send_b, k, line, k == 1)
        if k == 2:
            got_f, got_b, recv_far = lax.optimization_barrier((got_f, got_b, recv_far))
        if k > 1:
            send_f, send_b = hop(k - 1, line - k + 1, got_f, got_b)
    pieces = pl.pallas_call(
        final_kernel,
        out_shape=[jax.ShapeDtypeStruct((kr + HALF, part), F32)]
        + [jax.ShapeDtypeStruct((kr + 2 * HALF, part), BF16)] * (team - 1),
        grid_spec=pltpu.PrefetchScalarGridSpec(
            num_scalar_prefetch=1,
            grid=(1,),
            in_specs=[whole((slab, part)), whole((HALF, part))]
            + [whole((slab + 2 * HALF, part))] * 2,
            out_specs=[whole((kr + HALF, part))] + [whole((kr + 2 * HALF, part))] * (team - 1),
        ),
        compiler_params=params(),
        cost_estimate=CHEAP,
        name="final",
    )(where, grads, head, got_f, got_b)
    pieces = [mate(piece, r) for r, piece in enumerate(pieces)]
    grad_weight, heads, std = pl.pallas_call(
        assemble_kernel,
        out_shape=(
            jax.ShapeDtypeStruct((kr, width), F32),
            jax.ShapeDtypeStruct((heads_n, width), F32),
            jax.ShapeDtypeStruct((1, LANES), F32),
        ),
        grid_spec=pltpu.PrefetchScalarGridSpec(
            num_scalar_prefetch=1,
            grid=(1,),
            in_specs=[whole(piece.shape) for piece in pieces],
            out_specs=[whole((kr, width)), whole((heads_n, width)), whole((1, LANES))],
        ),
        compiler_params=params(),
        cost_estimate=CHEAP,
        name="assemble",
    )(where, *pieces)
    grad_head = heads.T
    grad_std = std[0, :nact]

    recv_near = recv_near.reshape(line, team, some, per_peer, part)
    recv_far = recv_far.reshape(line, team, some, per_peer, part)

    def from_member(c, m):
        r = c ^ m
        return recv_near[:, c, r] if r < some else recv_far[:, c, r - some]

    hidden_out = jnp.concatenate(
        [jnp.stack([from_member(c, m) for m in range(team)], 1) for c in range(team)], -1
    ).reshape(rows, width)
    return (hidden_out, grad_weight, grad_head, grad_std)


def solution(mesh):
    return jax.shard_map(
        local,
        mesh=mesh,
        in_specs=(
            P(("groups", "fsdp"), None),
            P(("groups", "fsdp"), None),
            P(("groups", "fsdp"), None),
            P(("groups", "fsdp"), None),
            P(("groups", "fsdp")),
            P(("groups", "fsdp"), None),
            P(("groups", "fsdp"), None),
            P(),
            P("fsdp", None),
            P(),
            P(),
        ),
        out_specs=(
            P(("groups", "fsdp"), None),
            P(("groups", "fsdp"), None),
            P("groups", None),
            P("groups"),
        ),
        check_vma=False,
    )
```

```python
import functools

import jax
import jax.numpy as jnp
from jax import lax
from jax.experimental import pallas as pl
from jax.experimental.pallas import tpu as pltpu
from jax.sharding import PartitionSpec as P

GAMMA = 0.99
LAMBDA_GAE = 0.95
CLIP_EPS = 0.2
NORM_EPS = 1e-05
F32 = jnp.float32
BF16 = jnp.bfloat16
LANES = 128
HALF = 16
MIB = 1024 * 1024
CHEAP = pl.CostEstimate(flops=1, bytes_accessed=1, transcendentals=0)
COSTLY = pl.CostEstimate(flops=10**11, bytes_accessed=10**8, transcendentals=0)


def params(mib=50):
    return pltpu.CompilerParams(vmem_limit_bytes=mib * MIB, dimension_semantics=("arbitrary",))


def split(x):
    high = x.astype(BF16)
    return high, (x - high.astype(F32)).astype(BF16)


def dot(a, b):
    return jnp.dot(a, b, preferred_element_type=F32)


def dot_t(a, b):
    return lax.dot_general(a, b, (((1,), (1,)), ((), ())), preferred_element_type=F32)


def shifted(x, by):
    return pltpu.roll(x, LANES - by, 1)


def small_kernel(
    nact, per_peer, reward_ref, value_ref, done_ref, old_ref, noise_ref, perm_ref, small_ref, pair_ref, pad_ref, tall_ref
):
    envs, steps = reward_ref.shape
    rows = perm_ref.shape[1]

    def wide(x):
        pad_ref[...] = jnp.zeros_like(pad_ref)
        pad_ref[:, : x.shape[1]] = x
        return pad_ref[...]

    inside = lax.broadcasted_iota(jnp.int32, (envs, LANES), 1) < steps
    value = wide(value_ref[...])
    keep = 1.0 - wide(done_ref[...].astype(F32))
    delta = wide(reward_ref[...]) + GAMMA * shifted(value, 1) * keep - value
    gae = jnp.where(inside, delta, 0.0)
    factor = jnp.where(inside, GAMMA * LAMBDA_GAE * keep, 0.0)
    reach = 1
    while reach < steps:
        gae = gae + factor * shifted(gae, reach)
        factor = factor * shifted(factor, reach)
        reach *= 2
    ret = gae + value
    high, low = split(gae)
    mid, low = split(gae - high.astype(F32))
    lane = lax.broadcasted_iota(jnp.int32, (LANES, rows), 1)
    pick = jnp.where(
        lax.rem(lane, steps) == lax.broadcasted_iota(jnp.int32, (LANES, rows), 0), 1.0, 0.0
    ).astype(BF16)
    lane = lax.broadcasted_iota(jnp.int32, (envs, rows), 1)
    mine = lane // steps == lax.broadcasted_iota(jnp.int32, (envs, rows), 0)

    def flat(x):
        return jnp.sum(jnp.where(mine, dot(x, pick), 0.0), 0, keepdims=True)

    perm = perm_ref[...]
    slot = perm // rows * per_peer + lax.rem(perm, per_peer)
    row = lax.broadcasted_iota(jnp.int32, (HALF, rows), 0)

    def put(block, index, values):
        return jnp.where(row == index, values, block)

    def tall(x):
        tall_ref[...] = jnp.zeros_like(tall_ref)
        tall_ref[:nact, :] = x.astype(F32)
        return tall_ref[...]

    top = tall(old_ref[...])
    for index, values in enumerate((high, mid, low, ret.astype(BF16))):
        top = put(top, nact + index, flat(values))
    bottom = tall(noise_ref[...])
    bottom = put(bottom, nact, (slot // 256).astype(F32))
    bottom = put(bottom, nact + 1, lax.rem(slot, 256).astype(F32))
    small = jnp.concatenate([top, bottom], 0).astype(BF16)
    small_ref[...] = small
    gae = gae_of(small[:HALF], nact)
    lane = lax.broadcasted_iota(jnp.int32, pair_ref.shape, 1)
    pair = jnp.zeros(pair_ref.shape, F32)
    for first, value in ((0, gae), (3, gae * gae)):
        value = jnp.sum(value, 1, keepdims=True)
        for i in range(3):
            rounded = value.astype(BF16).astype(F32)
            pair = jnp.where(lane == first + i, rounded, pair)
            value = value - rounded
    pair_ref[...] = pair.astype(BF16)


def gae_of(small, nact):
    block = small.astype(F32)
    return block[nact : nact + 1] + block[nact + 1 : nact + 2] + block[nact + 2 : nact + 3]


def join_kernel(where_ref, *refs):
    pieces, pair_ref, block_ref = refs[:-2], refs[-2], refs[-1]
    kr = pieces[0].shape[0]
    for r, piece in enumerate(pieces):
        here = pl.ds(pl.multiple_of((where_ref[0] ^ r) * kr, kr), kr)
        block_ref[here, :] = piece[...]
    block_ref[kr * len(pieces) :, :] = pair_ref[...]


def norm_kernel(*refs):
    x_refs, gain_ref, normed_ref, turned_ref = refs[:-3], refs[-3], refs[-2], refs[-1]

    def one(x):
        xf = x.astype(F32)
        rms = lax.rsqrt(jnp.mean(xf * xf, -1, keepdims=True) + NORM_EPS)
        normed = xf * rms * gain_ref[...]
        normed_ref[...] = normed.astype(BF16)
        turned_ref[...] = normed.T.astype(BF16)

    if len(x_refs) == 1:
        one(x_refs[0][...])
    else:
        for i, ref in enumerate(x_refs):
            pl.when(pl.program_id(0) == i)(functools.partial(lambda ref: one(ref[...]), ref))


def norm(xs, gain):
    rows, width = xs[0].shape
    grid = rows // LANES if len(xs) == 1 else len(xs)
    source = (lambda i: (i, 0)) if len(xs) == 1 else (lambda i: (0, 0))
    return pl.pallas_call(
        norm_kernel,
        out_shape=(
            jax.ShapeDtypeStruct((rows * len(xs), width), BF16),
            jax.ShapeDtypeStruct((width, rows * len(xs)), BF16),
        ),
        grid=(grid,),
        in_specs=[pl.BlockSpec((LANES, width), source)] * len(xs)
        + [pl.BlockSpec((1, width), lambda i: (0, 0))],
        out_specs=[
            pl.BlockSpec((LANES, width), lambda i: (i, 0)),
            pl.BlockSpec((width, LANES), lambda i: (0, i)),
        ],
        compiler_params=params(58),
        cost_estimate=CHEAP,
        name="norm",
    )(*xs, gain)


def hidden_kernel(line, nact, packed, given, layout, where_ref, *refs):
    count = 1 if given else 2 * line - 3
    weights, refs = refs[:count], refs[count:]
    n_x = 1 + max(p[0] for pieces in layout for p in pieces)
    n_normed = 1 + max(p[1] for pieces in layout for p in pieces)
    xq_refs, refs = refs[:n_x], refs[n_x:]
    normed_refs, refs = refs[:n_normed], refs[n_normed:]
    row_ref, hw_ref, high_ref, sums_ref, send_ref = refs[:5]
    w_ref = weights[0] if given else refs[5]
    sorted_ref = refs[-1]
    z = where_ref[1]
    members = len(layout)
    rows = high_ref.shape[0] // members
    slab = w_ref.shape[0] // line

    if not given:
        own, fwd, bwd = weights[0], weights[1 : line - 1], weights[line - 1 :]
        w_ref[pl.ds(pl.multiple_of(z * slab, slab), slab), :] = own[:slab, :]
        for j in range(1, line):
            place = pl.multiple_of(lax.rem(z - j + line, line) * slab, slab)
            if j == 1:
                block = fwd[0][:slab, :]
            elif j == line - 1:
                block = bwd[0][:slab, :]
            else:
                block = jnp.where(z >= j, fwd[j - 1][:slab, :], bwd[line - j - 1][:slab, :])
            w_ref[pl.ds(place, slab), :] = block

    for m, pieces in enumerate(layout):
        at = m * rows
        for x, normed, first, size in pieces:
            piece = dot(normed_refs[normed][first : first + size, :], w_ref[...])
            sorted_ref[at : at + size, :] = piece + xq_refs[x][...].astype(F32)
            at += size
        here = slice(m * rows, (m + 1) * rows)
        hidden = sorted_ref[here, :]
        high, low = split(hidden)
        high_ref[here, :] = high
        heads = dot(high, hw_ref[...]) + dot(low, hw_ref[...])
        lane = lax.broadcasted_iota(jnp.int32, heads.shape, 1)
        square = jnp.sum(hidden * hidden, 1, keepdims=True)
        sums = jnp.where(lane == nact + 1, square, heads).T[:HALF]
        if not given:
            pair = jnp.zeros((HALF, LANES), F32)
            for ref in weights:
                pair = pair + ref[slab:, :LANES].astype(F32)
            pair = jnp.concatenate([pair[:1], jnp.zeros((1, rows - LANES), F32)], 1)
            row = lax.broadcasted_iota(jnp.int32, sums.shape, 0)
            sums = jnp.where(row == nact + 2, pair, sums)
        sums_ref[:, here] = sums
        slot = row_ref[HALF + nact : HALF + nact + 1, here].astype(F32) * 256.0
        slot = slot + row_ref[HALF + nact + 1 : HALF + nact + 2, here].astype(F32)
        slot = slot.astype(jnp.int32)
        order = lax.broadcasted_iota(jnp.int32, (rows, rows), 0) == slot
        ranked = dot(jnp.where(order, 1.0, 0.0).astype(BF16), high)
        if packed:
            sorted_ref[here, :] = ranked
        else:
            send_ref[here, :] = ranked.astype(BF16)
    if packed:
        n, size, _ = send_ref.shape
        peer = size // members
        for j in range(n):
            send_ref[j] = jnp.concatenate(
                [sorted_ref[r * rows + j * peer : r * rows + (j + 1) * peer, :] for r in range(members)],
                0,
            ).astype(BF16)


def rest_kernel(line, team, nact, width, total_rows, places, where_ref, *refs):
    sums, refs = refs[:team], refs[team:]
    row_ref, isd_ref, *high_refs = refs[:4]
    hw_ref, *turned_refs = refs[4:10]
    grad_ref = refs[10]
    firsts, (head_ref, ghid_ref) = refs[11:-2], refs[-2:]
    step = pl.program_id(0)
    scale = total_rows**-0.5
    slab, part = grad_ref.shape

    @pl.when(step == 0)
    def _():
        half = team // 2
        rows = high_refs[0].shape[0] // half
        row = lax.broadcasted_iota(jnp.int32, (HALF, rows), 0)
        isd = isd_ref[:, :1]
        pair = sums[0][nact + 2 : nact + 3, :LANES]
        for other in sums[1:]:
            pair = pair + other[nact + 2 : nact + 3, :LANES]
        lane = lax.broadcasted_iota(jnp.int32, (1, LANES), 1)
        mean = jnp.sum(jnp.where(lane < 3, pair, 0.0), 1, keepdims=True) / total_rows
        square = jnp.sum(jnp.where((lane >= 3) & (lane < 6), pair, 0.0), 1, keepdims=True) / total_rows
        spread = lax.rsqrt(square - mean * mean + NORM_EPS)
        std = jnp.zeros((HALF, rows), F32)
        head = jnp.zeros((HALF, part), F32)
        for r in range(team):
            here = slice(r * rows, (r + 1) * rows)
            total = sums[0][:, here]
            for s in range(1, team):
                total = total + sums[s][:, (r ^ s) * rows : ((r ^ s) + 1) * rows]
            rinv = lax.rsqrt(total[nact + 1 : nact + 2] / width + NORM_EPS)
            heads = total * rinv
            top = row_ref[:HALF, here].astype(F32)
            offset = jnp.where(row < nact, top - heads, 0.0)
            sample = row_ref[HALF:, here].astype(F32)
            advant = ((gae_of(row_ref[:HALF, here], nact) - mean) * spread).astype(BF16).astype(F32)
            ret = top[nact + 3 : nact + 4]
            logr = jnp.sum(
                -sample * offset * isd - 0.5 * offset * offset * isd * isd, 0, keepdims=True
            )
            ratio = jnp.exp(logr)
            clipped = jnp.clip(ratio, 1.0 - CLIP_EPS, 1.0 + CLIP_EPS)
            active = ratio * advant <= clipped * advant
            glogr = jnp.where(active, -scale * advant, 0.0) * ratio
            slope = sample * isd + offset * isd * isd
            ghead = jnp.where(
                row < nact, glogr * slope, jnp.where(row == nact, scale * (heads - ret), 0.0)
            )
            std = std + jnp.where(row < nact, glogr * slope * offset, 0.0)
            mean_gh = jnp.sum(ghead * heads, 0, keepdims=True) / width
            scaled = ghead * rinv
            high = high_refs[r // half][(r % half) * rows : (r % half + 1) * rows, :]
            both = dot(jnp.concatenate(split(scaled), 0), high)
            head = head + both[:HALF] + both[HALF:]
            turned = jnp.concatenate(
                [
                    scaled,
                    jnp.broadcast_to(rinv * rinv * mean_gh, (HALF, rows)),
                    jnp.zeros((LANES - 2 * HALF, rows), F32),
                ],
                0,
            ).T
            ghn = dot(jnp.concatenate(split(turned), 1), hw_ref[...])
            ghid = (ghn - high.astype(F32) * turned[:, HALF : HALF + 1]).astype(BF16)
            for first, size, place in places[r]:
                ghid_ref[place : place + size, :] = ghid[first : first + size]
        row = lax.broadcasted_iota(jnp.int32, (HALF, part), 0)
        lane = lax.broadcasted_iota(jnp.int32, (HALF, part), 1)
        std = jnp.where(row == lane, jnp.sum(std, 1, keepdims=True), 0.0)
        std = jnp.sum(std, 0, keepdims=True)
        head = jnp.where(row == nact + 1, std, head)
        head_ref[...] = head
        for ref in firsts:
            ref[slab:, :] = jnp.concatenate(split(head), 0)

    grad = dot(jnp.concatenate([ref[...] for ref in turned_refs], 1), ghid_ref[...])
    grad_ref[...] = grad
    for ref, index in zip(firsts, first_blocks(line)):

        @pl.when(step == index)
        def _(ref=ref):
            ref[:slab, :] = grad.astype(BF16)


def first_blocks(line):
    return sorted({line - 2, 2})


def hop_kernel(head_ref, *refs):
    head = head_ref[...]
    for mine, got, send in zip(refs[:2], refs[2:4], refs[4:]):
        slab = mine.shape[0]
        send[:slab, :] = (mine[...] + got[:slab, :].astype(F32)).astype(BF16)
        send[slab:, :] = jnp.concatenate(split(head + joined(got, slab)), 0)


def joined(ref, slab):
    return ref[slab : slab + HALF, :].astype(F32) + ref[slab + HALF :, :].astype(F32)


def final_kernel(where_ref, mine_ref, head_ref, *refs):
    got, pieces = refs[:2], refs[2:]
    q = where_ref[0]
    slab = mine_ref.shape[0]
    kr = slab // len(pieces)
    head = head_ref[...]
    for ref in got:
        head = head + joined(ref, slab)
    for r, piece in enumerate(pieces):
        here = pl.ds(pl.multiple_of((q ^ r) * kr, kr), kr)
        total = mine_ref[here, :]
        for ref in got:
            total = total + ref[here, :].astype(F32)
        if r == 0:
            piece[:kr, :] = total
            piece[kr:, :] = head
        else:
            piece[:kr, :] = total.astype(BF16)
            piece[kr:, :] = jnp.concatenate(split(head), 0)


def assemble_kernel(where_ref, *refs):
    pieces, (grad_ref, head_ref, std_ref) = refs[:-3], refs[-3:]
    heads_n = head_ref.shape[0]
    q = where_ref[0]
    kr, part = grad_ref.shape[0], pieces[0].shape[1]
    for r, piece in enumerate(pieces):
        here = pl.ds(pl.multiple_of((q ^ r) * part, part), part)
        grad_ref[:, here] = piece[:kr, :].astype(F32)
        head = piece[kr:, :] if r == 0 else joined(piece, kr)
        head_ref[:, here] = head[:heads_n]
        if r == 0:
            std_ref[...] = head[heads_n : heads_n + 1, :LANES]


def plain(shape):
    return pl.BlockSpec(shape, lambda i: (0,) * len(shape))


def whole(shape):
    return pl.BlockSpec(shape, lambda i, w: (0,) * len(shape))


def local(
    obs_feat,
    reward,
    value_old,
    done,
    minibatch_perm,
    old_mean,
    noise,
    gain_in,
    out_weight,
    head_weight,
    log_std,
):
    n = lax.axis_size("fsdp")
    me = lax.axis_index("fsdp")
    team = 4
    line = n // team
    q = me % team
    z = me // team
    rows, width = obs_feat.shape
    part = width // team
    kr = out_weight.shape[0]
    slab = kr * team
    nact = log_std.shape[0]
    heads_n = nact + 1
    per_peer = rows // n
    total_rows = rows * n
    team_rows = team * rows
    where = jnp.stack([q, z]).astype(jnp.int32)

    def mate(x, r):
        return lax.ppermute(x, "fsdp", [(i, i ^ r) for i in range(n)]) if r else x

    def up(x, low, high, wrap=False):
        steps = [(a, a + 1) for a in range(low, high)] + ([(line - 1, 0)] if wrap else [])
        return lax.ppermute(x, "fsdp", [(a * team + i, b * team + i) for a, b in steps for i in range(team)])

    def down(x, low, high, wrap=False):
        steps = [(a, a - 1) for a in range(low, high)] + ([(0, line - 1)] if wrap else [])
        return lax.ppermute(x, "fsdp", [(a * team + i, b * team + i) for a, b in steps for i in range(team)])

    pieces = [
        mate(lax.dynamic_slice(out_weight, (0, (q ^ r) * part), (kr, part)), r) for r in range(team)
    ]
    x_core = mate(obs_feat, 1)
    small, pair = pl.pallas_call(
        functools.partial(small_kernel, nact, per_peer),
        out_shape=(
            jax.ShapeDtypeStruct((2 * HALF, rows), BF16),
            jax.ShapeDtypeStruct((HALF, part), BF16),
        ),
        grid=(1,),
        in_specs=[
            plain(reward.shape),
            plain(value_old.shape),
            plain(done.shape),
            plain((nact, rows)),
            plain((nact, rows)),
            plain((1, rows)),
        ],
        out_specs=[plain((2 * HALF, rows)), plain((HALF, part))],
        scratch_shapes=[pltpu.VMEM((reward.shape[0], LANES), F32), pltpu.VMEM((HALF, rows), F32)],
        compiler_params=params(60),
        cost_estimate=CHEAP,
        name="small",
    )(reward, value_old, done, old_mean.T, noise.T, minibatch_perm[None, :])
    cut = rows - LANES
    obs_first = obs_feat[:cut]
    x_core, small, pair, pieces, where, obs_first, obs_late, head_weight, log_std = (
        lax.optimization_barrier(
            (x_core, small, pair, pieces, where, obs_first, obs_feat, head_weight, log_std)
        )
    )
    obs_last = obs_late[cut:]

    hw = lax.dynamic_slice(head_weight, (q * part, 0), (part, heads_n)).T
    hw_twice = jnp.pad(hw, ((0, LANES - heads_n), (0, 0)))
    hw_wide = hw_twice.T
    hw_twice = jnp.concatenate([hw_twice, hw_twice], 0)
    isd = jnp.pad(jnp.exp(-log_std), (0, HALF - nact))
    isd = jnp.broadcast_to(isd[:, None], (HALF, LANES))

    gain = gain_in[None, :]
    block = pl.pallas_call(
        join_kernel,
        out_shape=jax.ShapeDtypeStruct((slab + HALF, part), BF16),
        grid_spec=pltpu.PrefetchScalarGridSpec(
            num_scalar_prefetch=1,
            grid=(1,),
            in_specs=[whole((kr, part))] * team + [whole((HALF, part))],
            out_specs=whole((slab + HALF, part)),
        ),
        compiler_params=params(),
        cost_estimate=CHEAP,
        name="join",
    )(where, *pieces, pair)

    fs, bs = [up(block, 0, line - 1, True)], [down(block, 1, line, True)]
    far = mate(obs_first, 2)
    small_core = mate(small, 1)
    obs_late, small_core = lax.optimization_barrier((obs_late, small_core))
    normed_own, normed_core = norm([obs_late], gain), norm([x_core], gain)
    (fs, bs, far, small, small_core, normed_own, normed_core, obs_last, hw_wide, hw_twice, isd) = (
        lax.optimization_barrier(
            (fs, bs, far, small, small_core, normed_own, normed_core, obs_last, hw_wide, hw_twice, isd)
        )
    )
    small = jnp.concatenate([small, small_core], 1)
    small_far = mate(small, 2)
    for j in range(2, line - 1):
        fs.append(up(fs[-1], j - 1, line - 1))
        bs.append(down(bs[-1], 1, line - j + 1))
    diag = mate(far, 1)
    late = mate(obs_last, 2)
    normed_far, normed_diag = norm([far], gain), norm([diag], gain)
    fs, bs, late, small, small_far, normed_far, normed_diag = lax.optimization_barrier(
        (fs, bs, late, small, small_far, normed_far, normed_diag)
    )
    weights = [block] + fs + bs

    packed = per_peer % 8 == 0 and team // 2 * per_peer % 16 == 0
    some = team // 2
    some_rows = some * rows

    def hidden(weights, xs, normed, layout, rowdata):
        given = len(weights) == 1
        send_shape = (n, some * per_peer, part) if packed else (some_rows, part)
        out = pl.pallas_call(
            functools.partial(hidden_kernel, line, nact, packed, given, layout),
            out_shape=[
                jax.ShapeDtypeStruct((some_rows, part), BF16),
                jax.ShapeDtypeStruct((HALF, some_rows), F32),
                jax.ShapeDtypeStruct(send_shape, BF16),
            ]
            + ([] if given else [jax.ShapeDtypeStruct((width, part), BF16)]),
            grid_spec=pltpu.PrefetchScalarGridSpec(
                num_scalar_prefetch=1,
                grid=(1,),
                in_specs=[whole(weight.shape) for weight in weights]
                + [pl.BlockSpec((x.shape[0], part), lambda i, w: (0, w[0])) for x in xs]
                + [whole(x.shape) for x in normed]
                + [whole((2 * HALF, some_rows)), whole((part, LANES))],
                out_specs=[whole((some_rows, part)), whole((HALF, some_rows)), whole(send_shape)]
                + ([] if given else [whole((width, part))]),
                scratch_shapes=[pltpu.VMEM((some_rows, part), F32)],
            ),
            compiler_params=params(58),
            cost_estimate=CHEAP,
            name="hidden",
        )(where, *weights, *xs, *normed, rowdata, hw_wide)
        if not packed:
            high, sums, send, *weight = out
            send = send.reshape(some, n, per_peer, part).transpose(1, 0, 2, 3)
            return high, sums, send.reshape(n, some * per_peer, part), *weight
        return out

    def scatter(send):
        return lax.all_to_all(send, "fsdp", split_axis=0, concat_axis=0, tiled=True)

    small_all = jnp.concatenate([small, small_far], 1)
    layout = [[(0, 0, 0, rows)], [(1, 1, 0, rows)]]
    high_near, sums_near, send, weight = hidden(
        weights, [obs_feat, x_core], [normed_own[0], normed_core[0]], layout, small
    )
    recv_near = scatter(send)
    last = mate(late, 1)
    late, last, sums_near, small_all = lax.optimization_barrier((late, last, sums_near, small_all))
    normed_last = norm([late, last], gain)
    layout = [[(0, 0, 0, cut), (2, 2, 0, LANES)], [(1, 1, 0, cut), (3, 2, LANES, LANES)]]
    high_far, sums_far, send, *_ = hidden(
        [weight],
        [far, diag, late, last],
        [normed_far[0], normed_diag[0], normed_last[0]],
        layout,
        small_far,
    )
    sums = jnp.concatenate([sums_near, sums_far], 1)
    sums = [mate(sums, r) for r in range(team)]
    send, recv_near = lax.optimization_barrier((send, recv_near))
    recv_far = scatter(send)
    nfirst = len(first_blocks(line))
    turned = [pair[1] for pair in (normed_own, normed_core, normed_far, normed_diag, normed_last)]
    places = [[(0, rows, 0)], [(0, rows, rows)]] + [
        [(0, cut, 2 * rows + i * cut), (cut, LANES, 2 * rows + 2 * cut + i * LANES)] for i in range(2)
    ]
    outs = pl.pallas_call(
        functools.partial(rest_kernel, line, team, nact, width, total_rows, places),
        out_shape=[jax.ShapeDtypeStruct((width, part), F32)]
        + [jax.ShapeDtypeStruct((slab + 2 * HALF, part), BF16)] * nfirst
        + [jax.ShapeDtypeStruct((HALF, part), F32)],
        grid_spec=pltpu.PrefetchScalarGridSpec(
            num_scalar_prefetch=1,
            grid=(line,),
            in_specs=[whole((HALF, team_rows))] * team
            + [
                whole((2 * HALF, team_rows)),
                whole((HALF, LANES)),
                whole((some_rows, part)),
                whole((some_rows, part)),
                whole((2 * LANES, part)),
            ]
            + [
                pl.BlockSpec((slab, piece.shape[1]), lambda i, w: (lax.rem(w[1] + i, line), 0))
                for piece in turned
            ],
            out_specs=[pl.BlockSpec((slab, part), lambda i, w: (i, 0))]
            + [whole((slab + 2 * HALF, part))] * nfirst
            + [whole((HALF, part))],
            scratch_shapes=[pltpu.VMEM((team_rows, part), BF16)],
        ),
        compiler_params=params(58),
        cost_estimate=COSTLY,
        name="rest",
    )(where, *sums, small_all, isd, high_near, high_far, hw_twice, *turned)
    grads, firsts, head = outs[0], outs[1:-1], outs[-1]

    def hop(up_block, down_block, *got):
        return pl.pallas_call(
            hop_kernel,
            out_shape=[jax.ShapeDtypeStruct((slab + 2 * HALF, part), BF16)] * 2,
            grid=(1,),
            in_specs=[
                plain((HALF, part)),
                pl.BlockSpec((slab, part), lambda i: (up_block, 0)),
                pl.BlockSpec((slab, part), lambda i: (down_block, 0)),
            ]
            + [plain((slab + 2 * HALF, part))] * 2,
            out_specs=[plain((slab + 2 * HALF, part))] * 2,
            compiler_params=params(),
            cost_estimate=CHEAP,
            name="hop",
        )(head, grads, grads, *got)

    send_f, send_b = firsts[-1], firsts[0]
    for k in range(line - 2, 0, -1):
        got_f = up(send_f, 0, line - k, k == 1)
        got_b = down(send_b, k, line, k == 1)
        if k == 2:
            got_f, got_b, recv_far = lax.optimization_barrier((got_f, got_b, recv_far))
        if k > 1:
            send_f, send_b = hop(k - 1, line - k + 1, got_f, got_b)
    pieces = pl.pallas_call(
        final_kernel,
        out_shape=[jax.ShapeDtypeStruct((kr + HALF, part), F32)]
        + [jax.ShapeDtypeStruct((kr + 2 * HALF, part), BF16)] * (team - 1),
        grid_spec=pltpu.PrefetchScalarGridSpec(
            num_scalar_prefetch=1,
            grid=(1,),
            in_specs=[whole((slab, part)), whole((HALF, part))]
            + [whole((slab + 2 * HALF, part))] * 2,
            out_specs=[whole((kr + HALF, part))] + [whole((kr + 2 * HALF, part))] * (team - 1),
        ),
        compiler_params=params(),
        cost_estimate=CHEAP,
        name="final",
    )(where, grads, head, got_f, got_b)
    pieces = [mate(piece, r) for r, piece in enumerate(pieces)]
    grad_weight, heads, std = pl.pallas_call(
        assemble_kernel,
        out_shape=(
            jax.ShapeDtypeStruct((kr, width), F32),
            jax.ShapeDtypeStruct((heads_n, width), F32),
            jax.ShapeDtypeStruct((1, LANES), F32),
        ),
        grid_spec=pltpu.PrefetchScalarGridSpec(
            num_scalar_prefetch=1,
            grid=(1,),
            in_specs=[whole(piece.shape) for piece in pieces],
            out_specs=[whole((kr, width)), whole((heads_n, width)), whole((1, LANES))],
        ),
        compiler_params=params(),
        cost_estimate=CHEAP,
        name="assemble",
    )(where, *pieces)
    grad_head = heads.T
    grad_std = std[0, :nact]

    recv_near = recv_near.reshape(line, team, some, per_peer, part)
    recv_far = recv_far.reshape(line, team, some, per_peer, part)

    def from_member(c, m):
        r = c ^ m
        return recv_near[:, c, r] if r < some else recv_far[:, c, r - some]

    hidden_out = jnp.concatenate(
        [jnp.stack([from_member(c, m) for m in range(team)], 1) for c in range(team)], -1
    ).reshape(rows, width)
    return (hidden_out, grad_weight, grad_head, grad_std)


def solution(mesh):
    return jax.shard_map(
        local,
        mesh=mesh,
        in_specs=(
            P(("groups", "fsdp"), None),
            P(("groups", "fsdp"), None),
            P(("groups", "fsdp"), None),
            P(("groups", "fsdp"), None),
            P(("groups", "fsdp")),
            P(("groups", "fsdp"), None),
            P(("groups", "fsdp"), None),
            P(),
            P("fsdp", None),
            P(),
            P(),
        ),
        out_specs=(
            P(("groups", "fsdp"), None),
            P(("groups", "fsdp"), None),
            P("groups", None),
            P("groups"),
        ),
        check_vma=False,
    )
```

```python
import functools

import jax
import jax.numpy as jnp
from jax import lax
from jax.experimental import pallas as pl
from jax.experimental.pallas import tpu as pltpu
from jax.sharding import PartitionSpec as P

GAMMA = 0.99
LAMBDA_GAE = 0.95
CLIP_EPS = 0.2
NORM_EPS = 1e-05
F32 = jnp.float32
BF16 = jnp.bfloat16
LANES = 128
HALVES = 2
HALF = 16
MIB = 1024 * 1024
CHEAP = pl.CostEstimate(flops=1, bytes_accessed=1, transcendentals=0)
COSTLY = pl.CostEstimate(flops=10**11, bytes_accessed=10**8, transcendentals=0)


def params(mib=50):
    return pltpu.CompilerParams(vmem_limit_bytes=mib * MIB, dimension_semantics=("arbitrary",))


def split(x):
    high = x.astype(BF16)
    return high, (x - high.astype(F32)).astype(BF16)


def dot(a, b):
    return jnp.dot(a, b, preferred_element_type=F32)


def dot_t(a, b):
    return lax.dot_general(a, b, (((1,), (1,)), ((), ())), preferred_element_type=F32)


def shifted(x, by):
    return pltpu.roll(x, LANES - by, 1)


def small_kernel(
    nact, per_peer, reward_ref, value_ref, done_ref, old_ref, noise_ref, perm_ref, small_ref, pair_ref, pad_ref, tall_ref
):
    envs, steps = reward_ref.shape
    rows = perm_ref.shape[1]

    def wide(x):
        pad_ref[...] = jnp.zeros_like(pad_ref)
        pad_ref[:, : x.shape[1]] = x
        return pad_ref[...]

    inside = lax.broadcasted_iota(jnp.int32, (envs, LANES), 1) < steps
    value = wide(value_ref[...])
    keep = 1.0 - wide(done_ref[...].astype(F32))
    delta = wide(reward_ref[...]) + GAMMA * shifted(value, 1) * keep - value
    gae = jnp.where(inside, delta, 0.0)
    factor = jnp.where(inside, GAMMA * LAMBDA_GAE * keep, 0.0)
    reach = 1
    while reach < steps:
        gae = gae + factor * shifted(gae, reach)
        factor = factor * shifted(factor, reach)
        reach *= 2
    ret = gae + value
    high, low = split(gae)
    mid, low = split(gae - high.astype(F32))
    lane = lax.broadcasted_iota(jnp.int32, (LANES, rows), 1)
    pick = jnp.where(
        lax.rem(lane, steps) == lax.broadcasted_iota(jnp.int32, (LANES, rows), 0), 1.0, 0.0
    ).astype(BF16)
    lane = lax.broadcasted_iota(jnp.int32, (envs, rows), 1)
    mine = lane // steps == lax.broadcasted_iota(jnp.int32, (envs, rows), 0)

    def flat(x):
        return jnp.sum(jnp.where(mine, dot(x, pick), 0.0), 0, keepdims=True)

    perm = perm_ref[...]
    slot = perm // rows * per_peer + lax.rem(perm, per_peer)
    row = lax.broadcasted_iota(jnp.int32, (HALF, rows), 0)

    def put(block, index, values):
        return jnp.where(row == index, values, block)

    def tall(x):
        tall_ref[...] = jnp.zeros_like(tall_ref)
        tall_ref[:nact, :] = x.astype(F32)
        return tall_ref[...]

    top = tall(old_ref[...])
    for index, values in enumerate((high, mid, low, ret.astype(BF16))):
        top = put(top, nact + index, flat(values))
    bottom = tall(noise_ref[...])
    bottom = put(bottom, nact, (slot // 256).astype(F32))
    bottom = put(bottom, nact + 1, lax.rem(slot, 256).astype(F32))
    small = jnp.concatenate([top, bottom], 0).astype(BF16)
    small_ref[...] = small
    gae = gae_of(small[:HALF], nact)
    lane = lax.broadcasted_iota(jnp.int32, pair_ref.shape, 1)
    pair = jnp.zeros(pair_ref.shape, F32)
    for first, value in ((0, gae), (3, gae * gae)):
        value = jnp.sum(value, 1, keepdims=True)
        for i in range(3):
            rounded = value.astype(BF16).astype(F32)
            pair = jnp.where(lane == first + i, rounded, pair)
            value = value - rounded
    pair_ref[...] = pair.astype(BF16)


def gae_of(small, nact):
    block = small.astype(F32)
    return block[nact : nact + 1] + block[nact + 1 : nact + 2] + block[nact + 2 : nact + 3]


def join_kernel(where_ref, *refs):
    pieces, pair_ref, block_ref = refs[:-2], refs[-2], refs[-1]
    kr = pieces[0].shape[0]
    for r, piece in enumerate(pieces):
        here = pl.ds(pl.multiple_of((where_ref[0] ^ r) * kr, kr), kr)
        block_ref[here, :] = piece[...]
    block_ref[kr * len(pieces) :, :] = pair_ref[...]


def norm_kernel(*refs):
    x_refs, gain_ref, normed_ref, turned_ref = refs[:-3], refs[-3], refs[-2], refs[-1]

    def one(x):
        xf = x.astype(F32)
        rms = lax.rsqrt(jnp.mean(xf * xf, -1, keepdims=True) + NORM_EPS)
        normed = xf * rms * gain_ref[...]
        normed_ref[...] = normed.astype(BF16)
        turned_ref[...] = normed.T.astype(BF16)

    if len(x_refs) == 1:
        one(x_refs[0][...])
    else:
        for i, ref in enumerate(x_refs):
            pl.when(pl.program_id(0) == i)(functools.partial(lambda ref: one(ref[...]), ref))


def norm(xs, gain):
    rows, width = xs[0].shape
    grid = rows // LANES if len(xs) == 1 else len(xs)
    source = (lambda i: (i, 0)) if len(xs) == 1 else (lambda i: (0, 0))
    return pl.pallas_call(
        norm_kernel,
        out_shape=(
            jax.ShapeDtypeStruct((rows * len(xs), width), BF16),
            jax.ShapeDtypeStruct((width, rows * len(xs)), BF16),
        ),
        grid=(grid,),
        in_specs=[pl.BlockSpec((LANES, width), source)] * len(xs)
        + [pl.BlockSpec((1, width), lambda i: (0, 0))],
        out_specs=[
            pl.BlockSpec((LANES, width), lambda i: (i, 0)),
            pl.BlockSpec((width, LANES), lambda i: (0, i)),
        ],
        compiler_params=params(58),
        cost_estimate=CHEAP,
        name="norm",
    )(*xs, gain)


def early_kernel(line, pieces, where_ref, *refs):
    blocks, refs = refs[:3], refs[3:]
    xq_refs, normed_refs, (sum_ref, pair_ref) = refs[:pieces], refs[pieces:-2], refs[-2:]
    z = where_ref[1]
    slab = blocks[0].shape[0] - HALF
    at = 0
    for xq, normed in zip(xq_refs, normed_refs):
        rows = xq.shape[0]
        total = xq[...].astype(F32)
        for block, step in zip(blocks, (0, line - 1, 1)):
            place = pl.multiple_of(lax.rem(z + step, line) * slab, slab)
            total = total + dot(normed[:, pl.ds(place, slab)], block[:slab, :])
        sum_ref[at : at + rows, :] = total
        at += rows
    pair = jnp.zeros(pair_ref.shape, F32)
    for block in blocks:
        pair = pair + block[slab:, :LANES].astype(F32)
    pair_ref[...] = pair


def hidden_kernel(line, nact, packed, layout, where_ref, *refs):
    late = len(layout[0][0]) == 4
    n_x = 1 + max(index for pieces in layout for index, *_ in pieces)
    js = line - 3
    blocks, refs = refs[: 2 * js], refs[2 * js :]
    if late:
        near, refs = refs[:3], refs[3:]
        w_ref, refs = refs[-1], refs[:-1]
    else:
        early_ref, pair_ref, refs = refs[0], refs[1], refs[2:]
    n_columns = len(refs) - 6
    columns, refs = refs[:n_columns], refs[n_columns:]
    row_ref, hw_ref, high_ref, sums_ref, send_ref, sorted_ref = refs
    z = where_ref[1]
    members = len(layout)
    rows = high_ref.shape[0] // members
    slab = blocks[0].shape[0] - HALF

    def far_block(j):
        return jnp.where(z >= j, blocks[j - 2][:slab, :], blocks[js + line - j - 2][:slab, :])

    if late:
        for j in range(line):
            place = pl.multiple_of(lax.rem(z - j + line, line) * slab, slab)
            nearest = j in (0, 1, line - 1)
            w_ref[pl.ds(place, slab), :] = near[min(j, 2)][:slab, :] if nearest else far_block(j)

    for m, pieces in enumerate(layout):
        at = m * rows
        for index, size, *place in pieces:
            if late:
                normed = columns[n_x + place[0]][place[1] : place[1] + size, :]
                total = columns[index][...].astype(F32) + dot(normed, w_ref[...])
            else:
                total = early_ref[at : at + size, :]
                for j in range(2, line - 1):
                    total = total + dot(columns[index * js + j - 2][...], far_block(j))
            sorted_ref[at : at + size, :] = total
            at += size
        here = slice(m * rows, (m + 1) * rows)
        hidden = sorted_ref[here, :]
        high, low = split(hidden)
        high_ref[here, :] = high
        heads = dot_t(high, hw_ref[...]) + dot_t(low, hw_ref[...])
        lane = lax.broadcasted_iota(jnp.int32, heads.shape, 1)
        square = jnp.sum(hidden * hidden, 1, keepdims=True)
        sums = jnp.where(lane == nact + 1, square, heads).T[:HALF]
        pair = jnp.zeros((HALF, LANES), F32) if late else pair_ref[...]
        for ref in (*near, *blocks) if late else blocks:
            pair = pair + ref[slab:, :LANES].astype(F32)
        pair = jnp.concatenate([pair[:1], jnp.zeros((1, rows - LANES), F32)], 1)
        row = lax.broadcasted_iota(jnp.int32, sums.shape, 0)
        sums_ref[:, here] = jnp.where(row == nact + 2, pair, sums)
        slot = row_ref[HALF + nact : HALF + nact + 1, here].astype(F32) * 256.0
        slot = slot + row_ref[HALF + nact + 1 : HALF + nact + 2, here].astype(F32)
        slot = slot.astype(jnp.int32)
        order = lax.broadcasted_iota(jnp.int32, (rows, rows), 0) == slot
        ranked = dot(jnp.where(order, 1.0, 0.0).astype(BF16), high)
        if packed:
            sorted_ref[here, :] = ranked
        else:
            send_ref[here, :] = ranked.astype(BF16)
    if packed:
        n, size, _ = send_ref.shape
        peer = size // members
        for j in range(n):
            send_ref[j] = jnp.concatenate(
                [sorted_ref[r * rows + j * peer : r * rows + (j + 1) * peer, :] for r in range(members)],
                0,
            ).astype(BF16)


def rest_kernel(line, team, nact, width, total_rows, places, halves, where_ref, *refs):
    sums, refs = refs[:team], refs[team:]
    row_ref, isd_ref, *high_refs = refs[:4]
    hw_ref, *turned_refs = refs[4:10]
    grad_ref = refs[10]
    firsts, (head_ref, ghid_ref) = refs[11:-2], refs[-2:]
    step = pl.program_id(0)
    scale = total_rows**-0.5
    slab, part = grad_ref.shape

    @pl.when(step == 0)
    def _():
        half = team // 2
        rows = high_refs[0].shape[0] // half
        row = lax.broadcasted_iota(jnp.int32, (HALF, rows), 0)
        isd = isd_ref[:, :1]
        pair = sums[0][nact + 2 : nact + 3, :LANES]
        for other in sums[1:]:
            pair = pair + other[nact + 2 : nact + 3, :LANES]
        lane = lax.broadcasted_iota(jnp.int32, (1, LANES), 1)
        mean = jnp.sum(jnp.where(lane < 3, pair, 0.0), 1, keepdims=True) / total_rows
        square = jnp.sum(jnp.where((lane >= 3) & (lane < 6), pair, 0.0), 1, keepdims=True) / total_rows
        spread = lax.rsqrt(square - mean * mean + NORM_EPS)
        std = jnp.zeros((HALF, rows), F32)
        head = jnp.zeros((HALF, part), F32)
        for r in range(team):
            here = slice(r * rows, (r + 1) * rows)
            total = sums[0][:, here]
            for s in range(1, team):
                total = total + sums[s][:, (r ^ s) * rows : ((r ^ s) + 1) * rows]
            rinv = lax.rsqrt(total[nact + 1 : nact + 2] / width + NORM_EPS)
            heads = total * rinv
            top = row_ref[:HALF, here].astype(F32)
            offset = jnp.where(row < nact, top - heads, 0.0)
            sample = row_ref[HALF:, here].astype(F32)
            advant = ((gae_of(row_ref[:HALF, here], nact) - mean) * spread).astype(BF16).astype(F32)
            ret = top[nact + 3 : nact + 4]
            logr = jnp.sum(
                -sample * offset * isd - 0.5 * offset * offset * isd * isd, 0, keepdims=True
            )
            ratio = jnp.exp(logr)
            clipped = jnp.clip(ratio, 1.0 - CLIP_EPS, 1.0 + CLIP_EPS)
            active = ratio * advant <= clipped * advant
            glogr = jnp.where(active, -scale * advant, 0.0) * ratio
            slope = sample * isd + offset * isd * isd
            ghead = jnp.where(
                row < nact, glogr * slope, jnp.where(row == nact, scale * (heads - ret), 0.0)
            )
            std = std + jnp.where(row < nact, glogr * slope * offset, 0.0)
            mean_gh = jnp.sum(ghead * heads, 0, keepdims=True) / width
            scaled = ghead * rinv
            high = high_refs[r // half][(r % half) * rows : (r % half + 1) * rows, :]
            both = dot(jnp.concatenate(split(scaled), 0), high)
            head = head + both[:HALF] + both[HALF:]
            turned = jnp.concatenate(
                [
                    scaled,
                    jnp.broadcast_to(rinv * rinv * mean_gh, (HALF, rows)),
                    jnp.zeros((LANES - 2 * HALF, rows), F32),
                ],
                0,
            ).T
            ghn = dot(jnp.concatenate(split(turned), 1), hw_ref[...])
            ghid = (ghn - high.astype(F32) * turned[:, HALF : HALF + 1]).astype(BF16)
            for first, size, place in places[r]:
                ghid_ref[place : place + size, :] = ghid[first : first + size]
        row = lax.broadcasted_iota(jnp.int32, (HALF, part), 0)
        lane = lax.broadcasted_iota(jnp.int32, (HALF, part), 1)
        std = jnp.where(row == lane, jnp.sum(std, 1, keepdims=True), 0.0)
        std = jnp.sum(std, 0, keepdims=True)
        head = jnp.where(row == nact + 1, std, head)
        head_ref[...] = head
        for i, ref in enumerate(firsts):
            cols = ref.shape[1]
            h = i % halves
            ref[slab:, :] = head[:, h * cols : (h + 1) * cols].astype(BF16)

    grad = dot(jnp.concatenate([ref[...] for ref in turned_refs], 1), ghid_ref[...])
    grad_ref[...] = grad
    for i, index in enumerate(first_blocks(line)):

        @pl.when(step == index)
        def _(i=i):
            for h, ref in enumerate(firsts[i * halves : (i + 1) * halves]):
                cols = ref.shape[1]
                ref[:slab, :] = grad[:, h * cols : (h + 1) * cols].astype(BF16)


def first_blocks(line):
    return sorted({line - 2, 2})


def hop_kernel(head_ref, *refs):
    head = head_ref[...]
    for mine, got, send in zip(refs[:2], refs[2:4], refs[4:]):
        slab = mine.shape[0]
        send[:slab, :] = (mine[...] + got[:slab, :].astype(F32)).astype(BF16)
        send[slab:, :] = (head + got[slab:, :].astype(F32)).astype(BF16)


def final_kernel(where_ref, mine_ref, head_ref, *refs):
    got, pieces = refs[:2], refs[2:]
    q = where_ref[0]
    slab = mine_ref.shape[0]
    kr = slab // len(pieces)
    head = head_ref[...]
    for ref in got:
        head = head + ref[slab:, :].astype(F32)
    for r, piece in enumerate(pieces):
        here = pl.ds(pl.multiple_of((q ^ r) * kr, kr), kr)
        total = mine_ref[here, :]
        for ref in got:
            total = total + ref[here, :].astype(F32)
        piece[:kr, :] = total.astype(piece.dtype)
        piece[kr:, :] = head.astype(piece.dtype)


def assemble_kernel(halves, where_ref, *refs):
    pieces, (grad_ref, head_ref, std_ref) = refs[:-3], refs[-3:]
    heads_n = head_ref.shape[0]
    q = where_ref[0]
    kr, cols = grad_ref.shape[0], pieces[0].shape[1]
    team = len(pieces) // halves
    for i, piece in enumerate(pieces):
        h, r = i // team, i % team
        here = pl.ds(pl.multiple_of(((q ^ r) * halves + h) * cols, cols), cols)
        grad_ref[:, here] = piece[:kr, :].astype(F32)
        head = piece[kr:, :].astype(F32)
        head_ref[:, here] = head[:heads_n]
        if i == 0:
            std_ref[...] = head[heads_n : heads_n + 1, :LANES]


def plain(shape):
    return pl.BlockSpec(shape, lambda i: (0,) * len(shape))


def whole(shape):
    return pl.BlockSpec(shape, lambda i, w: (0,) * len(shape))


def local(
    obs_feat,
    reward,
    value_old,
    done,
    minibatch_perm,
    old_mean,
    noise,
    gain_in,
    out_weight,
    head_weight,
    log_std,
):
    n = lax.axis_size("fsdp")
    me = lax.axis_index("fsdp")
    team = 4
    line = n // team
    q = me % team
    z = me // team
    rows, width = obs_feat.shape
    part = width // team
    kr = out_weight.shape[0]
    slab = kr * team
    nact = log_std.shape[0]
    heads_n = nact + 1
    per_peer = rows // n
    total_rows = rows * n
    team_rows = team * rows
    where = jnp.stack([q, z]).astype(jnp.int32)

    def mate(x, r):
        return lax.ppermute(x, "fsdp", [(i, i ^ r) for i in range(n)]) if r else x

    def up(x, low, high, wrap=False):
        steps = [(a, a + 1) for a in range(low, high)] + ([(line - 1, 0)] if wrap else [])
        return lax.ppermute(x, "fsdp", [(a * team + i, b * team + i) for a, b in steps for i in range(team)])

    def down(x, low, high, wrap=False):
        steps = [(a, a - 1) for a in range(low, high)] + ([(0, line - 1)] if wrap else [])
        return lax.ppermute(x, "fsdp", [(a * team + i, b * team + i) for a, b in steps for i in range(team)])

    pieces = [
        mate(lax.dynamic_slice(out_weight, (0, (q ^ r) * part), (kr, part)), r) for r in range(team)
    ]
    x_core = mate(obs_feat, 1)
    small, pair = pl.pallas_call(
        functools.partial(small_kernel, nact, per_peer),
        out_shape=(
            jax.ShapeDtypeStruct((2 * HALF, rows), BF16),
            jax.ShapeDtypeStruct((HALF, part), BF16),
        ),
        grid=(1,),
        in_specs=[
            plain(reward.shape),
            plain(value_old.shape),
            plain(done.shape),
            plain((nact, rows)),
            plain((nact, rows)),
            plain((1, rows)),
        ],
        out_specs=[plain((2 * HALF, rows)), plain((HALF, part))],
        scratch_shapes=[pltpu.VMEM((reward.shape[0], LANES), F32), pltpu.VMEM((HALF, rows), F32)],
        compiler_params=params(60),
        cost_estimate=CHEAP,
        name="small",
    )(reward, value_old, done, old_mean.T, noise.T, minibatch_perm[None, :])
    cut = rows - LANES
    obs_first = obs_feat[:cut]
    x_core, small, pair, pieces, where, obs_first, obs_late, head_weight, log_std = (
        lax.optimization_barrier(
            (x_core, small, pair, pieces, where, obs_first, obs_feat, head_weight, log_std)
        )
    )
    obs_last = obs_late[cut:]

    hw = lax.dynamic_slice(head_weight, (q * part, 0), (part, heads_n)).T
    hw_twice = jnp.pad(hw, ((0, LANES - heads_n), (0, 0)))
    hw_twice = jnp.concatenate([hw_twice, hw_twice], 0)
    isd = jnp.pad(jnp.exp(-log_std), (0, HALF - nact))
    isd = jnp.broadcast_to(isd[:, None], (HALF, LANES))

    gain = gain_in[None, :]
    block = pl.pallas_call(
        join_kernel,
        out_shape=jax.ShapeDtypeStruct((slab + HALF, part), BF16),
        grid_spec=pltpu.PrefetchScalarGridSpec(
            num_scalar_prefetch=1,
            grid=(1,),
            in_specs=[whole((kr, part))] * team + [whole((HALF, part))],
            out_specs=whole((slab + HALF, part)),
        ),
        compiler_params=params(),
        cost_estimate=CHEAP,
        name="join",
    )(where, *pieces, pair)

    fs, bs = [up(block, 0, line - 1, True)], [down(block, 1, line, True)]
    far = mate(obs_first, 2)
    small_core = mate(small, 1)
    obs_late, small_core = lax.optimization_barrier((obs_late, small_core))
    normed_own, normed_core = norm([obs_late], gain), norm([x_core], gain)
    (fs, bs, far, small, small_core, normed_own, normed_core, obs_last, hw_twice, isd) = (
        lax.optimization_barrier(
            (fs, bs, far, small, small_core, normed_own, normed_core, obs_last, hw_twice, isd)
        )
    )
    small = jnp.concatenate([small, small_core], 1)
    small_far = mate(small, 2)
    for j in range(2, line - 1):
        fs.append(up(fs[-1], j - 1, line - 1))
        bs.append(down(bs[-1], 1, line - j + 1))
    diag = mate(far, 1)
    late = mate(obs_last, 2)
    normed_far = norm([far], gain)
    near_blocks = [block, fs[0], bs[0]]

    def early(xs, normed):
        size = sum(x.shape[0] for x in xs)
        return pl.pallas_call(
            functools.partial(early_kernel, line, len(xs)),
            out_shape=(
                jax.ShapeDtypeStruct((size, part), F32),
                jax.ShapeDtypeStruct((HALF, LANES), F32),
            ),
            grid_spec=pltpu.PrefetchScalarGridSpec(
                num_scalar_prefetch=1,
                grid=(1,),
                in_specs=[whole(block.shape)] * 3
                + [pl.BlockSpec((x.shape[0], part), lambda i, w: (0, w[0])) for x in xs]
                + [whole(x.shape) for x in normed],
                out_specs=[whole((size, part)), whole((HALF, LANES))],
            ),
            compiler_params=params(58),
            cost_estimate=CHEAP,
            name="early",
        )(where, *near_blocks, *xs, *normed)

    in_columns = slab % LANES == 0
    early_near = early([obs_late, x_core], [normed_own[0], normed_core[0]]) if in_columns else ()
    fs, bs, late, small, small_far, normed_far, diag, early_near = lax.optimization_barrier(
        (fs, bs, late, small, small_far, normed_far, diag, early_near)
    )
    far_blocks = fs[1:] + bs[1:]

    packed = per_peer % 8 == 0 and team // 2 * per_peer % 16 == 0
    some = team // 2
    some_rows = some * rows

    def hidden(layout, rowdata, operands, specs, scratch=()):
        send_shape = (n, some * per_peer, part) if packed else (some_rows, part)
        out = pl.pallas_call(
            functools.partial(hidden_kernel, line, nact, packed, layout),
            out_shape=[
                jax.ShapeDtypeStruct((some_rows, part), BF16),
                jax.ShapeDtypeStruct((HALF, some_rows), F32),
                jax.ShapeDtypeStruct(send_shape, BF16),
            ],
            grid_spec=pltpu.PrefetchScalarGridSpec(
                num_scalar_prefetch=1,
                grid=(1,),
                in_specs=[whole(block.shape)] * len(far_blocks)
                + specs
                + [whole((2 * HALF, some_rows)), whole((LANES, part))],
                out_specs=[whole((some_rows, part)), whole((HALF, some_rows)), whole(send_shape)],
                scratch_shapes=[pltpu.VMEM((some_rows, part), F32), *scratch],
            ),
            compiler_params=params(58),
            cost_estimate=CHEAP,
            name="hidden",
        )(where, *far_blocks, *operands, rowdata, hw_twice)
        if not packed:
            high, sums, send = out
            send = send.reshape(some, n, per_peer, part).transpose(1, 0, 2, 3)
            return high, sums, send.reshape(n, some * per_peer, part)
        return out

    def scatter(send):
        return lax.all_to_all(send, "fsdp", split_axis=0, concat_axis=0, tiled=True)

    small_all = jnp.concatenate([small, small_far], 1)
    def at_once(layout, rowdata, xs, normed):
        return hidden(
            layout,
            rowdata,
            [*near_blocks, *xs, *normed],
            [whole(block.shape) for block in near_blocks]
            + [pl.BlockSpec((x.shape[0], part), lambda i, w: (0, w[0])) for x in xs]
            + [whole(x.shape) for x in normed],
            [pltpu.VMEM((width, part), BF16)],
        )

    normed = [normed_own[0], normed_core[0]]
    if in_columns:
        columns = [(x, j) for x in normed for j in range(2, line - 1)]
        high_near, sums_near, send = hidden(
            [[(0, rows)], [(1, rows)]],
            small,
            [*early_near] + [x for x, _ in columns],
            [whole(x.shape) for x in early_near]
            + [
                pl.BlockSpec((rows, slab), lambda i, w, j=j: (0, lax.rem(w[1] - j + line, line)))
                for _, j in columns
            ],
        )
    else:
        layout = [[(0, rows, 0, 0)], [(1, rows, 1, 0)]]
        high_near, sums_near, send = at_once(layout, small, [obs_late, x_core], normed)
    recv_near = scatter(send)
    last = mate(late, 1)
    late, last, diag, sums_near, small_all = lax.optimization_barrier(
        (late, last, diag, sums_near, small_all)
    )
    normed_diag = norm([diag], gain)
    normed_last = norm([late, last], gain)
    high_far, sums_far, send = at_once(
        [[(0, cut, 0, 0), (2, LANES, 2, 0)], [(1, cut, 1, 0), (3, LANES, 2, LANES)]],
        small_far,
        [far, diag, late, last],
        [normed_far[0], normed_diag[0], normed_last[0]],
    )
    sums = jnp.concatenate([sums_near, sums_far], 1)
    sums = [mate(sums, r) for r in range(team)]
    send, recv_near = lax.optimization_barrier((send, recv_near))
    recv_far = scatter(send)
    nfirst = len(first_blocks(line))
    halves = HALVES
    cols = part // halves
    message = (slab + HALF, cols)
    turned = [pair[1] for pair in (normed_own, normed_core, normed_far, normed_diag, normed_last)]
    places = [[(0, rows, 0)], [(0, rows, rows)]] + [
        [(0, cut, 2 * rows + i * cut), (cut, LANES, 2 * rows + 2 * cut + i * LANES)] for i in range(2)
    ]
    outs = pl.pallas_call(
        functools.partial(rest_kernel, line, team, nact, width, total_rows, places, halves),
        out_shape=[jax.ShapeDtypeStruct((width, part), F32)]
        + [jax.ShapeDtypeStruct(message, BF16)] * (nfirst * halves)
        + [jax.ShapeDtypeStruct((HALF, part), F32)],
        grid_spec=pltpu.PrefetchScalarGridSpec(
            num_scalar_prefetch=1,
            grid=(line,),
            in_specs=[whole((HALF, team_rows))] * team
            + [
                whole((2 * HALF, team_rows)),
                whole((HALF, LANES)),
                whole((some_rows, part)),
                whole((some_rows, part)),
                whole((2 * LANES, part)),
            ]
            + [
                pl.BlockSpec((slab, piece.shape[1]), lambda i, w: (lax.rem(w[1] + i, line), 0))
                for piece in turned
            ],
            out_specs=[pl.BlockSpec((slab, part), lambda i, w: (i, 0))]
            + [whole(message)] * (nfirst * halves)
            + [whole((HALF, part))],
            scratch_shapes=[pltpu.VMEM((team_rows, part), BF16)],
        ),
        compiler_params=params(58),
        cost_estimate=COSTLY,
        name="rest",
    )(where, *sums, small_all, isd, high_near, high_far, hw_twice, *turned)
    grads, firsts, head = outs[0], outs[1:-1], outs[-1]

    def hop(h, up_block, down_block, *got):
        return pl.pallas_call(
            hop_kernel,
            out_shape=[jax.ShapeDtypeStruct(message, BF16)] * 2,
            grid=(1,),
            in_specs=[
                pl.BlockSpec((HALF, cols), lambda i: (0, h)),
                pl.BlockSpec((slab, cols), lambda i: (up_block, h)),
                pl.BlockSpec((slab, cols), lambda i: (down_block, h)),
            ]
            + [plain(message)] * 2,
            out_specs=[plain(message)] * 2,
            compiler_params=params(),
            cost_estimate=CHEAP,
            name="hop",
        )(head, grads, grads, *got)

    def final(h, *got):
        return pl.pallas_call(
            final_kernel,
            out_shape=[jax.ShapeDtypeStruct((kr + HALF, cols), F32)]
            + [jax.ShapeDtypeStruct((kr + HALF, cols), BF16)] * (team - 1),
            grid_spec=pltpu.PrefetchScalarGridSpec(
                num_scalar_prefetch=1,
                grid=(1,),
                in_specs=[
                    pl.BlockSpec((slab, cols), lambda i, w: (0, h)),
                    pl.BlockSpec((HALF, cols), lambda i, w: (0, h)),
                ]
                + [whole(message)] * 2,
                out_specs=[whole((kr + HALF, cols))] * team,
            ),
            compiler_params=params(),
            cost_estimate=CHEAP,
            name="final",
        )(where, grads, head, *got)

    got = [(firsts[h - halves], firsts[h]) for h in range(halves)]
    for k in range(line - 2, 0, -1):
        if k < line - 2:
            got = [hop(h, k, line - k, *got[h]) for h in range(halves)]
        got = [(up(f, 0, line - k, k == 1), down(b, k, line, k == 1)) for f, b in got]
        if k == 2:
            got, recv_far = lax.optimization_barrier((got, recv_far)) if halves == 1 else (got, recv_far)
    pieces = []
    for h in range(halves):
        pieces += [mate(piece, r) for r, piece in enumerate(final(h, *got[h]))]
    grad_weight, heads, std = pl.pallas_call(
        functools.partial(assemble_kernel, halves),
        out_shape=(
            jax.ShapeDtypeStruct((kr, width), F32),
            jax.ShapeDtypeStruct((heads_n, width), F32),
            jax.ShapeDtypeStruct((1, LANES), F32),
        ),
        grid_spec=pltpu.PrefetchScalarGridSpec(
            num_scalar_prefetch=1,
            grid=(1,),
            in_specs=[whole(piece.shape) for piece in pieces],
            out_specs=[whole((kr, width)), whole((heads_n, width)), whole((1, LANES))],
        ),
        compiler_params=params(),
        cost_estimate=CHEAP,
        name="assemble",
    )(where, *pieces)
    grad_head = heads.T
    grad_std = std[0, :nact]

    recv_near = recv_near.reshape(line, team, some, per_peer, part)
    recv_far = recv_far.reshape(line, team, some, per_peer, part)

    def from_member(c, m):
        r = c ^ m
        return recv_near[:, c, r] if r < some else recv_far[:, c, r - some]

    hidden_out = jnp.concatenate(
        [jnp.stack([from_member(c, m) for m in range(team)], 1) for c in range(team)], -1
    ).reshape(rows, width)
    return (hidden_out, grad_weight, grad_head, grad_std)


def solution(mesh):
    return jax.shard_map(
        local,
        mesh=mesh,
        in_specs=(
            P(("groups", "fsdp"), None),
            P(("groups", "fsdp"), None),
            P(("groups", "fsdp"), None),
            P(("groups", "fsdp"), None),
            P(("groups", "fsdp")),
            P(("groups", "fsdp"), None),
            P(("groups", "fsdp"), None),
            P(),
            P("fsdp", None),
            P(),
            P(),
        ),
        out_specs=(
            P(("groups", "fsdp"), None),
            P(("groups", "fsdp"), None),
            P("groups", None),
            P("groups"),
        ),
        check_vma=False,
    )
```

```python
import functools

import jax
import jax.numpy as jnp
from jax import lax
from jax.experimental import pallas as pl
from jax.experimental.pallas import tpu as pltpu
from jax.sharding import PartitionSpec as P

GAMMA = 0.99
LAMBDA_GAE = 0.95
CLIP_EPS = 0.2
NORM_EPS = 1e-05
F32 = jnp.float32
BF16 = jnp.bfloat16
LANES = 128
HALVES = 2
SMALL = 8
HALF = 16
MIB = 1024 * 1024
CHEAP = pl.CostEstimate(flops=1, bytes_accessed=1, transcendentals=0)
COSTLY = pl.CostEstimate(flops=10**11, bytes_accessed=10**8, transcendentals=0)


def params(mib=50):
    return pltpu.CompilerParams(vmem_limit_bytes=mib * MIB, dimension_semantics=("arbitrary",))


def split(x):
    high = x.astype(BF16)
    return high, (x - high.astype(F32)).astype(BF16)


def dot(a, b):
    return jnp.dot(a, b, preferred_element_type=F32)


def dot_t(a, b):
    return lax.dot_general(a, b, (((1,), (1,)), ((), ())), preferred_element_type=F32)


def shifted(x, by):
    return pltpu.roll(x, LANES - by, 1)


def small_kernel(
    nact, per_peer, reward_ref, value_ref, done_ref, old_ref, noise_ref, perm_ref, small_ref, pair_ref, pad_ref, tall_ref
):
    envs, steps = reward_ref.shape
    rows = perm_ref.shape[1]

    def wide(x):
        pad_ref[...] = jnp.zeros_like(pad_ref)
        pad_ref[:, : x.shape[1]] = x
        return pad_ref[...]

    inside = lax.broadcasted_iota(jnp.int32, (envs, LANES), 1) < steps
    value = wide(value_ref[...])
    keep = 1.0 - wide(done_ref[...].astype(F32))
    delta = wide(reward_ref[...]) + GAMMA * shifted(value, 1) * keep - value
    gae = jnp.where(inside, delta, 0.0)
    factor = jnp.where(inside, GAMMA * LAMBDA_GAE * keep, 0.0)
    reach = 1
    while reach < steps:
        gae = gae + factor * shifted(gae, reach)
        factor = factor * shifted(factor, reach)
        reach *= 2
    ret = gae + value
    high, low = split(gae)
    mid, low = split(gae - high.astype(F32))
    lane = lax.broadcasted_iota(jnp.int32, (LANES, rows), 1)
    pick = jnp.where(
        lax.rem(lane, steps) == lax.broadcasted_iota(jnp.int32, (LANES, rows), 0), 1.0, 0.0
    ).astype(BF16)
    lane = lax.broadcasted_iota(jnp.int32, (envs, rows), 1)
    mine = lane // steps == lax.broadcasted_iota(jnp.int32, (envs, rows), 0)

    def flat(x):
        return jnp.sum(jnp.where(mine, dot(x, pick), 0.0), 0, keepdims=True)

    perm = perm_ref[...]
    slot = perm // rows * per_peer + lax.rem(perm, per_peer)
    row = lax.broadcasted_iota(jnp.int32, (HALF, rows), 0)

    def put(block, index, values):
        return jnp.where(row == index, values, block)

    def tall(x):
        tall_ref[...] = jnp.zeros_like(tall_ref)
        tall_ref[:nact, :] = x.astype(F32)
        return tall_ref[...]

    top = tall(old_ref[...])
    for index, values in enumerate((high, mid, low, ret.astype(BF16))):
        top = put(top, nact + index, flat(values))
    bottom = tall(noise_ref[...])
    bottom = put(bottom, nact, (slot // 256).astype(F32))
    bottom = put(bottom, nact + 1, lax.rem(slot, 256).astype(F32))
    small = jnp.concatenate([top, bottom], 0).astype(BF16)
    small_ref[...] = small
    gae = gae_of(small[:HALF], nact)
    lane = lax.broadcasted_iota(jnp.int32, pair_ref.shape, 1)
    pair = jnp.zeros(pair_ref.shape, F32)
    for first, value in ((0, gae), (3, gae * gae)):
        value = jnp.sum(value, 1, keepdims=True)
        for i in range(3):
            rounded = value.astype(BF16).astype(F32)
            pair = jnp.where(lane == first + i, rounded, pair)
            value = value - rounded
    pair_ref[...] = pair.astype(BF16)


def gae_of(small, nact):
    block = small.astype(F32)
    return block[nact : nact + 1] + block[nact + 1 : nact + 2] + block[nact + 2 : nact + 3]


def join_kernel(where_ref, *refs):
    pieces, pair_ref, block_ref = refs[:-2], refs[-2], refs[-1]
    kr = pieces[0].shape[0]
    for r, piece in enumerate(pieces):
        here = pl.ds(pl.multiple_of((where_ref[0] ^ r) * kr, kr), kr)
        block_ref[here, :] = piece[...]
    block_ref[kr * len(pieces) :, :] = pair_ref[...]


def norm_kernel(*refs):
    x_refs, gain_ref, normed_ref, turned_ref = refs[:-3], refs[-3], refs[-2], refs[-1]

    def one(x):
        xf = x.astype(F32)
        rms = lax.rsqrt(jnp.mean(xf * xf, -1, keepdims=True) + NORM_EPS)
        normed = xf * rms * gain_ref[...]
        normed_ref[...] = normed.astype(BF16)
        turned_ref[...] = normed.T.astype(BF16)

    if len(x_refs) == 1:
        one(x_refs[0][...])
    else:
        for i, ref in enumerate(x_refs):
            pl.when(pl.program_id(0) == i)(functools.partial(lambda ref: one(ref[...]), ref))


def norm(xs, gain):
    rows, width = xs[0].shape
    grid = rows // LANES if len(xs) == 1 else len(xs)
    source = (lambda i: (i, 0)) if len(xs) == 1 else (lambda i: (0, 0))
    return pl.pallas_call(
        norm_kernel,
        out_shape=(
            jax.ShapeDtypeStruct((rows * len(xs), width), BF16),
            jax.ShapeDtypeStruct((width, rows * len(xs)), BF16),
        ),
        grid=(grid,),
        in_specs=[pl.BlockSpec((LANES, width), source)] * len(xs)
        + [pl.BlockSpec((1, width), lambda i: (0, 0))],
        out_specs=[
            pl.BlockSpec((LANES, width), lambda i: (i, 0)),
            pl.BlockSpec((width, LANES), lambda i: (0, i)),
        ],
        compiler_params=params(58),
        cost_estimate=CHEAP,
        name="norm",
    )(*xs, gain)


def early_kernel(line, pieces, where_ref, *refs):
    blocks, refs = refs[:3], refs[3:]
    xq_refs, normed_refs, (sum_ref, pair_ref) = refs[:pieces], refs[pieces:-2], refs[-2:]
    z = where_ref[1]
    slab = blocks[0].shape[0] - HALF
    at = 0
    for xq, normed in zip(xq_refs, normed_refs):
        rows = xq.shape[0]
        total = xq[...].astype(F32)
        for block, step in zip(blocks, (0, line - 1, 1)):
            place = pl.multiple_of(lax.rem(z + step, line) * slab, slab)
            total = total + dot(normed[:, pl.ds(place, slab)], block[:slab, :])
        sum_ref[at : at + rows, :] = total
        at += rows
    pair = jnp.zeros(pair_ref.shape, F32)
    for block in blocks:
        pair = pair + block[slab:, :LANES].astype(F32)
    pair_ref[...] = pair


def hidden_kernel(line, nact, packed, layout, where_ref, *refs):
    late = len(layout[0][0]) == 4
    n_x = 1 + max(index for pieces in layout for index, *_ in pieces)
    js = line - 3
    blocks, refs = refs[: 2 * js], refs[2 * js :]
    if late:
        near, refs = refs[:3], refs[3:]
        w_ref, refs = refs[-1], refs[:-1]
    else:
        early_ref, pair_ref, refs = refs[0], refs[1], refs[2:]
    n_columns = len(refs) - 5
    columns, refs = refs[:n_columns], refs[n_columns:]
    row_ref, hidden_ref, sums_ref, send_ref, sorted_ref = refs
    z = where_ref[1]
    members = len(layout)
    rows = hidden_ref.shape[0] // members
    slab = blocks[0].shape[0] - HALF

    def far_block(j):
        return jnp.where(z >= j, blocks[j - 2][:slab, :], blocks[js + line - j - 2][:slab, :])

    if late:
        for j in range(line):
            place = pl.multiple_of(lax.rem(z - j + line, line) * slab, slab)
            nearest = j in (0, 1, line - 1)
            w_ref[pl.ds(place, slab), :] = near[min(j, 2)][:slab, :] if nearest else far_block(j)

    for m, pieces in enumerate(layout):
        at = m * rows
        for index, size, *place in pieces:
            if late:
                normed = columns[n_x + place[0]][place[1] : place[1] + size, :]
                total = columns[index][...].astype(F32) + dot(normed, w_ref[...])
            else:
                total = early_ref[at : at + size, :]
                for j in range(2, line - 1):
                    total = total + dot(columns[index * js + j - 2][...], far_block(j))
            sorted_ref[at : at + size, :] = total
            at += size
        here = slice(m * rows, (m + 1) * rows)
        hidden = sorted_ref[here, :]
        hidden_ref[here, :] = hidden
        high = hidden.astype(BF16)
        square = jnp.sum(hidden * hidden, 1, keepdims=True)
        square = jnp.broadcast_to(square, (rows, LANES)).T[:SMALL]
        pair = jnp.zeros((HALF, LANES), F32) if late else pair_ref[...]
        for ref in (*near, *blocks) if late else blocks:
            pair = pair + ref[slab:, :LANES].astype(F32)
        pair = jnp.concatenate([pair[:1], jnp.zeros((1, rows - LANES), F32)], 1)
        row = lax.broadcasted_iota(jnp.int32, square.shape, 0)
        sums_ref[:, here] = jnp.where(row == 1, pair, square)
        slot = row_ref[HALF + nact : HALF + nact + 1, here].astype(F32) * 256.0
        slot = slot + row_ref[HALF + nact + 1 : HALF + nact + 2, here].astype(F32)
        slot = slot.astype(jnp.int32)
        order = lax.broadcasted_iota(jnp.int32, (rows, rows), 0) == slot
        ranked = dot(jnp.where(order, 1.0, 0.0).astype(BF16), high)
        if packed:
            sorted_ref[here, :] = ranked
        else:
            send_ref[here, :] = ranked.astype(BF16)
    if packed:
        n, size, _ = send_ref.shape
        peer = size // members
        for j in range(n):
            send_ref[j] = jnp.concatenate(
                [sorted_ref[r * rows + j * peer : r * rows + (j + 1) * peer, :] for r in range(members)],
                0,
            ).astype(BF16)


def heads_kernel(team, width, *refs):
    squares, (near_ref, far_ref, hw_ref, normed_ref, heads_ref, rinv_ref) = refs[:team], refs[team:]
    step = pl.program_id(0)
    rows = near_ref.shape[0]
    total = jnp.zeros((1, rows), F32)
    for s, ref in enumerate(squares):
        place = pl.multiple_of((step ^ s) * rows, LANES)
        total = total + ref[:1, pl.ds(place, rows)]
    rinv = lax.rsqrt(total / width + NORM_EPS)
    rinv_ref[...] = jnp.broadcast_to(rinv, rinv_ref.shape)
    column = jnp.broadcast_to(rinv, (LANES, rows)).T[:, :1]
    hidden = jnp.where(step < team // 2, near_ref[...], far_ref[...])
    normed = (hidden * column).astype(BF16)
    normed_ref[...] = normed
    heads_ref[...] = dot_t(normed, hw_ref[...]).T[:HALF]


def rest_kernel(line, team, nact, width, total_rows, places, halves, where_ref, *refs):
    sums, pairs, refs = refs[:team], refs[team : 2 * team], refs[2 * team :]
    row_ref, log_std_ref, rinv_ref, high_ref = refs[:4]
    hw_ref, *turned_refs = refs[4:10]
    grad_ref = refs[10]
    firsts, (head_ref, ghid_ref) = refs[11:-2], refs[-2:]
    step = pl.program_id(0)
    scale = total_rows**-0.5
    slab, part = grad_ref.shape

    @pl.when(step == 0)
    def _():
        rows = high_ref.shape[0] // team
        row = lax.broadcasted_iota(jnp.int32, (HALF, rows), 0)
        diagonal = lax.broadcasted_iota(jnp.int32, (HALF, nact), 0) == lax.broadcasted_iota(
            jnp.int32, (HALF, nact), 1
        )
        std_log = jnp.sum(jnp.where(diagonal, log_std_ref[...], 0.0), 1, keepdims=True)
        isd = jnp.where(lax.broadcasted_iota(jnp.int32, (HALF, 1), 0) < nact, jnp.exp(-std_log), 0.0)
        pair = pairs[0][1:2, :]
        for other in pairs[1:]:
            pair = pair + other[1:2, :]
        lane = lax.broadcasted_iota(jnp.int32, (1, LANES), 1)
        mean = jnp.sum(jnp.where(lane < 3, pair, 0.0), 1, keepdims=True) / total_rows
        square = jnp.sum(jnp.where((lane >= 3) & (lane < 6), pair, 0.0), 1, keepdims=True) / total_rows
        spread = lax.rsqrt(square - mean * mean + NORM_EPS)
        std = jnp.zeros((HALF, rows), F32)
        head = jnp.zeros((HALF, part), F32)
        for r in range(team):
            here = slice(r * rows, (r + 1) * rows)
            total = sums[0][:, here]
            for s in range(1, team):
                total = total + sums[s][:, (r ^ s) * rows : ((r ^ s) + 1) * rows]
            heads = total
            rinv = rinv_ref[:1, here]
            top = row_ref[:HALF, here].astype(F32)
            offset = jnp.where(row < nact, top - heads, 0.0)
            sample = row_ref[HALF:, here].astype(F32)
            advant = ((gae_of(row_ref[:HALF, here], nact) - mean) * spread).astype(BF16).astype(F32)
            ret = top[nact + 3 : nact + 4]
            logr = jnp.sum(
                -sample * offset * isd - 0.5 * offset * offset * isd * isd, 0, keepdims=True
            )
            ratio = jnp.exp(logr)
            clipped = jnp.clip(ratio, 1.0 - CLIP_EPS, 1.0 + CLIP_EPS)
            active = ratio * advant <= clipped * advant
            glogr = jnp.where(active, -scale * advant, 0.0) * ratio
            slope = sample * isd + offset * isd * isd
            ghead = jnp.where(
                row < nact, glogr * slope, jnp.where(row == nact, scale * (heads - ret), 0.0)
            )
            std = std + jnp.where(row < nact, glogr * slope * offset, 0.0)
            mean_gh = jnp.sum(ghead * heads, 0, keepdims=True) / width
            scaled = ghead * rinv
            high = high_ref[here, :]
            both = dot(jnp.concatenate(split(ghead), 0), high)
            head = head + both[:HALF] + both[HALF:]
            turned = jnp.concatenate(
                [
                    scaled,
                    jnp.broadcast_to(rinv * mean_gh, (HALF, rows)),
                    jnp.zeros((LANES - 2 * HALF, rows), F32),
                ],
                0,
            ).T
            ghn = dot(jnp.concatenate(split(turned), 1), hw_ref[...])
            ghid = (ghn - high.astype(F32) * turned[:, HALF : HALF + 1]).astype(BF16)
            for first, size, place in places[r]:
                ghid_ref[place : place + size, :] = ghid[first : first + size]
        row = lax.broadcasted_iota(jnp.int32, (HALF, part), 0)
        lane = lax.broadcasted_iota(jnp.int32, (HALF, part), 1)
        std = jnp.where(row == lane, jnp.sum(std, 1, keepdims=True), 0.0)
        std = jnp.sum(std, 0, keepdims=True)
        head = jnp.where(row == nact + 1, std, head)
        head_ref[...] = head
        for i, ref in enumerate(firsts):
            cols = ref.shape[1]
            h = i % halves
            ref[slab:, :] = head[:, h * cols : (h + 1) * cols].astype(BF16)

    grad = dot(jnp.concatenate([ref[...] for ref in turned_refs], 1), ghid_ref[...])
    grad_ref[...] = grad
    for i, index in enumerate(first_blocks(line)):

        @pl.when(step == index)
        def _(i=i):
            for h, ref in enumerate(firsts[i * halves : (i + 1) * halves]):
                cols = ref.shape[1]
                ref[:slab, :] = grad[:, h * cols : (h + 1) * cols].astype(BF16)


def first_blocks(line):
    return sorted({line - 2, 2})


def hop_kernel(head_ref, *refs):
    head = head_ref[...]
    for mine, got, send in zip(refs[:2], refs[2:4], refs[4:]):
        slab = mine.shape[0]
        send[:slab, :] = (mine[...] + got[:slab, :].astype(F32)).astype(BF16)
        send[slab:, :] = (head + got[slab:, :].astype(F32)).astype(BF16)


def final_kernel(where_ref, mine_ref, head_ref, *refs):
    got, pieces = refs[:2], refs[2:]
    q = where_ref[0]
    slab = mine_ref.shape[0]
    kr = slab // len(pieces)
    head = head_ref[...]
    for ref in got:
        head = head + ref[slab:, :].astype(F32)
    for r, piece in enumerate(pieces):
        here = pl.ds(pl.multiple_of((q ^ r) * kr, kr), kr)
        total = mine_ref[here, :]
        for ref in got:
            total = total + ref[here, :].astype(F32)
        piece[:kr, :] = total.astype(piece.dtype)
        piece[kr:, :] = head.astype(piece.dtype)


def assemble_kernel(halves, where_ref, *refs):
    pieces, (grad_ref, head_ref) = refs[:-2], refs[-2:]
    heads_n = head_ref.shape[0]
    q = where_ref[0]
    kr, cols = grad_ref.shape[0], pieces[0].shape[1]
    team = len(pieces) // halves
    for i, piece in enumerate(pieces):
        h, r = i // team, i % team
        here = pl.ds(pl.multiple_of(((q ^ r) * halves + h) * cols, cols), cols)
        grad_ref[:, here] = piece[:kr, :].astype(F32)
        head = piece[kr:, :].astype(F32)
        head_ref[:, here] = head[:heads_n]


def plain(shape):
    return pl.BlockSpec(shape, lambda i: (0,) * len(shape))


def whole(shape):
    return pl.BlockSpec(shape, lambda i, w: (0,) * len(shape))


def local(
    obs_feat,
    reward,
    value_old,
    done,
    minibatch_perm,
    old_mean,
    noise,
    gain_in,
    out_weight,
    head_weight,
    log_std,
):
    n = lax.axis_size("fsdp")
    me = lax.axis_index("fsdp")
    team = 4
    line = n // team
    q = me % team
    z = me // team
    rows, width = obs_feat.shape
    part = width // team
    kr = out_weight.shape[0]
    slab = kr * team
    nact = log_std.shape[0]
    heads_n = nact + 1
    per_peer = rows // n
    total_rows = rows * n
    team_rows = team * rows
    where = jnp.stack([q, z]).astype(jnp.int32)

    def mate(x, r):
        return lax.ppermute(x, "fsdp", [(i, i ^ r) for i in range(n)]) if r else x

    def up(x, low, high, wrap=False):
        steps = [(a, a + 1) for a in range(low, high)] + ([(line - 1, 0)] if wrap else [])
        return lax.ppermute(x, "fsdp", [(a * team + i, b * team + i) for a, b in steps for i in range(team)])

    def down(x, low, high, wrap=False):
        steps = [(a, a - 1) for a in range(low, high)] + ([(0, line - 1)] if wrap else [])
        return lax.ppermute(x, "fsdp", [(a * team + i, b * team + i) for a, b in steps for i in range(team)])

    pieces = [
        mate(lax.dynamic_slice(out_weight, (0, (q ^ r) * part), (kr, part)), r) for r in range(team)
    ]
    x_core = mate(obs_feat, 1)
    small, pair = pl.pallas_call(
        functools.partial(small_kernel, nact, per_peer),
        out_shape=(
            jax.ShapeDtypeStruct((2 * HALF, rows), BF16),
            jax.ShapeDtypeStruct((HALF, part), BF16),
        ),
        grid=(1,),
        in_specs=[
            plain(reward.shape),
            plain(value_old.shape),
            plain(done.shape),
            plain((nact, rows)),
            plain((nact, rows)),
            plain((1, rows)),
        ],
        out_specs=[plain((2 * HALF, rows)), plain((HALF, part))],
        scratch_shapes=[pltpu.VMEM((reward.shape[0], LANES), F32), pltpu.VMEM((HALF, rows), F32)],
        compiler_params=params(60),
        cost_estimate=CHEAP,
        name="small",
    )(reward, value_old, done, old_mean.T, noise.T, minibatch_perm[None, :])
    cut = rows - LANES
    obs_first = obs_feat[:cut]
    x_core, small, pair, pieces, where, obs_first, obs_late, head_weight, log_std = (
        lax.optimization_barrier(
            (x_core, small, pair, pieces, where, obs_first, obs_feat, head_weight, log_std)
        )
    )
    obs_last = obs_late[cut:]

    hw = lax.dynamic_slice(head_weight, (q * part, 0), (part, heads_n)).T
    hw_twice = jnp.pad(hw, ((0, LANES - heads_n), (0, 0)))
    hw_twice = jnp.concatenate([hw_twice, hw_twice], 0)

    gain = gain_in[None, :]
    block = pl.pallas_call(
        join_kernel,
        out_shape=jax.ShapeDtypeStruct((slab + HALF, part), BF16),
        grid_spec=pltpu.PrefetchScalarGridSpec(
            num_scalar_prefetch=1,
            grid=(1,),
            in_specs=[whole((kr, part))] * team + [whole((HALF, part))],
            out_specs=whole((slab + HALF, part)),
        ),
        compiler_params=params(),
        cost_estimate=CHEAP,
        name="join",
    )(where, *pieces, pair)

    fs, bs = [up(block, 0, line - 1, True)], [down(block, 1, line, True)]
    far = mate(obs_first, 2)
    small_core = mate(small, 1)
    obs_late, small_core = lax.optimization_barrier((obs_late, small_core))
    normed_own, normed_core = norm([obs_late], gain), norm([x_core], gain)
    small = jnp.concatenate([small, small_core], 1)
    small_far = mate(small, 2)
    (fs, bs, far, small, small_far, normed_own, normed_core, obs_last, hw_twice) = (
        lax.optimization_barrier(
            (fs, bs, far, small, small_far, normed_own, normed_core, obs_last, hw_twice)
        )
    )
    for j in range(2, line - 1):
        fs.append(up(fs[-1], j - 1, line - 1))
        bs.append(down(bs[-1], 1, line - j + 1))
    diag = mate(far, 1)
    late = mate(obs_last, 2)
    normed_far, normed_diag = norm([far], gain), norm([diag], gain)
    near_blocks = [block, fs[0], bs[0]]

    def early(xs, normed):
        size = sum(x.shape[0] for x in xs)
        return pl.pallas_call(
            functools.partial(early_kernel, line, len(xs)),
            out_shape=(
                jax.ShapeDtypeStruct((size, part), F32),
                jax.ShapeDtypeStruct((HALF, LANES), F32),
            ),
            grid_spec=pltpu.PrefetchScalarGridSpec(
                num_scalar_prefetch=1,
                grid=(1,),
                in_specs=[whole(block.shape)] * 3
                + [pl.BlockSpec((x.shape[0], part), lambda i, w: (0, w[0])) for x in xs]
                + [whole(x.shape) for x in normed],
                out_specs=[whole((size, part)), whole((HALF, LANES))],
            ),
            compiler_params=params(58),
            cost_estimate=CHEAP,
            name="early",
        )(where, *near_blocks, *xs, *normed)

    in_columns = slab % LANES == 0
    early_near = early([obs_late, x_core], [normed_own[0], normed_core[0]]) if in_columns else ()
    fs, bs, late, small, small_far, normed_far, normed_diag, early_near = lax.optimization_barrier(
        (fs, bs, late, small, small_far, normed_far, normed_diag, early_near)
    )
    far_blocks = fs[1:] + bs[1:]

    packed = per_peer % 8 == 0 and team // 2 * per_peer % 16 == 0
    some = team // 2
    some_rows = some * rows

    def hidden(layout, rowdata, operands, specs, scratch=()):
        send_shape = (n, some * per_peer, part) if packed else (some_rows, part)
        out = pl.pallas_call(
            functools.partial(hidden_kernel, line, nact, packed, layout),
            out_shape=[
                jax.ShapeDtypeStruct((some_rows, part), F32),
                jax.ShapeDtypeStruct((SMALL, some_rows), F32),
                jax.ShapeDtypeStruct(send_shape, BF16),
            ],
            grid_spec=pltpu.PrefetchScalarGridSpec(
                num_scalar_prefetch=1,
                grid=(1,),
                in_specs=[whole(block.shape)] * len(far_blocks)
                + specs
                + [whole((2 * HALF, some_rows))],
                out_specs=[whole((some_rows, part)), whole((SMALL, some_rows)), whole(send_shape)],
                scratch_shapes=[pltpu.VMEM((some_rows, part), F32), *scratch],
            ),
            compiler_params=params(58),
            cost_estimate=CHEAP,
            name="hidden",
        )(where, *far_blocks, *operands, rowdata)
        if not packed:
            high, sums, send = out
            send = send.reshape(some, n, per_peer, part).transpose(1, 0, 2, 3)
            return high, sums, send.reshape(n, some * per_peer, part)
        return out

    def scatter(send):
        return lax.all_to_all(send, "fsdp", split_axis=0, concat_axis=0, tiled=True)

    small_all = jnp.concatenate([small, small_far], 1)
    def at_once(layout, rowdata, xs, normed):
        return hidden(
            layout,
            rowdata,
            [*near_blocks, *xs, *normed],
            [whole(block.shape) for block in near_blocks]
            + [pl.BlockSpec((x.shape[0], part), lambda i, w: (0, w[0])) for x in xs]
            + [whole(x.shape) for x in normed],
            [pltpu.VMEM((width, part), BF16)],
        )

    normed = [normed_own[0], normed_core[0]]
    if in_columns:
        columns = [(x, j) for x in normed for j in range(2, line - 1)]
        hidden_near, sums_near, send = hidden(
            [[(0, rows)], [(1, rows)]],
            small,
            [*early_near] + [x for x, _ in columns],
            [whole(x.shape) for x in early_near]
            + [
                pl.BlockSpec((rows, slab), lambda i, w, j=j: (0, lax.rem(w[1] - j + line, line)))
                for _, j in columns
            ],
        )
    else:
        layout = [[(0, rows, 0, 0)], [(1, rows, 1, 0)]]
        hidden_near, sums_near, send = at_once(layout, small, [obs_late, x_core], normed)
    recv_near = scatter(send)
    last = mate(late, 1)
    late, last, sums_near, small_all = lax.optimization_barrier((late, last, sums_near, small_all))
    normed_last = norm([late, last], gain)
    hidden_far, sums_far, send = at_once(
        [[(0, cut, 0, 0), (2, LANES, 2, 0)], [(1, cut, 1, 0), (3, LANES, 2, LANES)]],
        small_far,
        [far, diag, late, last],
        [normed_far[0], normed_diag[0], normed_last[0]],
    )
    sums = jnp.concatenate([sums_near, sums_far], 1)
    squares = [mate(sums, r) for r in range(team)]
    normed_hidden, heads, rinv = pl.pallas_call(
        functools.partial(heads_kernel, team, width),
        out_shape=(
            jax.ShapeDtypeStruct((team_rows, part), BF16),
            jax.ShapeDtypeStruct((HALF, team_rows), F32),
            jax.ShapeDtypeStruct((SMALL, team_rows), F32),
        ),
        grid=(team,),
        in_specs=[plain((SMALL, team_rows))] * team
        + [
            pl.BlockSpec((rows, part), lambda i: (jnp.minimum(i, some - 1), 0)),
            pl.BlockSpec((rows, part), lambda i: (jnp.maximum(i - some, 0), 0)),
            plain((LANES, part)),
        ],
        out_specs=[
            pl.BlockSpec((rows, part), lambda i: (i, 0)),
            pl.BlockSpec((HALF, rows), lambda i: (0, i)),
            pl.BlockSpec((SMALL, rows), lambda i: (0, i)),
        ],
        compiler_params=params(58),
        cost_estimate=CHEAP,
        name="heads",
    )(*squares, hidden_near, hidden_far, hw_twice)
    sums = [mate(heads, r) for r in range(team)]
    send, recv_near = lax.optimization_barrier((send, recv_near))
    recv_far = scatter(send)
    nfirst = len(first_blocks(line))
    halves = HALVES
    cols = part // halves
    message = (slab + HALF, cols)
    turned = [pair[1] for pair in (normed_own, normed_core, normed_far, normed_diag, normed_last)]
    places = [[(0, rows, 0)], [(0, rows, rows)]] + [
        [(0, cut, 2 * rows + i * cut), (cut, LANES, 2 * rows + 2 * cut + i * LANES)] for i in range(2)
    ]
    outs = pl.pallas_call(
        functools.partial(rest_kernel, line, team, nact, width, total_rows, places, halves),
        out_shape=[jax.ShapeDtypeStruct((width, part), F32)]
        + [jax.ShapeDtypeStruct(message, BF16)] * (nfirst * halves)
        + [jax.ShapeDtypeStruct((HALF, part), F32)],
        grid_spec=pltpu.PrefetchScalarGridSpec(
            num_scalar_prefetch=1,
            grid=(line,),
            in_specs=[whole((HALF, team_rows))] * team
            + [pl.BlockSpec((SMALL, LANES), lambda i, w: (0, 0))] * team
            + [
                whole((2 * HALF, team_rows)),
                whole((1, nact)),
                whole((SMALL, team_rows)),
                whole((team_rows, part)),
                whole((2 * LANES, part)),
            ]
            + [
                pl.BlockSpec((slab, piece.shape[1]), lambda i, w: (lax.rem(w[1] + i, line), 0))
                for piece in turned
            ],
            out_specs=[pl.BlockSpec((slab, part), lambda i, w: (i, 0))]
            + [whole(message)] * (nfirst * halves)
            + [whole((HALF, part))],
            scratch_shapes=[pltpu.VMEM((team_rows, part), BF16)],
        ),
        compiler_params=params(58),
        cost_estimate=COSTLY,
        name="rest",
    )(where, *sums, *squares, small_all, log_std[None, :], rinv, normed_hidden, hw_twice, *turned)
    grads, firsts, head = outs[0], outs[1:-1], outs[-1]

    def hop(h, up_block, down_block, *got):
        return pl.pallas_call(
            hop_kernel,
            out_shape=[jax.ShapeDtypeStruct(message, BF16)] * 2,
            grid=(1,),
            in_specs=[
                pl.BlockSpec((HALF, cols), lambda i: (0, h)),
                pl.BlockSpec((slab, cols), lambda i: (up_block, h)),
                pl.BlockSpec((slab, cols), lambda i: (down_block, h)),
            ]
            + [plain(message)] * 2,
            out_specs=[plain(message)] * 2,
            compiler_params=params(),
            cost_estimate=CHEAP,
            name="hop",
        )(head, grads, grads, *got)

    def final(h, *got):
        return pl.pallas_call(
            final_kernel,
            out_shape=[jax.ShapeDtypeStruct((kr + HALF, cols), F32)]
            + [jax.ShapeDtypeStruct((kr + HALF, cols), BF16)] * (team - 1),
            grid_spec=pltpu.PrefetchScalarGridSpec(
                num_scalar_prefetch=1,
                grid=(1,),
                in_specs=[
                    pl.BlockSpec((slab, cols), lambda i, w: (0, h)),
                    pl.BlockSpec((HALF, cols), lambda i, w: (0, h)),
                ]
                + [whole(message)] * 2,
                out_specs=[whole((kr + HALF, cols))] * team,
            ),
            compiler_params=params(),
            cost_estimate=CHEAP,
            name="final",
        )(where, grads, head, *got)

    recv_near = recv_near.reshape(line, team, some, per_peer, part)
    recv_far = recv_far.reshape(line, team, some, per_peer, part)

    def from_member(c, m):
        r = c ^ m
        return recv_near[:, c, r] if r < some else recv_far[:, c, r - some]

    hidden_out = jnp.concatenate(
        [jnp.stack([from_member(c, m) for m in range(team)], 1) for c in range(team)], -1
    ).reshape(rows, width)
    got = [(firsts[h - halves], firsts[h]) for h in range(halves)]
    for k in range(line - 2, 0, -1):
        if k < line - 2:
            got = [hop(h, k, line - k, *got[h]) for h in range(halves)]
        got = [(up(f, 0, line - k, k == 1), down(b, k, line, k == 1)) for f, b in got]
        if k == 2:
            got[0], hidden_out = lax.optimization_barrier((got[0], hidden_out))
    pieces = []
    for h in range(halves):
        pieces += [mate(piece, r) for r, piece in enumerate(final(h, *got[h]))]
    grad_weight, heads = pl.pallas_call(
        functools.partial(assemble_kernel, halves),
        out_shape=(
            jax.ShapeDtypeStruct((kr, width), F32),
            jax.ShapeDtypeStruct((heads_n, width), F32),
        ),
        grid_spec=pltpu.PrefetchScalarGridSpec(
            num_scalar_prefetch=1,
            grid=(1,),
            in_specs=[whole(piece.shape) for piece in pieces],
            out_specs=[whole((kr, width)), whole((heads_n, width))],
        ),
        compiler_params=params(),
        cost_estimate=CHEAP,
        name="assemble",
    )(where, *pieces)
    grad_head = heads.T
    grad_std = pieces[0][kr + heads_n, :nact]

    return (hidden_out, grad_weight, grad_head, grad_std)


def solution(mesh):
    return jax.shard_map(
        local,
        mesh=mesh,
        in_specs=(
            P(("groups", "fsdp"), None),
            P(("groups", "fsdp"), None),
            P(("groups", "fsdp"), None),
            P(("groups", "fsdp"), None),
            P(("groups", "fsdp")),
            P(("groups", "fsdp"), None),
            P(("groups", "fsdp"), None),
            P(),
            P("fsdp", None),
            P(),
            P(),
        ),
        out_specs=(
            P(("groups", "fsdp"), None),
            P(("groups", "fsdp"), None),
            P("groups", None),
            P("groups"),
        ),
        check_vma=False,
    )
```

```python
import functools

import jax
import jax.numpy as jnp
from jax import lax
from jax.experimental import pallas as pl
from jax.experimental.pallas import tpu as pltpu
from jax.sharding import PartitionSpec as P

GAMMA = 0.99
LAMBDA_GAE = 0.95
CLIP_EPS = 0.2
NORM_EPS = 1e-05
F32 = jnp.float32
BF16 = jnp.bfloat16
LANES = 128
HALVES = 2
SMALL = 8
HALF = 16
MIB = 1024 * 1024
CHEAP = pl.CostEstimate(flops=1, bytes_accessed=1, transcendentals=0)
COSTLY = pl.CostEstimate(flops=10**11, bytes_accessed=10**8, transcendentals=0)


def params(mib=50):
    return pltpu.CompilerParams(vmem_limit_bytes=mib * MIB, dimension_semantics=("arbitrary",))


def split(x):
    high = x.astype(BF16)
    return high, (x - high.astype(F32)).astype(BF16)


def dot(a, b):
    return jnp.dot(a, b, preferred_element_type=F32)


def dot_t(a, b):
    return lax.dot_general(a, b, (((1,), (1,)), ((), ())), preferred_element_type=F32)


def shifted(x, by):
    return pltpu.roll(x, LANES - by, 1)


def small_kernel(
    nact, per_peer, reward_ref, value_ref, done_ref, old_ref, noise_ref, perm_ref, small_ref, pair_ref, pad_ref, tall_ref
):
    envs, steps = reward_ref.shape
    rows = perm_ref.shape[1]

    def wide(x):
        pad_ref[...] = jnp.zeros_like(pad_ref)
        pad_ref[:, : x.shape[1]] = x
        return pad_ref[...]

    inside = lax.broadcasted_iota(jnp.int32, (envs, LANES), 1) < steps
    value = wide(value_ref[...])
    keep = 1.0 - wide(done_ref[...].astype(F32))
    delta = wide(reward_ref[...]) + GAMMA * shifted(value, 1) * keep - value
    gae = jnp.where(inside, delta, 0.0)
    factor = jnp.where(inside, GAMMA * LAMBDA_GAE * keep, 0.0)
    reach = 1
    while reach < steps:
        gae = gae + factor * shifted(gae, reach)
        factor = factor * shifted(factor, reach)
        reach *= 2
    ret = gae + value
    high, low = split(gae)
    mid, low = split(gae - high.astype(F32))
    lane = lax.broadcasted_iota(jnp.int32, (LANES, rows), 1)
    pick = jnp.where(
        lax.rem(lane, steps) == lax.broadcasted_iota(jnp.int32, (LANES, rows), 0), 1.0, 0.0
    ).astype(BF16)
    lane = lax.broadcasted_iota(jnp.int32, (envs, rows), 1)
    mine = lane // steps == lax.broadcasted_iota(jnp.int32, (envs, rows), 0)

    def flat(x):
        return jnp.sum(jnp.where(mine, dot(x, pick), 0.0), 0, keepdims=True)

    perm = perm_ref[...]
    slot = perm // rows * per_peer + lax.rem(perm, per_peer)
    row = lax.broadcasted_iota(jnp.int32, (HALF, rows), 0)

    def put(block, index, values):
        return jnp.where(row == index, values, block)

    def tall(x):
        tall_ref[...] = jnp.zeros_like(tall_ref)
        tall_ref[:nact, :] = x.astype(F32)
        return tall_ref[...]

    top = tall(old_ref[...])
    for index, values in enumerate((high, mid, low, ret.astype(BF16))):
        top = put(top, nact + index, flat(values))
    bottom = tall(noise_ref[...])
    bottom = put(bottom, nact, (slot // 256).astype(F32))
    bottom = put(bottom, nact + 1, lax.rem(slot, 256).astype(F32))
    small = jnp.concatenate([top, bottom], 0).astype(BF16)
    small_ref[...] = small
    gae = gae_of(small[:HALF], nact)
    lane = lax.broadcasted_iota(jnp.int32, pair_ref.shape, 1)
    pair = jnp.zeros(pair_ref.shape, F32)
    for first, value in ((0, gae), (3, gae * gae)):
        value = jnp.sum(value, 1, keepdims=True)
        for i in range(3):
            rounded = value.astype(BF16).astype(F32)
            pair = jnp.where(lane == first + i, rounded, pair)
            value = value - rounded
    pair_ref[...] = pair.astype(BF16)


def gae_of(small, nact):
    block = small.astype(F32)
    return block[nact : nact + 1] + block[nact + 1 : nact + 2] + block[nact + 2 : nact + 3]


def join_kernel(where_ref, *refs):
    pieces, pair_ref, block_ref = refs[:-2], refs[-2], refs[-1]
    kr = pieces[0].shape[0]
    for r, piece in enumerate(pieces):
        here = pl.ds(pl.multiple_of((where_ref[0] ^ r) * kr, kr), kr)
        block_ref[here, :] = piece[...]
    block_ref[kr * len(pieces) :, :] = pair_ref[...]


def norm_kernel(*refs):
    x_refs, gain_ref, normed_ref, turned_ref = refs[:-3], refs[-3], refs[-2], refs[-1]

    def one(x):
        xf = x.astype(F32)
        rms = lax.rsqrt(jnp.mean(xf * xf, -1, keepdims=True) + NORM_EPS)
        normed = xf * rms * gain_ref[...]
        normed_ref[...] = normed.astype(BF16)
        turned_ref[...] = normed.T.astype(BF16)

    if len(x_refs) == 1:
        one(x_refs[0][...])
    else:
        for i, ref in enumerate(x_refs):
            pl.when(pl.program_id(0) == i)(functools.partial(lambda ref: one(ref[...]), ref))


def norm(xs, gain):
    rows, width = xs[0].shape
    grid = rows // LANES if len(xs) == 1 else len(xs)
    source = (lambda i: (i, 0)) if len(xs) == 1 else (lambda i: (0, 0))
    return pl.pallas_call(
        norm_kernel,
        out_shape=(
            jax.ShapeDtypeStruct((rows * len(xs), width), BF16),
            jax.ShapeDtypeStruct((width, rows * len(xs)), BF16),
        ),
        grid=(grid,),
        in_specs=[pl.BlockSpec((LANES, width), source)] * len(xs)
        + [pl.BlockSpec((1, width), lambda i: (0, 0))],
        out_specs=[
            pl.BlockSpec((LANES, width), lambda i: (i, 0)),
            pl.BlockSpec((width, LANES), lambda i: (0, i)),
        ],
        compiler_params=params(58),
        cost_estimate=CHEAP,
        name="norm",
    )(*xs, gain)


def early_kernel(line, pieces, where_ref, *refs):
    blocks, refs = refs[:3], refs[3:]
    xq_refs, normed_refs, (sum_ref, pair_ref) = refs[:pieces], refs[pieces:-2], refs[-2:]
    z = where_ref[1]
    slab = blocks[0].shape[0] - HALF
    at = 0
    for xq, normed in zip(xq_refs, normed_refs):
        rows = xq.shape[0]
        total = xq[...].astype(F32)
        for block, step in zip(blocks, (0, line - 1, 1)):
            place = pl.multiple_of(lax.rem(z + step, line) * slab, slab)
            total = total + dot(normed[:, pl.ds(place, slab)], block[:slab, :])
        sum_ref[at : at + rows, :] = total
        at += rows
    pair = jnp.zeros(pair_ref.shape, F32)
    for block in blocks:
        pair = pair + block[slab:, :LANES].astype(F32)
    pair_ref[...] = pair


def hidden_kernel(line, nact, packed, layout, raw, joined, where_ref, *refs):
    late = len(layout[0][0]) == 4
    n_x = 1 + max(index for pieces in layout for index, *_ in pieces)
    js = line - 3
    blocks, refs = refs[: 2 * js], refs[2 * js :]
    if late:
        near, refs = refs[:3], refs[3:]
        w_ref, refs = refs[-1], refs[:-1]
        gain_ref = refs[-7 if joined else -6]
    else:
        early_ref, pair_ref, refs = refs[0], refs[1], refs[2:]
    n_columns = len(refs) - 5
    columns, refs = refs[:n_columns], refs[n_columns:]
    row_ref, hidden_ref, sums_ref, send_ref, sorted_ref = refs
    z = where_ref[1]
    members = len(layout)
    rows = hidden_ref.shape[0] // members
    slab = blocks[0].shape[0] - HALF

    def far_block(j):
        return jnp.where(z >= j, blocks[j - 2][:slab, :], blocks[js + line - j - 2][:slab, :])

    if late:
        for j in range(line):
            place = pl.multiple_of(lax.rem(z - j + line, line) * slab, slab)
            nearest = j in (0, 1, line - 1)
            w_ref[pl.ds(place, slab), :] = near[min(j, 2)][:slab, :] if nearest else far_block(j)

    ahead = columns[-1].shape[1] if joined else 0
    if joined:
        sums_ref[:, :ahead] = columns[-1][...]
    for m, pieces in enumerate(layout):
        at = m * rows
        for index, size, *place in pieces:
            if late:
                normed = columns[n_x + place[0]][place[1] : place[1] + size, :]
                if place[0] in raw:
                    xf = normed.astype(F32)
                    rms = lax.rsqrt(jnp.mean(xf * xf, -1, keepdims=True) + NORM_EPS)
                    normed = (xf * rms * gain_ref[...]).astype(BF16)
                total = columns[index][...].astype(F32) + dot(normed, w_ref[...])
            else:
                total = early_ref[at : at + size, :]
                for j in range(2, line - 1):
                    total = total + dot(columns[index * js + j - 2][...], far_block(j))
            sorted_ref[at : at + size, :] = total
            at += size
        here = slice(m * rows, (m + 1) * rows)
        hidden = sorted_ref[here, :]
        hidden_ref[here, :] = hidden
        high = hidden.astype(BF16)
        square = jnp.sum(hidden * hidden, 1, keepdims=True)
        square = jnp.broadcast_to(square, (rows, LANES)).T[:SMALL]
        pair = jnp.zeros((HALF, LANES), F32) if late else pair_ref[...]
        for ref in (*near, *blocks) if late else blocks:
            pair = pair + ref[slab:, :LANES].astype(F32)
        pair = jnp.concatenate([pair[:1], jnp.zeros((1, rows - LANES), F32)], 1)
        row = lax.broadcasted_iota(jnp.int32, square.shape, 0)
        sums_ref[:, ahead + m * rows : ahead + (m + 1) * rows] = jnp.where(row == 1, pair, square)
        slot = row_ref[HALF + nact : HALF + nact + 1, here].astype(F32) * 256.0
        slot = slot + row_ref[HALF + nact + 1 : HALF + nact + 2, here].astype(F32)
        slot = slot.astype(jnp.int32)
        order = lax.broadcasted_iota(jnp.int32, (rows, rows), 0) == slot
        ranked = dot(jnp.where(order, 1.0, 0.0).astype(BF16), high)
        if packed:
            sorted_ref[here, :] = ranked
        else:
            send_ref[here, :] = ranked.astype(BF16)
    if packed:
        n, size, _ = send_ref.shape
        peer = size // members
        for j in range(n):
            send_ref[j] = jnp.concatenate(
                [sorted_ref[r * rows + j * peer : r * rows + (j + 1) * peer, :] for r in range(members)],
                0,
            ).astype(BF16)


def heads_kernel(team, width, *refs):
    squares, (near_ref, far_ref, hw_ref, normed_ref, heads_ref, rinv_ref) = refs[:team], refs[team:]
    step = pl.program_id(0)
    rows = near_ref.shape[0]
    total = jnp.zeros((1, rows), F32)
    for s, ref in enumerate(squares):
        place = pl.multiple_of((step ^ s) * rows, LANES)
        total = total + ref[:1, pl.ds(place, rows)]
    rinv = lax.rsqrt(total / width + NORM_EPS)
    rinv_ref[...] = jnp.broadcast_to(rinv, rinv_ref.shape)
    column = jnp.broadcast_to(rinv, (LANES, rows)).T[:, :1]
    hidden = jnp.where(step < team // 2, near_ref[...], far_ref[...])
    normed = (hidden * column).astype(BF16)
    normed_ref[...] = normed
    heads_ref[...] = dot_t(normed, hw_ref[...]).T[:HALF]


def rest_kernel(line, team, nact, width, total_rows, places, halves, where_ref, *refs):
    sums, pairs, refs = refs[:team], refs[team : 2 * team], refs[2 * team :]
    row_ref, log_std_ref, rinv_ref, high_ref = refs[:4]
    hw_ref, *turned_refs = refs[4:10]
    grad_ref = refs[10]
    firsts, (head_ref, ghid_ref) = refs[11:-2], refs[-2:]
    step = pl.program_id(0)
    scale = total_rows**-0.5
    slab, part = grad_ref.shape

    @pl.when(step == 0)
    def _():
        rows = high_ref.shape[0] // team
        row = lax.broadcasted_iota(jnp.int32, (HALF, rows), 0)
        diagonal = lax.broadcasted_iota(jnp.int32, (HALF, nact), 0) == lax.broadcasted_iota(
            jnp.int32, (HALF, nact), 1
        )
        std_log = jnp.sum(jnp.where(diagonal, log_std_ref[...], 0.0), 1, keepdims=True)
        isd = jnp.where(lax.broadcasted_iota(jnp.int32, (HALF, 1), 0) < nact, jnp.exp(-std_log), 0.0)
        pair = pairs[0][1:2, :]
        for other in pairs[1:]:
            pair = pair + other[1:2, :]
        lane = lax.broadcasted_iota(jnp.int32, (1, LANES), 1)
        mean = jnp.sum(jnp.where(lane < 3, pair, 0.0), 1, keepdims=True) / total_rows
        square = jnp.sum(jnp.where((lane >= 3) & (lane < 6), pair, 0.0), 1, keepdims=True) / total_rows
        spread = lax.rsqrt(square - mean * mean + NORM_EPS)
        std = jnp.zeros((HALF, rows), F32)
        head = jnp.zeros((HALF, part), F32)
        for r in range(team):
            here = slice(r * rows, (r + 1) * rows)
            total = sums[0][:, here]
            for s in range(1, team):
                total = total + sums[s][:, (r ^ s) * rows : ((r ^ s) + 1) * rows]
            heads = total
            rinv = rinv_ref[:1, here]
            top = row_ref[:HALF, here].astype(F32)
            offset = jnp.where(row < nact, top - heads, 0.0)
            sample = row_ref[HALF:, here].astype(F32)
            advant = ((gae_of(row_ref[:HALF, here], nact) - mean) * spread).astype(BF16).astype(F32)
            ret = top[nact + 3 : nact + 4]
            logr = jnp.sum(
                -sample * offset * isd - 0.5 * offset * offset * isd * isd, 0, keepdims=True
            )
            ratio = jnp.exp(logr)
            clipped = jnp.clip(ratio, 1.0 - CLIP_EPS, 1.0 + CLIP_EPS)
            active = ratio * advant <= clipped * advant
            glogr = jnp.where(active, -scale * advant, 0.0) * ratio
            slope = sample * isd + offset * isd * isd
            ghead = jnp.where(
                row < nact, glogr * slope, jnp.where(row == nact, scale * (heads - ret), 0.0)
            )
            std = std + jnp.where(row < nact, glogr * slope * offset, 0.0)
            mean_gh = jnp.sum(ghead * heads, 0, keepdims=True) / width
            scaled = ghead * rinv
            high = high_ref[here, :]
            both = dot(jnp.concatenate(split(ghead), 0), high)
            head = head + both[:HALF] + both[HALF:]
            turned = jnp.concatenate(
                [
                    scaled,
                    jnp.broadcast_to(rinv * mean_gh, (HALF, rows)),
                    jnp.zeros((LANES - 2 * HALF, rows), F32),
                ],
                0,
            ).T
            ghn = dot(jnp.concatenate(split(turned), 1), hw_ref[...])
            ghid = (ghn - high.astype(F32) * turned[:, HALF : HALF + 1]).astype(BF16)
            for first, size, place in places[r]:
                ghid_ref[place : place + size, :] = ghid[first : first + size]
        row = lax.broadcasted_iota(jnp.int32, (HALF, part), 0)
        lane = lax.broadcasted_iota(jnp.int32, (HALF, part), 1)
        std = jnp.where(row == lane, jnp.sum(std, 1, keepdims=True), 0.0)
        std = jnp.sum(std, 0, keepdims=True)
        head = jnp.where(row == nact + 1, std, head)
        head_ref[...] = head
        for i, ref in enumerate(firsts):
            cols = ref.shape[1]
            h = i % halves
            ref[slab:, :] = head[:, h * cols : (h + 1) * cols].astype(BF16)

    grad = dot(jnp.concatenate([ref[...] for ref in turned_refs], 1), ghid_ref[...])
    grad_ref[...] = grad
    for i, index in enumerate(first_blocks(line)):

        @pl.when(step == index)
        def _(i=i):
            for h, ref in enumerate(firsts[i * halves : (i + 1) * halves]):
                cols = ref.shape[1]
                ref[:slab, :] = grad[:, h * cols : (h + 1) * cols].astype(BF16)


def first_blocks(line):
    return sorted({line - 2, 2})


def hop_kernel(head_ref, *refs):
    head = head_ref[...]
    for mine, got, send in zip(refs[:2], refs[2:4], refs[4:]):
        slab = mine.shape[0]
        send[:slab, :] = (mine[...] + got[:slab, :].astype(F32)).astype(BF16)
        send[slab:, :] = (head + got[slab:, :].astype(F32)).astype(BF16)


def final_kernel(where_ref, mine_ref, head_ref, *refs):
    got, pieces = refs[:2], refs[2:]
    q = where_ref[0]
    slab = mine_ref.shape[0]
    kr = slab // len(pieces)
    head = head_ref[...]
    for ref in got:
        head = head + ref[slab:, :].astype(F32)
    for r, piece in enumerate(pieces):
        here = pl.ds(pl.multiple_of((q ^ r) * kr, kr), kr)
        total = mine_ref[here, :]
        for ref in got:
            total = total + ref[here, :].astype(F32)
        piece[:kr, :] = total.astype(piece.dtype)
        piece[kr:, :] = head.astype(piece.dtype)


def assemble_kernel(halves, where_ref, *refs):
    pieces, (grad_ref, head_ref) = refs[:-2], refs[-2:]
    heads_n = head_ref.shape[0]
    q = where_ref[0]
    kr, cols = grad_ref.shape[0], pieces[0].shape[1]
    team = len(pieces) // halves
    for i, piece in enumerate(pieces):
        h, r = i // team, i % team
        here = pl.ds(pl.multiple_of(((q ^ r) * halves + h) * cols, cols), cols)
        grad_ref[:, here] = piece[:kr, :].astype(F32)
        head = piece[kr:, :].astype(F32)
        head_ref[:, here] = head[:heads_n]


def plain(shape):
    return pl.BlockSpec(shape, lambda i: (0,) * len(shape))


def whole(shape):
    return pl.BlockSpec(shape, lambda i, w: (0,) * len(shape))


def local(
    obs_feat,
    reward,
    value_old,
    done,
    minibatch_perm,
    old_mean,
    noise,
    gain_in,
    out_weight,
    head_weight,
    log_std,
):
    n = lax.axis_size("fsdp")
    me = lax.axis_index("fsdp")
    team = 4
    line = n // team
    q = me % team
    z = me // team
    rows, width = obs_feat.shape
    part = width // team
    kr = out_weight.shape[0]
    slab = kr * team
    nact = log_std.shape[0]
    heads_n = nact + 1
    per_peer = rows // n
    total_rows = rows * n
    team_rows = team * rows
    where = jnp.stack([q, z]).astype(jnp.int32)

    def mate(x, r):
        return lax.ppermute(x, "fsdp", [(i, i ^ r) for i in range(n)]) if r else x

    def up(x, low, high, wrap=False):
        steps = [(a, a + 1) for a in range(low, high)] + ([(line - 1, 0)] if wrap else [])
        return lax.ppermute(x, "fsdp", [(a * team + i, b * team + i) for a, b in steps for i in range(team)])

    def down(x, low, high, wrap=False):
        steps = [(a, a - 1) for a in range(low, high)] + ([(0, line - 1)] if wrap else [])
        return lax.ppermute(x, "fsdp", [(a * team + i, b * team + i) for a, b in steps for i in range(team)])

    pieces = [
        mate(lax.dynamic_slice(out_weight, (0, (q ^ r) * part), (kr, part)), r) for r in range(team)
    ]
    x_core = mate(obs_feat, 1)
    small, pair = pl.pallas_call(
        functools.partial(small_kernel, nact, per_peer),
        out_shape=(
            jax.ShapeDtypeStruct((2 * HALF, rows), BF16),
            jax.ShapeDtypeStruct((HALF, part), BF16),
        ),
        grid=(1,),
        in_specs=[
            plain(reward.shape),
            plain(value_old.shape),
            plain(done.shape),
            plain((nact, rows)),
            plain((nact, rows)),
            plain((1, rows)),
        ],
        out_specs=[plain((2 * HALF, rows)), plain((HALF, part))],
        scratch_shapes=[pltpu.VMEM((reward.shape[0], LANES), F32), pltpu.VMEM((HALF, rows), F32)],
        compiler_params=params(60),
        cost_estimate=CHEAP,
        name="small",
    )(reward, value_old, done, old_mean.T, noise.T, minibatch_perm[None, :])
    cut = rows - LANES
    obs_first = obs_feat[:cut]
    x_core, small, pair, pieces, where, obs_first, obs_late, head_weight, log_std = (
        lax.optimization_barrier(
            (x_core, small, pair, pieces, where, obs_first, obs_feat, head_weight, log_std)
        )
    )
    obs_last = obs_late[cut:]

    hw = lax.dynamic_slice(head_weight, (q * part, 0), (part, heads_n)).T
    hw_twice = jnp.pad(hw, ((0, LANES - heads_n), (0, 0)))
    hw_twice = jnp.concatenate([hw_twice, hw_twice], 0)

    gain = gain_in[None, :]
    block = pl.pallas_call(
        join_kernel,
        out_shape=jax.ShapeDtypeStruct((slab + HALF, part), BF16),
        grid_spec=pltpu.PrefetchScalarGridSpec(
            num_scalar_prefetch=1,
            grid=(1,),
            in_specs=[whole((kr, part))] * team + [whole((HALF, part))],
            out_specs=whole((slab + HALF, part)),
        ),
        compiler_params=params(),
        cost_estimate=CHEAP,
        name="join",
    )(where, *pieces, pair)

    fs, bs = [up(block, 0, line - 1, True)], [down(block, 1, line, True)]
    far = mate(obs_first, 2)
    small_core = mate(small, 1)
    obs_late, small_core = lax.optimization_barrier((obs_late, small_core))
    normed_own, normed_core = norm([obs_late], gain), norm([x_core], gain)
    small = jnp.concatenate([small, small_core], 1)
    small_far = mate(small, 2)
    (fs, bs, far, small, small_far, normed_own, normed_core, obs_last, hw_twice) = (
        lax.optimization_barrier(
            (fs, bs, far, small, small_far, normed_own, normed_core, obs_last, hw_twice)
        )
    )
    for j in range(2, line - 1):
        fs.append(up(fs[-1], j - 1, line - 1))
        bs.append(down(bs[-1], 1, line - j + 1))
    diag = mate(far, 1)
    late = mate(obs_last, 2)
    normed_far, normed_diag = norm([far], gain), norm([diag], gain)
    near_blocks = [block, fs[0], bs[0]]

    def early(xs, normed):
        size = sum(x.shape[0] for x in xs)
        return pl.pallas_call(
            functools.partial(early_kernel, line, len(xs)),
            out_shape=(
                jax.ShapeDtypeStruct((size, part), F32),
                jax.ShapeDtypeStruct((HALF, LANES), F32),
            ),
            grid_spec=pltpu.PrefetchScalarGridSpec(
                num_scalar_prefetch=1,
                grid=(1,),
                in_specs=[whole(block.shape)] * 3
                + [pl.BlockSpec((x.shape[0], part), lambda i, w: (0, w[0])) for x in xs]
                + [whole(x.shape) for x in normed],
                out_specs=[whole((size, part)), whole((HALF, LANES))],
            ),
            compiler_params=params(58),
            cost_estimate=CHEAP,
            name="early",
        )(where, *near_blocks, *xs, *normed)

    in_columns = slab % LANES == 0
    early_near = early([obs_late, x_core], [normed_own[0], normed_core[0]]) if in_columns else ()
    fs, bs, late, small, small_far, normed_far, normed_diag, early_near = lax.optimization_barrier(
        (fs, bs, late, small, small_far, normed_far, normed_diag, early_near)
    )
    far_blocks = fs[1:] + bs[1:]

    packed = per_peer % 8 == 0 and team // 2 * per_peer % 16 == 0
    some = team // 2
    some_rows = some * rows

    def hidden(layout, rowdata, operands, specs, scratch=(), raw=(), joined=False):
        sum_rows = team_rows if joined else some_rows
        send_shape = (n, some * per_peer, part) if packed else (some_rows, part)
        out = pl.pallas_call(
            functools.partial(hidden_kernel, line, nact, packed, layout, raw, joined),
            out_shape=[
                jax.ShapeDtypeStruct((some_rows, part), F32),
                jax.ShapeDtypeStruct((SMALL, sum_rows), F32),
                jax.ShapeDtypeStruct(send_shape, BF16),
            ],
            grid_spec=pltpu.PrefetchScalarGridSpec(
                num_scalar_prefetch=1,
                grid=(1,),
                in_specs=[whole(block.shape)] * len(far_blocks)
                + specs
                + [whole((2 * HALF, some_rows))],
                out_specs=[whole((some_rows, part)), whole((SMALL, sum_rows)), whole(send_shape)],
                scratch_shapes=[pltpu.VMEM((some_rows, part), F32), *scratch],
            ),
            compiler_params=params(58),
            cost_estimate=CHEAP,
            name="hidden",
        )(where, *far_blocks, *operands, rowdata)
        if not packed:
            high, sums, send = out
            send = send.reshape(some, n, per_peer, part).transpose(1, 0, 2, 3)
            return high, sums, send.reshape(n, some * per_peer, part)
        return out

    def scatter(send):
        return lax.all_to_all(send, "fsdp", split_axis=0, concat_axis=0, tiled=True)

    def at_once(layout, rowdata, xs, normed, raw=(), others=()):
        return hidden(
            layout,
            rowdata,
            [*near_blocks, *xs, *normed, gain, *others],
            [whole(block.shape) for block in near_blocks]
            + [pl.BlockSpec((x.shape[0], part), lambda i, w: (0, w[0])) for x in xs]
            + [whole(x.shape) for x in (*normed, gain, *others)],
            [pltpu.VMEM((width, part), BF16)],
            raw,
            len(others) > 0,
        )

    normed = [normed_own[0], normed_core[0]]
    if in_columns:
        columns = [(x, j) for x in normed for j in range(2, line - 1)]
        hidden_near, sums_near, send = hidden(
            [[(0, rows)], [(1, rows)]],
            small,
            [*early_near] + [x for x, _ in columns],
            [whole(x.shape) for x in early_near]
            + [
                pl.BlockSpec((rows, slab), lambda i, w, j=j: (0, lax.rem(w[1] - j + line, line)))
                for _, j in columns
            ],
        )
    else:
        layout = [[(0, rows, 0, 0)], [(1, rows, 1, 0)]]
        hidden_near, sums_near, send = at_once(layout, small, [obs_late, x_core], normed)
    recv_near = scatter(send)
    last = mate(late, 1)
    late, last, sums_near = lax.optimization_barrier((late, last, sums_near))
    hidden_far, sums, send = at_once(
        [[(0, cut, 0, 0), (2, LANES, 2, 0)], [(1, cut, 1, 0), (3, LANES, 3, 0)]],
        small_far,
        [far, diag, late, last],
        [normed_far[0], normed_diag[0], late, last],
        (2, 3),
        (sums_near,),
    )
    squares = [mate(sums, r) for r in range(team)]
    late, last, small, small_far, sums = lax.optimization_barrier((late, last, small, small_far, sums))
    normed_last = norm([late, last], gain)
    small_all = jnp.concatenate([small, small_far], 1)
    squares, normed_last, small_all = lax.optimization_barrier((squares, normed_last, small_all))
    normed_hidden, heads, rinv = pl.pallas_call(
        functools.partial(heads_kernel, team, width),
        out_shape=(
            jax.ShapeDtypeStruct((team_rows, part), BF16),
            jax.ShapeDtypeStruct((HALF, team_rows), F32),
            jax.ShapeDtypeStruct((SMALL, team_rows), F32),
        ),
        grid=(team,),
        in_specs=[plain((SMALL, team_rows))] * team
        + [
            pl.BlockSpec((rows, part), lambda i: (jnp.minimum(i, some - 1), 0)),
            pl.BlockSpec((rows, part), lambda i: (jnp.maximum(i - some, 0), 0)),
            plain((LANES, part)),
        ],
        out_specs=[
            pl.BlockSpec((rows, part), lambda i: (i, 0)),
            pl.BlockSpec((HALF, rows), lambda i: (0, i)),
            pl.BlockSpec((SMALL, rows), lambda i: (0, i)),
        ],
        compiler_params=params(58),
        cost_estimate=CHEAP,
        name="heads",
    )(*squares, hidden_near, hidden_far, hw_twice)
    sums = [mate(heads, r) for r in range(team)]
    send, recv_near = lax.optimization_barrier((send, recv_near))
    recv_far = scatter(send)
    nfirst = len(first_blocks(line))
    halves = HALVES
    cols = part // halves
    message = (slab + HALF, cols)
    turned = [pair[1] for pair in (normed_own, normed_core, normed_far, normed_diag, normed_last)]
    places = [[(0, rows, 0)], [(0, rows, rows)]] + [
        [(0, cut, 2 * rows + i * cut), (cut, LANES, 2 * rows + 2 * cut + i * LANES)] for i in range(2)
    ]
    outs = pl.pallas_call(
        functools.partial(rest_kernel, line, team, nact, width, total_rows, places, halves),
        out_shape=[jax.ShapeDtypeStruct((width, part), F32)]
        + [jax.ShapeDtypeStruct(message, BF16)] * (nfirst * halves)
        + [jax.ShapeDtypeStruct((HALF, part), F32)],
        grid_spec=pltpu.PrefetchScalarGridSpec(
            num_scalar_prefetch=1,
            grid=(line,),
            in_specs=[whole((HALF, team_rows))] * team
            + [pl.BlockSpec((SMALL, LANES), lambda i, w: (0, 0))] * team
            + [
                whole((2 * HALF, team_rows)),
                whole((1, nact)),
                whole((SMALL, team_rows)),
                whole((team_rows, part)),
                whole((2 * LANES, part)),
            ]
            + [
                pl.BlockSpec((slab, piece.shape[1]), lambda i, w: (lax.rem(w[1] + i, line), 0))
                for piece in turned
            ],
            out_specs=[pl.BlockSpec((slab, part), lambda i, w: (i, 0))]
            + [whole(message)] * (nfirst * halves)
            + [whole((HALF, part))],
            scratch_shapes=[pltpu.VMEM((team_rows, part), BF16)],
        ),
        compiler_params=params(58),
        cost_estimate=COSTLY,
        name="rest",
    )(where, *sums, *squares, small_all, log_std[None, :], rinv, normed_hidden, hw_twice, *turned)
    grads, firsts, head = outs[0], outs[1:-1], outs[-1]

    def hop(h, up_block, down_block, *got):
        return pl.pallas_call(
            hop_kernel,
            out_shape=[jax.ShapeDtypeStruct(message, BF16)] * 2,
            grid=(1,),
            in_specs=[
                pl.BlockSpec((HALF, cols), lambda i: (0, h)),
                pl.BlockSpec((slab, cols), lambda i: (up_block, h)),
                pl.BlockSpec((slab, cols), lambda i: (down_block, h)),
            ]
            + [plain(message)] * 2,
            out_specs=[plain(message)] * 2,
            compiler_params=params(),
            cost_estimate=CHEAP,
            name="hop",
        )(head, grads, grads, *got)

    def final(h, *got):
        return pl.pallas_call(
            final_kernel,
            out_shape=[jax.ShapeDtypeStruct((kr + HALF, cols), F32)]
            + [jax.ShapeDtypeStruct((kr + HALF, cols), BF16)] * (team - 1),
            grid_spec=pltpu.PrefetchScalarGridSpec(
                num_scalar_prefetch=1,
                grid=(1,),
                in_specs=[
                    pl.BlockSpec((slab, cols), lambda i, w: (0, h)),
                    pl.BlockSpec((HALF, cols), lambda i, w: (0, h)),
                ]
                + [whole(message)] * 2,
                out_specs=[whole((kr + HALF, cols))] * team,
            ),
            compiler_params=params(),
            cost_estimate=CHEAP,
            name="final",
        )(where, grads, head, *got)

    recv_near = recv_near.reshape(line, team, some, per_peer, part)
    recv_far = recv_far.reshape(line, team, some, per_peer, part)

    def from_member(c, m):
        r = c ^ m
        return recv_near[:, c, r] if r < some else recv_far[:, c, r - some]

    hidden_out = jnp.concatenate(
        [jnp.stack([from_member(c, m) for m in range(team)], 1) for c in range(team)], -1
    ).reshape(rows, width)
    got = [(firsts[h - halves], firsts[h]) for h in range(halves)]
    for k in range(line - 2, 0, -1):
        if k < line - 2:
            got = [hop(h, k, line - k, *got[h]) for h in range(halves)]
        got = [(up(f, 0, line - k, k == 1), down(b, k, line, k == 1)) for f, b in got]
        if k == 2:
            got[0], hidden_out = lax.optimization_barrier((got[0], hidden_out))
    pieces = []
    for h in range(halves):
        pieces += [mate(piece, r) for r, piece in enumerate(final(h, *got[h]))]
    grad_weight, heads = pl.pallas_call(
        functools.partial(assemble_kernel, halves),
        out_shape=(
            jax.ShapeDtypeStruct((kr, width), F32),
            jax.ShapeDtypeStruct((heads_n, width), F32),
        ),
        grid_spec=pltpu.PrefetchScalarGridSpec(
            num_scalar_prefetch=1,
            grid=(1,),
            in_specs=[whole(piece.shape) for piece in pieces],
            out_specs=[whole((kr, width)), whole((heads_n, width))],
        ),
        compiler_params=params(),
        cost_estimate=CHEAP,
        name="assemble",
    )(where, *pieces)
    grad_head = heads.T
    grad_std = pieces[0][kr + heads_n, :nact]

    return (hidden_out, grad_weight, grad_head, grad_std)


def solution(mesh):
    return jax.shard_map(
        local,
        mesh=mesh,
        in_specs=(
            P(("groups", "fsdp"), None),
            P(("groups", "fsdp"), None),
            P(("groups", "fsdp"), None),
            P(("groups", "fsdp"), None),
            P(("groups", "fsdp")),
            P(("groups", "fsdp"), None),
            P(("groups", "fsdp"), None),
            P(),
            P("fsdp", None),
            P(),
            P(),
        ),
        out_specs=(
            P(("groups", "fsdp"), None),
            P(("groups", "fsdp"), None),
            P("groups", None),
            P("groups"),
        ),
        check_vma=False,
    )
```

```python
import functools

import jax
import jax.numpy as jnp
from jax import lax
from jax.experimental import pallas as pl
from jax.experimental.pallas import tpu as pltpu
from jax.sharding import PartitionSpec as P

GAMMA = 0.99
LAMBDA_GAE = 0.95
CLIP_EPS = 0.2
NORM_EPS = 1e-05
F32 = jnp.float32
BF16 = jnp.bfloat16
LANES = 128
HALVES = 2
SMALL = 8
HALF = 16
MIB = 1024 * 1024
CHEAP = pl.CostEstimate(flops=1, bytes_accessed=1, transcendentals=0)
COSTLY = pl.CostEstimate(flops=10**11, bytes_accessed=10**8, transcendentals=0)


def params(mib=50):
    return pltpu.CompilerParams(vmem_limit_bytes=mib * MIB, dimension_semantics=("arbitrary",))


def split(x):
    high = x.astype(BF16)
    return high, (x - high.astype(F32)).astype(BF16)


def dot(a, b):
    return jnp.dot(a, b, preferred_element_type=F32)


def dot_t(a, b):
    return lax.dot_general(a, b, (((1,), (1,)), ((), ())), preferred_element_type=F32)


def shifted(x, by):
    return pltpu.roll(x, LANES - by, 1)


def small_kernel(
    nact, per_peer, reward_ref, value_ref, done_ref, old_ref, noise_ref, perm_ref, small_ref, pair_ref, pad_ref, tall_ref
):
    envs, steps = reward_ref.shape
    rows = perm_ref.shape[1]

    def wide(x):
        pad_ref[...] = jnp.zeros_like(pad_ref)
        pad_ref[:, : x.shape[1]] = x
        return pad_ref[...]

    inside = lax.broadcasted_iota(jnp.int32, (envs, LANES), 1) < steps
    value = wide(value_ref[...])
    keep = 1.0 - wide(done_ref[...].astype(F32))
    delta = wide(reward_ref[...]) + GAMMA * shifted(value, 1) * keep - value
    gae = jnp.where(inside, delta, 0.0)
    factor = jnp.where(inside, GAMMA * LAMBDA_GAE * keep, 0.0)
    reach = 1
    while reach < steps:
        gae = gae + factor * shifted(gae, reach)
        factor = factor * shifted(factor, reach)
        reach *= 2
    ret = gae + value
    high, low = split(gae)
    mid, low = split(gae - high.astype(F32))
    lane = lax.broadcasted_iota(jnp.int32, (LANES, rows), 1)
    pick = jnp.where(
        lax.rem(lane, steps) == lax.broadcasted_iota(jnp.int32, (LANES, rows), 0), 1.0, 0.0
    ).astype(BF16)
    lane = lax.broadcasted_iota(jnp.int32, (envs, rows), 1)
    mine = lane // steps == lax.broadcasted_iota(jnp.int32, (envs, rows), 0)

    def flat(x):
        return jnp.sum(jnp.where(mine, dot(x, pick), 0.0), 0, keepdims=True)

    perm = perm_ref[...]
    slot = perm // rows * per_peer + lax.rem(perm, per_peer)
    row = lax.broadcasted_iota(jnp.int32, (HALF, rows), 0)

    def put(block, index, values):
        return jnp.where(row == index, values, block)

    def tall(x):
        tall_ref[...] = jnp.zeros_like(tall_ref)
        tall_ref[:nact, :] = x.astype(F32)
        return tall_ref[...]

    top = tall(old_ref[...])
    for index, values in enumerate((high, mid, low, ret.astype(BF16))):
        top = put(top, nact + index, flat(values))
    bottom = tall(noise_ref[...])
    bottom = put(bottom, nact, (slot // 256).astype(F32))
    bottom = put(bottom, nact + 1, lax.rem(slot, 256).astype(F32))
    small = jnp.concatenate([top, bottom], 0).astype(BF16)
    small_ref[...] = small
    gae = gae_of(small[:HALF], nact)
    lane = lax.broadcasted_iota(jnp.int32, pair_ref.shape, 1)
    pair = jnp.zeros(pair_ref.shape, F32)
    for first, value in ((0, gae), (3, gae * gae)):
        value = jnp.sum(value, 1, keepdims=True)
        for i in range(3):
            rounded = value.astype(BF16).astype(F32)
            pair = jnp.where(lane == first + i, rounded, pair)
            value = value - rounded
    pair_ref[...] = pair.astype(BF16)


def gae_of(small, nact):
    block = small.astype(F32)
    return block[nact : nact + 1] + block[nact + 1 : nact + 2] + block[nact + 2 : nact + 3]


def join_kernel(where_ref, *refs):
    pieces, pair_ref, block_ref = refs[:-2], refs[-2], refs[-1]
    kr = pieces[0].shape[0]
    for r, piece in enumerate(pieces):
        here = pl.ds(pl.multiple_of((where_ref[0] ^ r) * kr, kr), kr)
        block_ref[here, :] = piece[...]
    block_ref[kr * len(pieces) :, :] = pair_ref[...]


def norm_kernel(*refs):
    x_refs, gain_ref, normed_ref, turned_ref = refs[:-3], refs[-3], refs[-2], refs[-1]

    def one(x):
        xf = x.astype(F32)
        rms = lax.rsqrt(jnp.mean(xf * xf, -1, keepdims=True) + NORM_EPS)
        normed = xf * rms * gain_ref[...]
        normed_ref[...] = normed.astype(BF16)
        turned_ref[...] = normed.T.astype(BF16)

    if len(x_refs) == 1:
        one(x_refs[0][...])
    else:
        for i, ref in enumerate(x_refs):
            pl.when(pl.program_id(0) == i)(functools.partial(lambda ref: one(ref[...]), ref))


def norm(xs, gain):
    rows, width = xs[0].shape
    grid = rows // LANES if len(xs) == 1 else len(xs)
    source = (lambda i: (i, 0)) if len(xs) == 1 else (lambda i: (0, 0))
    return pl.pallas_call(
        norm_kernel,
        out_shape=(
            jax.ShapeDtypeStruct((rows * len(xs), width), BF16),
            jax.ShapeDtypeStruct((width, rows * len(xs)), BF16),
        ),
        grid=(grid,),
        in_specs=[pl.BlockSpec((LANES, width), source)] * len(xs)
        + [pl.BlockSpec((1, width), lambda i: (0, 0))],
        out_specs=[
            pl.BlockSpec((LANES, width), lambda i: (i, 0)),
            pl.BlockSpec((width, LANES), lambda i: (0, i)),
        ],
        compiler_params=params(58),
        cost_estimate=CHEAP,
        name="norm",
    )(*xs, gain)


def early_kernel(line, pieces, where_ref, *refs):
    blocks, refs = refs[:3], refs[3:]
    xq_refs, normed_refs, (sum_ref, pair_ref) = refs[:pieces], refs[pieces:-2], refs[-2:]
    z = where_ref[1]
    slab = blocks[0].shape[0] - HALF
    at = 0
    for xq, normed in zip(xq_refs, normed_refs):
        rows = xq.shape[0]
        total = xq[...].astype(F32)
        for block, step in zip(blocks, (0, line - 1, 1)):
            place = pl.multiple_of(lax.rem(z + step, line) * slab, slab)
            total = total + dot(normed[:, pl.ds(place, slab)], block[:slab, :])
        sum_ref[at : at + rows, :] = total
        at += rows
    pair = jnp.zeros(pair_ref.shape, F32)
    for block in blocks:
        pair = pair + block[slab:, :LANES].astype(F32)
    pair_ref[...] = pair


def hidden_kernel(line, nact, packed, layout, raw, joined, where_ref, *refs):
    late = len(layout[0][0]) == 4
    n_x = 1 + max(index for pieces in layout for index, *_ in pieces)
    js = line - 3
    blocks, refs = refs[: 2 * js], refs[2 * js :]
    if late:
        near, refs = refs[:3], refs[3:]
        w_ref, refs = refs[-1], refs[:-1]
        gain_ref = refs[-7 if joined else -6]
    else:
        early_ref, pair_ref, refs = refs[0], refs[1], refs[2:]
    n_columns = len(refs) - 5
    columns, refs = refs[:n_columns], refs[n_columns:]
    row_ref, hidden_ref, sums_ref, send_ref, sorted_ref = refs
    z = where_ref[1]
    members = len(layout)
    rows = hidden_ref.shape[0] // members
    slab = blocks[0].shape[0] - HALF

    def far_block(j):
        return jnp.where(z >= j, blocks[j - 2][:slab, :], blocks[js + line - j - 2][:slab, :])

    if late:
        for j in range(line):
            place = pl.multiple_of(lax.rem(z - j + line, line) * slab, slab)
            nearest = j in (0, 1, line - 1)
            w_ref[pl.ds(place, slab), :] = near[min(j, 2)][:slab, :] if nearest else far_block(j)

    ahead = columns[-1].shape[1] if joined else 0
    if joined:
        sums_ref[:, :ahead] = columns[-1][...]
    for m, pieces in enumerate(layout):
        at = m * rows
        for index, size, *place in pieces:
            if late:
                normed = columns[n_x + place[0]][place[1] : place[1] + size, :]
                if place[0] in raw:
                    xf = normed.astype(F32)
                    rms = lax.rsqrt(jnp.mean(xf * xf, -1, keepdims=True) + NORM_EPS)
                    normed = (xf * rms * gain_ref[...]).astype(BF16)
                total = columns[index][...].astype(F32) + dot(normed, w_ref[...])
            else:
                total = early_ref[at : at + size, :]
                for j in range(2, line - 1):
                    total = total + dot(columns[index * js + j - 2][...], far_block(j))
            sorted_ref[at : at + size, :] = total
            at += size
        here = slice(m * rows, (m + 1) * rows)
        hidden = sorted_ref[here, :]
        hidden_ref[here, :] = hidden
        high = hidden.astype(BF16)
        square = jnp.sum(hidden * hidden, 1, keepdims=True)
        square = jnp.broadcast_to(square, (rows, LANES)).T[:SMALL]
        pair = jnp.zeros((HALF, LANES), F32) if late else pair_ref[...]
        for ref in (*near, *blocks) if late else blocks:
            pair = pair + ref[slab:, :LANES].astype(F32)
        pair = jnp.concatenate([pair[:1], jnp.zeros((1, rows - LANES), F32)], 1)
        row = lax.broadcasted_iota(jnp.int32, square.shape, 0)
        sums_ref[:, ahead + m * rows : ahead + (m + 1) * rows] = jnp.where(row == 1, pair, square)
        bottom = row_ref[HALF:, here].astype(F32)
        slot = (bottom[nact : nact + 1] * 256.0 + bottom[nact + 1 : nact + 2]).astype(jnp.int32)
        order = lax.broadcasted_iota(jnp.int32, (rows, rows), 0) == slot
        ranked = dot(jnp.where(order, 1.0, 0.0).astype(BF16), high)
        if packed:
            sorted_ref[here, :] = ranked
        else:
            send_ref[here, :] = ranked.astype(BF16)
    if packed:
        n, size, _ = send_ref.shape
        peer = size // members
        for j in range(n):
            send_ref[j] = jnp.concatenate(
                [sorted_ref[r * rows + j * peer : r * rows + (j + 1) * peer, :] for r in range(members)],
                0,
            ).astype(BF16)


def heads_kernel(team, width, *refs):
    squares, (near_ref, far_ref, hw_ref, normed_ref, heads_ref, rinv_ref) = refs[:team], refs[team:]
    some = team // 2
    rows = near_ref.shape[0] // some

    def run(first, hidden_ref):
        for m in range(some):
            here = slice(m * rows, (m + 1) * rows)
            total = jnp.zeros((1, rows), F32)
            for s, ref in enumerate(squares):
                place = ((first + m) ^ s) * rows
                total = total + ref[:1, place : place + rows]
            rinv = lax.rsqrt(total / width + NORM_EPS)
            rinv_ref[:, here] = jnp.broadcast_to(rinv, (SMALL, rows))
            column = jnp.broadcast_to(rinv, (LANES, rows)).T[:, :1]
            normed = (hidden_ref[here, :] * column).astype(BF16)
            normed_ref[here, :] = normed
            heads_ref[:, here] = dot_t(normed, hw_ref[...]).T[:HALF]

    pl.when(pl.program_id(0) == 0)(lambda: run(0, near_ref))
    pl.when(pl.program_id(0) == 1)(lambda: run(some, far_ref))


def rest_kernel(line, team, nact, width, total_rows, places, halves, where_ref, *refs):
    sums, pairs, refs = refs[:team], refs[team : 2 * team], refs[2 * team :]
    row_ref, log_std_ref, rinv_ref, high_ref = refs[:4]
    hw_ref, *turned_refs = refs[4:10]
    grad_ref = refs[10]
    firsts, (head_ref, ghid_ref) = refs[11:-2], refs[-2:]
    step = pl.program_id(0)
    scale = total_rows**-0.5
    slab, part = grad_ref.shape

    @pl.when(step == 0)
    def _():
        rows = high_ref.shape[0] // team
        row = lax.broadcasted_iota(jnp.int32, (HALF, rows), 0)
        diagonal = lax.broadcasted_iota(jnp.int32, (HALF, nact), 0) == lax.broadcasted_iota(
            jnp.int32, (HALF, nact), 1
        )
        std_log = jnp.sum(jnp.where(diagonal, log_std_ref[...], 0.0), 1, keepdims=True)
        isd = jnp.where(lax.broadcasted_iota(jnp.int32, (HALF, 1), 0) < nact, jnp.exp(-std_log), 0.0)
        pair = pairs[0][1:2, :]
        for other in pairs[1:]:
            pair = pair + other[1:2, :]
        lane = lax.broadcasted_iota(jnp.int32, (1, LANES), 1)
        mean = jnp.sum(jnp.where(lane < 3, pair, 0.0), 1, keepdims=True) / total_rows
        square = jnp.sum(jnp.where((lane >= 3) & (lane < 6), pair, 0.0), 1, keepdims=True) / total_rows
        spread = lax.rsqrt(square - mean * mean + NORM_EPS)
        std = jnp.zeros((HALF, rows), F32)
        head = jnp.zeros((HALF, part), F32)
        for r in range(team):
            here = slice(r * rows, (r + 1) * rows)
            total = sums[0][:, here]
            for s in range(1, team):
                total = total + sums[s][:, (r ^ s) * rows : ((r ^ s) + 1) * rows]
            heads = total
            rinv = rinv_ref[:1, here]
            top = row_ref[:HALF, here].astype(F32)
            offset = jnp.where(row < nact, top - heads, 0.0)
            sample = row_ref[HALF:, here].astype(F32)
            advant = ((gae_of(row_ref[:HALF, here], nact) - mean) * spread).astype(BF16).astype(F32)
            ret = top[nact + 3 : nact + 4]
            logr = jnp.sum(
                -sample * offset * isd - 0.5 * offset * offset * isd * isd, 0, keepdims=True
            )
            ratio = jnp.exp(logr)
            clipped = jnp.clip(ratio, 1.0 - CLIP_EPS, 1.0 + CLIP_EPS)
            active = ratio * advant <= clipped * advant
            glogr = jnp.where(active, -scale * advant, 0.0) * ratio
            slope = sample * isd + offset * isd * isd
            ghead = jnp.where(
                row < nact, glogr * slope, jnp.where(row == nact, scale * (heads - ret), 0.0)
            )
            std = std + jnp.where(row < nact, glogr * slope * offset, 0.0)
            mean_gh = jnp.sum(ghead * heads, 0, keepdims=True) / width
            scaled = ghead * rinv
            high = high_ref[here, :]
            both = dot(jnp.concatenate(split(ghead), 0), high)
            head = head + both[:HALF] + both[HALF:]
            turned = jnp.concatenate(
                [
                    scaled,
                    jnp.broadcast_to(rinv * mean_gh, (HALF, rows)),
                    jnp.zeros((LANES - 2 * HALF, rows), F32),
                ],
                0,
            ).T
            ghn = dot(jnp.concatenate(split(turned), 1), hw_ref[...])
            ghid = (ghn - high.astype(F32) * turned[:, HALF : HALF + 1]).astype(BF16)
            for first, size, place in places[r]:
                ghid_ref[place : place + size, :] = ghid[first : first + size]
        row = lax.broadcasted_iota(jnp.int32, (HALF, part), 0)
        lane = lax.broadcasted_iota(jnp.int32, (HALF, part), 1)
        std = jnp.where(row == lane, jnp.sum(std, 1, keepdims=True), 0.0)
        std = jnp.sum(std, 0, keepdims=True)
        head = jnp.where(row == nact + 1, std, head)
        head_ref[...] = head
        for i, ref in enumerate(firsts):
            cols = ref.shape[1]
            h = i % halves
            ref[slab:, :] = head[:, h * cols : (h + 1) * cols].astype(BF16)

    grad = dot(jnp.concatenate([ref[...] for ref in turned_refs], 1), ghid_ref[...])
    grad_ref[...] = grad
    for i, index in enumerate(first_blocks(line)):

        @pl.when(step == index)
        def _(i=i):
            for h, ref in enumerate(firsts[i * halves : (i + 1) * halves]):
                cols = ref.shape[1]
                ref[:slab, :] = grad[:, h * cols : (h + 1) * cols].astype(BF16)


def first_blocks(line):
    return sorted({line - 2, 2})


def hop_kernel(head_ref, *refs):
    head = head_ref[...]
    for mine, got, send in zip(refs[:2], refs[2:4], refs[4:]):
        slab = mine.shape[0]
        send[:slab, :] = (mine[...] + got[:slab, :].astype(F32)).astype(BF16)
        send[slab:, :] = (head + got[slab:, :].astype(F32)).astype(BF16)


def final_kernel(where_ref, mine_ref, head_ref, *refs):
    got, pieces = refs[:2], refs[2:]
    q = where_ref[0]
    slab = mine_ref.shape[0]
    kr = slab // len(pieces)
    head = head_ref[...]
    for ref in got:
        head = head + ref[slab:, :].astype(F32)
    for r, piece in enumerate(pieces):
        here = pl.ds(pl.multiple_of((q ^ r) * kr, kr), kr)
        total = mine_ref[here, :]
        for ref in got:
            total = total + ref[here, :].astype(F32)
        piece[:kr, :] = total.astype(piece.dtype)
        piece[kr:, :] = head.astype(piece.dtype)


def assemble_kernel(halves, where_ref, *refs):
    pieces, (grad_ref, head_ref) = refs[:-2], refs[-2:]
    heads_n = head_ref.shape[0]
    q = where_ref[0]
    kr, cols = grad_ref.shape[0], pieces[0].shape[1]
    team = len(pieces) // halves
    for i, piece in enumerate(pieces):
        h, r = i // team, i % team
        here = pl.ds(pl.multiple_of(((q ^ r) * halves + h) * cols, cols), cols)
        grad_ref[:, here] = piece[:kr, :].astype(F32)
        head = piece[kr:, :].astype(F32)
        head_ref[:, here] = head[:heads_n]


def plain(shape):
    return pl.BlockSpec(shape, lambda i: (0,) * len(shape))


def whole(shape):
    return pl.BlockSpec(shape, lambda i, w: (0,) * len(shape))


def local(
    obs_feat,
    reward,
    value_old,
    done,
    minibatch_perm,
    old_mean,
    noise,
    gain_in,
    out_weight,
    head_weight,
    log_std,
):
    n = lax.axis_size("fsdp")
    me = lax.axis_index("fsdp")
    team = 4
    line = n // team
    q = me % team
    z = me // team
    rows, width = obs_feat.shape
    part = width // team
    kr = out_weight.shape[0]
    slab = kr * team
    nact = log_std.shape[0]
    heads_n = nact + 1
    per_peer = rows // n
    total_rows = rows * n
    team_rows = team * rows
    where = jnp.stack([q, z]).astype(jnp.int32)

    def mate(x, r):
        return lax.ppermute(x, "fsdp", [(i, i ^ r) for i in range(n)]) if r else x

    def up(x, low, high, wrap=False):
        steps = [(a, a + 1) for a in range(low, high)] + ([(line - 1, 0)] if wrap else [])
        return lax.ppermute(x, "fsdp", [(a * team + i, b * team + i) for a, b in steps for i in range(team)])

    def down(x, low, high, wrap=False):
        steps = [(a, a - 1) for a in range(low, high)] + ([(0, line - 1)] if wrap else [])
        return lax.ppermute(x, "fsdp", [(a * team + i, b * team + i) for a, b in steps for i in range(team)])

    pieces = [
        mate(lax.dynamic_slice(out_weight, (0, (q ^ r) * part), (kr, part)), r) for r in range(team)
    ]
    x_core = mate(obs_feat, 1)
    small, pair = pl.pallas_call(
        functools.partial(small_kernel, nact, per_peer),
        out_shape=(
            jax.ShapeDtypeStruct((2 * HALF, rows), BF16),
            jax.ShapeDtypeStruct((HALF, part), BF16),
        ),
        grid=(1,),
        in_specs=[
            plain(reward.shape),
            plain(value_old.shape),
            plain(done.shape),
            plain((nact, rows)),
            plain((nact, rows)),
            plain((1, rows)),
        ],
        out_specs=[plain((2 * HALF, rows)), plain((HALF, part))],
        scratch_shapes=[pltpu.VMEM((reward.shape[0], LANES), F32), pltpu.VMEM((HALF, rows), F32)],
        compiler_params=params(60),
        cost_estimate=CHEAP,
        name="small",
    )(reward, value_old, done, old_mean.T, noise.T, minibatch_perm[None, :])
    cut = rows - LANES
    obs_first = obs_feat[:cut]
    x_core, small, pair, pieces, where, obs_first, obs_late, head_weight, log_std = (
        lax.optimization_barrier(
            (x_core, small, pair, pieces, where, obs_first, obs_feat, head_weight, log_std)
        )
    )
    obs_last = obs_late[cut:]

    hw = lax.dynamic_slice(head_weight, (q * part, 0), (part, heads_n)).T
    hw_twice = jnp.pad(hw, ((0, LANES - heads_n), (0, 0)))
    hw_twice = jnp.concatenate([hw_twice, hw_twice], 0)

    gain = gain_in[None, :]
    block = pl.pallas_call(
        join_kernel,
        out_shape=jax.ShapeDtypeStruct((slab + HALF, part), BF16),
        grid_spec=pltpu.PrefetchScalarGridSpec(
            num_scalar_prefetch=1,
            grid=(1,),
            in_specs=[whole((kr, part))] * team + [whole((HALF, part))],
            out_specs=whole((slab + HALF, part)),
        ),
        compiler_params=params(),
        cost_estimate=CHEAP,
        name="join",
    )(where, *pieces, pair)

    fs, bs = [up(block, 0, line - 1, True)], [down(block, 1, line, True)]
    far = mate(obs_first, 2)
    small_core = mate(small, 1)
    obs_late, small_core = lax.optimization_barrier((obs_late, small_core))
    normed_own, normed_core = norm([obs_late], gain), norm([x_core], gain)
    small = jnp.concatenate([small, small_core], 1)
    small_far = mate(small, 2)
    (fs, bs, far, small, small_far, normed_own, normed_core, obs_last, hw_twice) = (
        lax.optimization_barrier(
            (fs, bs, far, small, small_far, normed_own, normed_core, obs_last, hw_twice)
        )
    )
    for j in range(2, line - 1):
        fs.append(up(fs[-1], j - 1, line - 1))
        bs.append(down(bs[-1], 1, line - j + 1))
    diag = mate(far, 1)
    late = mate(obs_last, 2)
    normed_far, normed_diag = norm([far], gain), norm([diag], gain)
    near_blocks = [block, fs[0], bs[0]]

    def early(xs, normed):
        size = sum(x.shape[0] for x in xs)
        return pl.pallas_call(
            functools.partial(early_kernel, line, len(xs)),
            out_shape=(
                jax.ShapeDtypeStruct((size, part), F32),
                jax.ShapeDtypeStruct((HALF, LANES), F32),
            ),
            grid_spec=pltpu.PrefetchScalarGridSpec(
                num_scalar_prefetch=1,
                grid=(1,),
                in_specs=[whole(block.shape)] * 3
                + [pl.BlockSpec((x.shape[0], part), lambda i, w: (0, w[0])) for x in xs]
                + [whole(x.shape) for x in normed],
                out_specs=[whole((size, part)), whole((HALF, LANES))],
            ),
            compiler_params=params(58),
            cost_estimate=CHEAP,
            name="early",
        )(where, *near_blocks, *xs, *normed)

    in_columns = slab % LANES == 0
    early_near = early([obs_late, x_core], [normed_own[0], normed_core[0]]) if in_columns else ()
    fs, bs, late, small, small_far, normed_far, normed_diag, early_near = lax.optimization_barrier(
        (fs, bs, late, small, small_far, normed_far, normed_diag, early_near)
    )
    far_blocks = fs[1:] + bs[1:]

    packed = per_peer % 8 == 0 and team // 2 * per_peer % 16 == 0
    some = team // 2
    some_rows = some * rows

    def hidden(layout, rowdata, operands, specs, scratch=(), raw=(), joined=False):
        sum_rows = team_rows if joined else some_rows
        send_shape = (n, some * per_peer, part) if packed else (some_rows, part)
        out = pl.pallas_call(
            functools.partial(hidden_kernel, line, nact, packed, layout, raw, joined),
            out_shape=[
                jax.ShapeDtypeStruct((some_rows, part), F32),
                jax.ShapeDtypeStruct((SMALL, sum_rows), F32),
                jax.ShapeDtypeStruct(send_shape, BF16),
            ],
            grid_spec=pltpu.PrefetchScalarGridSpec(
                num_scalar_prefetch=1,
                grid=(1,),
                in_specs=[whole(block.shape)] * len(far_blocks)
                + specs
                + [whole((2 * HALF, some_rows))],
                out_specs=[whole((some_rows, part)), whole((SMALL, sum_rows)), whole(send_shape)],
                scratch_shapes=[pltpu.VMEM((some_rows, part), F32), *scratch],
            ),
            compiler_params=params(58),
            cost_estimate=CHEAP,
            name="hidden",
        )(where, *far_blocks, *operands, rowdata)
        if not packed:
            high, sums, send = out
            send = send.reshape(some, n, per_peer, part).transpose(1, 0, 2, 3)
            return high, sums, send.reshape(n, some * per_peer, part)
        return out

    def scatter(send):
        return lax.all_to_all(send, "fsdp", split_axis=0, concat_axis=0, tiled=True)

    def at_once(layout, rowdata, xs, normed, raw=(), others=()):
        return hidden(
            layout,
            rowdata,
            [*near_blocks, *xs, *normed, gain, *others],
            [whole(block.shape) for block in near_blocks]
            + [pl.BlockSpec((x.shape[0], part), lambda i, w: (0, w[0])) for x in xs]
            + [whole(x.shape) for x in (*normed, gain, *others)],
            [pltpu.VMEM((width, part), BF16)],
            raw,
            len(others) > 0,
        )

    normed = [normed_own[0], normed_core[0]]
    if in_columns:
        columns = [(x, j) for x in normed for j in range(2, line - 1)]
        hidden_near, sums_near, send = hidden(
            [[(0, rows)], [(1, rows)]],
            small,
            [*early_near] + [x for x, _ in columns],
            [whole(x.shape) for x in early_near]
            + [
                pl.BlockSpec((rows, slab), lambda i, w, j=j: (0, lax.rem(w[1] - j + line, line)))
                for _, j in columns
            ],
        )
    else:
        layout = [[(0, rows, 0, 0)], [(1, rows, 1, 0)]]
        hidden_near, sums_near, send = at_once(layout, small, [obs_late, x_core], normed)
    recv_near = scatter(send)
    last = mate(late, 1)
    late, last, sums_near = lax.optimization_barrier((late, last, sums_near))
    hidden_far, sums, send = at_once(
        [[(0, cut, 0, 0), (2, LANES, 2, 0)], [(1, cut, 1, 0), (3, LANES, 3, 0)]],
        small_far,
        [far, diag, late, last],
        [normed_far[0], normed_diag[0], late, last],
        (2, 3),
        (sums_near,),
    )
    squares = [mate(sums, r) for r in range(team)]
    late, last, small, small_far, sums = lax.optimization_barrier((late, last, small, small_far, sums))
    normed_last = norm([late, last], gain)
    small_all = jnp.concatenate([small, small_far], 1)
    squares, normed_last, small_all = lax.optimization_barrier((squares, normed_last, small_all))
    normed_hidden, heads, rinv = pl.pallas_call(
        functools.partial(heads_kernel, team, width),
        out_shape=(
            jax.ShapeDtypeStruct((team_rows, part), BF16),
            jax.ShapeDtypeStruct((HALF, team_rows), F32),
            jax.ShapeDtypeStruct((SMALL, team_rows), F32),
        ),
        grid=(2,),
        in_specs=[plain((SMALL, team_rows))] * team
        + [plain((some_rows, part)), plain((some_rows, part)), plain((LANES, part))],
        out_specs=[
            pl.BlockSpec((some_rows, part), lambda i: (i, 0)),
            pl.BlockSpec((HALF, some_rows), lambda i: (0, i)),
            pl.BlockSpec((SMALL, some_rows), lambda i: (0, i)),
        ],
        compiler_params=params(58),
        cost_estimate=CHEAP,
        name="heads",
    )(*squares, hidden_near, hidden_far, hw_twice)
    sums = [mate(heads, r) for r in range(team)]
    send, recv_near = lax.optimization_barrier((send, recv_near))
    recv_far = scatter(send)
    nfirst = len(first_blocks(line))
    halves = HALVES
    cols = part // halves
    message = (slab + HALF, cols)
    turned = [pair[1] for pair in (normed_own, normed_core, normed_far, normed_diag, normed_last)]
    places = [[(0, rows, 0)], [(0, rows, rows)]] + [
        [(0, cut, 2 * rows + i * cut), (cut, LANES, 2 * rows + 2 * cut + i * LANES)] for i in range(2)
    ]
    outs = pl.pallas_call(
        functools.partial(rest_kernel, line, team, nact, width, total_rows, places, halves),
        out_shape=[jax.ShapeDtypeStruct((width, part), F32)]
        + [jax.ShapeDtypeStruct(message, BF16)] * (nfirst * halves)
        + [jax.ShapeDtypeStruct((HALF, part), F32)],
        grid_spec=pltpu.PrefetchScalarGridSpec(
            num_scalar_prefetch=1,
            grid=(line,),
            in_specs=[whole((HALF, team_rows))] * team
            + [pl.BlockSpec((SMALL, LANES), lambda i, w: (0, 0))] * team
            + [
                whole((2 * HALF, team_rows)),
                whole((1, nact)),
                whole((SMALL, team_rows)),
                whole((team_rows, part)),
                whole((2 * LANES, part)),
            ]
            + [
                pl.BlockSpec((slab, piece.shape[1]), lambda i, w: (lax.rem(w[1] + i, line), 0))
                for piece in turned
            ],
            out_specs=[pl.BlockSpec((slab, part), lambda i, w: (i, 0))]
            + [whole(message)] * (nfirst * halves)
            + [whole((HALF, part))],
            scratch_shapes=[pltpu.VMEM((team_rows, part), BF16)],
        ),
        compiler_params=params(58),
        cost_estimate=COSTLY,
        name="rest",
    )(where, *sums, *squares, small_all, log_std[None, :], rinv, normed_hidden, hw_twice, *turned)
    grads, firsts, head = outs[0], outs[1:-1], outs[-1]

    def hop(h, up_block, down_block, *got):
        return pl.pallas_call(
            hop_kernel,
            out_shape=[jax.ShapeDtypeStruct(message, BF16)] * 2,
            grid=(1,),
            in_specs=[
                pl.BlockSpec((HALF, cols), lambda i: (0, h)),
                pl.BlockSpec((slab, cols), lambda i: (up_block, h)),
                pl.BlockSpec((slab, cols), lambda i: (down_block, h)),
            ]
            + [plain(message)] * 2,
            out_specs=[plain(message)] * 2,
            compiler_params=params(),
            cost_estimate=CHEAP,
            name="hop",
        )(head, grads, grads, *got)

    def final(h, *got):
        return pl.pallas_call(
            final_kernel,
            out_shape=[jax.ShapeDtypeStruct((kr + HALF, cols), F32)]
            + [jax.ShapeDtypeStruct((kr + HALF, cols), BF16)] * (team - 1),
            grid_spec=pltpu.PrefetchScalarGridSpec(
                num_scalar_prefetch=1,
                grid=(1,),
                in_specs=[
                    pl.BlockSpec((slab, cols), lambda i, w: (0, h)),
                    pl.BlockSpec((HALF, cols), lambda i, w: (0, h)),
                ]
                + [whole(message)] * 2,
                out_specs=[whole((kr + HALF, cols))] * team,
            ),
            compiler_params=params(),
            cost_estimate=CHEAP,
            name="final",
        )(where, grads, head, *got)

    recv_near = recv_near.reshape(line, team, some, per_peer, part)
    recv_far = recv_far.reshape(line, team, some, per_peer, part)

    def from_member(c, m):
        r = c ^ m
        return recv_near[:, c, r] if r < some else recv_far[:, c, r - some]

    hidden_out = jnp.concatenate(
        [jnp.stack([from_member(c, m) for m in range(team)], 1) for c in range(team)], -1
    ).reshape(rows, width)
    got = [(firsts[h - halves], firsts[h]) for h in range(halves)]
    for k in range(line - 2, 0, -1):
        if k < line - 2:
            got = [hop(h, k, line - k, *got[h]) for h in range(halves)]
        got = [(up(f, 0, line - k, k == 1), down(b, k, line, k == 1)) for f, b in got]
        if k == 2:
            got[0], hidden_out = lax.optimization_barrier((got[0], hidden_out))
    pieces = []
    for h in range(halves):
        pieces += [mate(piece, r) for r, piece in enumerate(final(h, *got[h]))]
    grad_weight, heads = pl.pallas_call(
        functools.partial(assemble_kernel, halves),
        out_shape=(
            jax.ShapeDtypeStruct((kr, width), F32),
            jax.ShapeDtypeStruct((heads_n, width), F32),
        ),
        grid_spec=pltpu.PrefetchScalarGridSpec(
            num_scalar_prefetch=1,
            grid=(1,),
            in_specs=[whole(piece.shape) for piece in pieces],
            out_specs=[whole((kr, width)), whole((heads_n, width))],
        ),
        compiler_params=params(),
        cost_estimate=CHEAP,
        name="assemble",
    )(where, *pieces)
    grad_head = heads.T
    grad_std = pieces[0][kr + heads_n, :nact]

    return (hidden_out, grad_weight, grad_head, grad_std)


def solution(mesh):
    return jax.shard_map(
        local,
        mesh=mesh,
        in_specs=(
            P(("groups", "fsdp"), None),
            P(("groups", "fsdp"), None),
            P(("groups", "fsdp"), None),
            P(("groups", "fsdp"), None),
            P(("groups", "fsdp")),
            P(("groups", "fsdp"), None),
            P(("groups", "fsdp"), None),
            P(),
            P("fsdp", None),
            P(),
            P(),
        ),
        out_specs=(
            P(("groups", "fsdp"), None),
            P(("groups", "fsdp"), None),
            P("groups", None),
            P("groups"),
        ),
        check_vma=False,
    )
```
